32 devices in a mesh: dp: 8 (over z, x), tensor: 4 (over y, core).
Axes of the slice: x: 2, y: 2, z: 4, core: 2. Of those that a mesh axis runs over, the one named last changes fastest.
Arguments:
- inputs: bfloat16 [12288, 768], P('dp'), may hold values from -8 to 8
- pair_lengths: int32 [24, 4], P('dp'), may hold values from 1 to 384, 512 in all within a row
- out_grad: bfloat16 [12288, 768], P('dp'), may hold values from -6 to 6
- w_qkv: float32 [2, 768, 3, 768], P(None, 'dp', None, 'tensor'), may hold values from -0.21875 to 0.21875
- m_qkv: float32 [2, 768, 3, 768], P(None, 'dp', None, 'tensor'), may hold values from -7.968413e-06 to 7.968413e-06
- v_qkv: float32 [2, 768, 3, 768], P(None, 'dp', None, 'tensor'), may hold values from 1.763767e-13 to 7.055068e-13
- w_out: float32 [2, 768, 768], P(None, ('tensor', 'dp')), may hold values from -0.625 to 0.625
- m_out: float32 [2, 768, 768], P(None, ('tensor', 'dp')), may hold values from -7.968413e-06 to 7.968413e-06
- v_out: float32 [2, 768, 768], P(None, ('tensor', 'dp')), may hold values from 1.763767e-13 to 7.055068e-13
- w_up: float32 [2, 768, 3072], P(None, 'dp', 'tensor'), may hold values from -0.21875 to 0.21875
- m_up: float32 [2, 768, 3072], P(None, 'dp', 'tensor'), may hold values from -7.968413e-06 to 7.968413e-06
- v_up: float32 [2, 768, 3072], P(None, 'dp', 'tensor'), may hold values from 1.763767e-13 to 7.055068e-13
- w_down: float32 [2, 3072, 768], P(None, ('tensor', 'dp')), may hold values from -0.109375 to 0.109375
- m_down: float32 [2, 3072, 768], P(None, ('tensor', 'dp')), may hold values from -7.968413e-06 to 7.968413e-06
- v_down: float32 [2, 3072, 768], P(None, ('tensor', 'dp')), may hold values from 1.763767e-13 to 7.055068e-13
- vectors: float32 [2, 6, 768], replicated, may hold values from -2 to 2
- m_vectors: float32 [2, 6, 768], replicated, may hold values from -2.390524e-05 to 2.390524e-05
- v_vectors: float32 [2, 6, 768], replicated, may hold values from 1.5873903e-12 to 6.349561e-12
- qv_bias: float32 [2, 2, 768], P(None, None, 'tensor'), may hold values from -1.5 to 1.5
- m_qv_bias: float32 [2, 2, 768], P(None, None, 'tensor'), may hold values from -2.390524e-05 to 2.390524e-05
- v_qv_bias: float32 [2, 2, 768], P(None, None, 'tensor'), may hold values from 1.5873903e-12 to 6.349561e-12
- up_bias: float32 [2, 3072], P(None, 'tensor'), may hold values from -1.5 to 1.5
- m_up_bias: float32 [2, 3072], P(None, 'tensor'), may hold values from -7.968413e-06 to 7.968413e-06
- v_up_bias: float32 [2, 3072], P(None, 'tensor'), may hold values from 1.763767e-13 to 7.055068e-13
Outputs:
- activations: bfloat16 [12288, 768], P('dp')
- input_grad: float32 [12288, 768], P('dp')
- grad_norm: float32 [], replicated
- new_qkv: float32 [2, 768, 3, 768], P(None, 'dp', None, 'tensor')
- new_m_qkv: float32 [2, 768, 3, 768], P(None, 'dp', None, 'tensor')
- new_v_qkv: float32 [2, 768, 3, 768], P(None, 'dp', None, 'tensor')
- new_out: float32 [2, 768, 768], P(None, ('tensor', 'dp'))
- new_m_out: float32 [2, 768, 768], P(None, ('tensor', 'dp'))
- new_v_out: float32 [2, 768, 768], P(None, ('tensor', 'dp'))
- new_up: float32 [2, 768, 3072], P(None, 'dp', 'tensor')
- new_m_up: float32 [2, 768, 3072], P(None, 'dp', 'tensor')
- new_v_up: float32 [2, 768, 3072], P(None, 'dp', 'tensor')
- new_down: float32 [2, 3072, 768], P(None, ('tensor', 'dp'))
- new_m_down: float32 [2, 3072, 768], P(None, ('tensor', 'dp'))
- new_v_down: float32 [2, 3072, 768], P(None, ('tensor', 'dp'))
- new_vectors: float32 [2, 6, 768], replicated
- new_m_vectors: float32 [2, 6, 768], replicated
- new_v_vectors: float32 [2, 6, 768], replicated
- new_qv_bias: float32 [2, 2, 768], P(None, None, 'tensor')
- new_m_qv_bias: float32 [2, 2, 768], P(None, None, 'tensor')
- new_v_qv_bias: float32 [2, 2, 768], P(None, None, 'tensor')
- new_up_bias: float32 [2, 3072], P(None, 'tensor')
- new_m_up_bias: float32 [2, 3072], P(None, 'tensor')
- new_v_up_bias: float32 [2, 3072], P(None, 'tensor')
The draws below stay inside these ranges and needn't reach their ends.
Inputs may be any that keep to these rules, and one draw needn't show every extreme that they name: `pair_lengths`: each row holds the lengths of the 4 pairs of one pack in order; they sum to 512, and the longest in each row is 384.
All inputs are finite; a program needn't handle non-finite values.
Results may differ from the reference program's by a relative error of at most 0.03.
Values may be sent and summed in bfloat16 or wider, within the bound.
A program may use at most 192 MiB of HBM per device.

```python
import math
import jax
import jax.numpy as jnp
import numpy as np
from jax import lax

D = 768
HD = 64
FF = 3072
SEQ = 512
PAIRS = 4
LAYERS = 2
STEP = 10
PACKS_DEV = 3
MOST = 384
PACKS = 24
TOKENS = 12288
NPARAM = 14174208
N_DP = 8
N_TENSOR = 4


def draw_inputs(key, part):
    key = jax.random.fold_in(key, 11)
    ramp = jnp.linspace(0.0, 1.0, D, dtype=jnp.float32)
    noise = jnp.clip(jax.random.normal(key, (TOKENS, D), jnp.float32), -6.0, 6.0)
    scale = 0.75 + 0.55 * ramp
    return (noise * scale[None, :]).astype(jnp.float32).astype(jnp.bfloat16)


def draw_vectors(key, part):
    key = jax.random.fold_in(key, 23)
    first_key, second_key = jax.random.split(key)
    ramp = jnp.linspace(0.0, 1.0, D, dtype=jnp.float32)
    row_index = jnp.arange(6, dtype=jnp.int32)[None, :, None]
    gain_rows = (row_index == 0) | (row_index == 2)
    jitter = jax.random.uniform(first_key, (LAYERS, 6, D), jnp.float32, 0.8, 1.2)
    rising = 0.75 + 0.55 * ramp
    shifts = jnp.clip(0.3 * jax.random.normal(second_key, (LAYERS, 6, D), jnp.float32), -1.5, 1.5)
    return jnp.where(gain_rows, rising[None, None, :] * jitter, shifts).astype(jnp.float32)


def level_of(own_key, extent, shards, smallest, high):
    loudness = 1.0
    for dim, parts in shards:
        steps = jax.random.uniform(jax.random.fold_in(jax.random.fold_in(own_key, 6), dim), (parts,), jnp.float32, smallest / len(shards), high / len(shards))
        loudness = loudness * jnp.repeat(jnp.exp(steps), extent[dim] // parts).reshape((-1,) + (1,) * (len(extent) - 1 - dim))
    return loudness


def profile(number_of, total, bound, slope):
    portions = [(1 << 20) // math.isqrt(standing ** slope) + 1 for standing in range(2, number_of + 1)]
    surplus, holding = total - bound - (number_of - 1), [1] * (number_of - 1)
    while surplus > 0:
        movable = [i for i in range(number_of - 1) if holding[i] < bound]
        pool, remaining = sum([portions[i] for i in movable]), surplus
        for i in movable:
            more = min(bound - holding[i], max(1, remaining * portions[i] // pool), surplus)
            holding[i] = holding[i] + more
            surplus = surplus - more
    return np.array([bound] + holding)


def uneven(key, count, total, limit, slope):
    if count == 2:
        one = jax.random.randint(key, (), max(1, total - limit), min(limit, total - 1) + 1)
        return jnp.stack([one, total - one])
    tallies = jnp.asarray(profile(count, total, limit, slope), jnp.int32)
    twos = (count - 1) // 2
    giver, sink = tallies[1:1 + 2 * twos:2], tallies[2:2 + 2 * twos:2]
    slack = jnp.minimum(giver - 1, limit - sink)
    moved = jax.random.randint(jax.random.fold_in(key, 1), (twos,), 0, 1 << 20) % (slack + 1)
    tallies = tallies.at[1:1 + 2 * twos:2].set(giver - moved).at[2:2 + 2 * twos:2].set(sink + moved)
    return tallies[jax.random.permutation(jax.random.fold_in(key, 2), count)]


def normal_values(stream_key, shape, deviation, limit, cuts=(), held_as=jnp.bfloat16):
    loudness = level_of(stream_key, shape, cuts, -0.22, 0.18) if cuts else 1.0
    drawn = jax.random.normal(stream_key, shape, jnp.float32) * deviation * loudness
    return jnp.minimum(jnp.maximum(drawn, -limit), limit).astype(held_as)


def setup_inputs(seed: int = 0) -> dict:
    streams_of = jax.random.split(jax.random.key(seed), 25)
    return {
        "inputs": draw_inputs(jax.random.fold_in(streams_of[24], 71), 0),
        "pair_lengths": jax.vmap(lambda own: uneven(own, PAIRS, SEQ, MOST, 2))(jax.random.split(streams_of[1], PACKS)).reshape((PACKS, PAIRS)).astype(jnp.int32),
        "out_grad": normal_values(streams_of[2], (TOKENS, D), 1.0, 6.0, ((0, 8),)),
        "w_qkv": normal_values(streams_of[3], (LAYERS, D, 3, D), D ** -0.5, 0.21875, ((1, 8), (3, 4)), jnp.float32),
        "m_qkv": normal_values(streams_of[4], (LAYERS, D, 3, D), (0.0056 / NPARAM ** 0.5), 7.968413228809368e-06, ((1, 8), (3, 4)), jnp.float32),
        "v_qkv": jnp.clip(jnp.exp(math.log(7.055067792992309e-13) - 1.3862944 * jax.random.uniform(streams_of[5], (LAYERS, D, 3, D), jnp.float32) ** level_of(streams_of[5], (LAYERS, D, 3, D), ((1, 8), (3, 4)), -0.2, 0.2)), 1.7637669482480772e-13, 7.055067792992309e-13),
        "w_out": normal_values(streams_of[6], (LAYERS, D, D), (D // 8) ** -0.5, 0.625, ((1, 32),), jnp.float32),
        "m_out": normal_values(streams_of[7], (LAYERS, D, D), (0.0056 / NPARAM ** 0.5), 7.968413228809368e-06, ((1, 32),), jnp.float32),
        "v_out": jnp.clip(jnp.exp(math.log(7.055067792992309e-13) - 1.3862944 * jax.random.uniform(streams_of[8], (LAYERS, D, D), jnp.float32) ** level_of(streams_of[8], (LAYERS, D, D), ((1, 32),), -0.2, 0.2)), 1.7637669482480772e-13, 7.055067792992309e-13),
        "w_up": normal_values(streams_of[9], (LAYERS, D, FF), D ** -0.5, 0.21875, ((1, 8), (2, 4)), jnp.float32),
        "m_up": normal_values(streams_of[10], (LAYERS, D, FF), (0.0056 / NPARAM ** 0.5), 7.968413228809368e-06, ((1, 8), (2, 4)), jnp.float32),
        "v_up": jnp.clip(jnp.exp(math.log(7.055067792992309e-13) - 1.3862944 * jax.random.uniform(streams_of[11], (LAYERS, D, FF), jnp.float32) ** level_of(streams_of[11], (LAYERS, D, FF), ((1, 8), (2, 4)), -0.2, 0.2)), 1.7637669482480772e-13, 7.055067792992309e-13),
        "w_down": normal_values(streams_of[12], (LAYERS, FF, D), FF ** -0.5, 0.109375, ((1, 32),), jnp.float32),
        "m_down": normal_values(streams_of[13], (LAYERS, FF, D), (0.0056 / NPARAM ** 0.5), 7.968413228809368e-06, ((1, 32),), jnp.float32),
        "v_down": jnp.clip(jnp.exp(math.log(7.055067792992309e-13) - 1.3862944 * jax.random.uniform(streams_of[14], (LAYERS, FF, D), jnp.float32) ** level_of(streams_of[14], (LAYERS, FF, D), ((1, 32),), -0.2, 0.2)), 1.7637669482480772e-13, 7.055067792992309e-13),
        "vectors": draw_vectors(jax.random.fold_in(streams_of[24], 71), 0),
        "m_vectors": normal_values(streams_of[16], (LAYERS, 6, D), (0.017 / NPARAM ** 0.5), 2.3905240595922805e-05, (), jnp.float32),
        "v_vectors": jnp.clip(jnp.exp(jax.random.uniform(streams_of[17], (LAYERS, 6, D), jnp.float32, math.log(1.5873902669757967e-12), math.log(6.349561067903187e-12))), 1.5873902669757967e-12, 6.349561067903187e-12),
        "qv_bias": normal_values(streams_of[18], (LAYERS, 2, D), 0.3, 1.5, ((2, 4),), jnp.float32),
        "m_qv_bias": normal_values(streams_of[19], (LAYERS, 2, D), (0.017 / NPARAM ** 0.5), 2.3905240595922805e-05, ((2, 4),), jnp.float32),
        "v_qv_bias": jnp.clip(jnp.exp(math.log(6.349561067903187e-12) - 1.3862944 * jax.random.uniform(streams_of[20], (LAYERS, 2, D), jnp.float32) ** level_of(streams_of[20], (LAYERS, 2, D), ((2, 4),), -0.2, 0.2)), 1.5873902669757967e-12, 6.349561067903187e-12),
        "up_bias": normal_values(streams_of[21], (LAYERS, FF), 0.3, 1.5, ((1, 4),), jnp.float32),
        "m_up_bias": normal_values(streams_of[22], (LAYERS, FF), (0.0056 / NPARAM ** 0.5), 7.968413228809368e-06, ((1, 4),), jnp.float32),
        "v_up_bias": jnp.clip(jnp.exp(math.log(7.055067792992309e-13) - 1.3862944 * jax.random.uniform(streams_of[23], (LAYERS, FF), jnp.float32) ** level_of(streams_of[23], (LAYERS, FF), ((1, 4),), -0.2, 0.2)), 1.7637669482480772e-13, 7.055067792992309e-13),
    }


@jax.custom_vjp
def low(v):
    return lax.optimization_barrier(v.astype(jnp.bfloat16)).astype(jnp.float32)

@jax.custom_vjp
def low_back(v):
    return v

def low_keep(v):
    return (low(v), None)

def low_pass(kept, grad):
    return (grad,)

def back_keep(v):
    return (v, None)

def back_low(kept, grad):
    return (low(grad),)
low.defvjp(low_keep, low_pass)
low_back.defvjp(back_keep, back_low)
HIGH = lax.Precision.HIGHEST
NORM_EPS = 1e-05
CLIP_LIMIT = 0.05
BETA_ONE = 0.9
BETA_TWO = 0.999
LEARN_RATE = 0.1
VECTOR_RATE = 1.0
WEIGHT_DECAY = 0.01
ADAM_EPS = 1e-08

def layer_norm(rows_in, gain, shift):
    center = rows_in - lax.optimization_barrier(jnp.mean(rows_in, axis=-1, keepdims=True))
    spread = lax.optimization_barrier(jnp.mean(center * center, axis=-1, keepdims=True))
    return center * lax.rsqrt(spread + NORM_EPS) * gain + shift

def pair_mask(lengths):
    ends = jnp.cumsum(lengths)
    positions = jnp.arange(SEQ, dtype=jnp.int32)
    pair_of = lax.optimization_barrier(jnp.sum((positions[:, None] >= ends[None, :]).astype(jnp.int32), axis=1))
    return pair_of[:, None] == pair_of[None, :]

def pack_attention(items):
    queries, key_rows, values, allowed = items
    scores = jnp.einsum('qhe,khe->hqk', queries, key_rows, precision=HIGH) * HD ** (-0.5)
    scores = low_back(scores)
    scores = jnp.where(allowed[None], scores, -1e+30)
    probs = low(jax.nn.softmax(scores, axis=-1))
    return jnp.einsum('hqk,khe->qhe', probs, values, precision=HIGH)

def encoder_layer(stream, qkv_weight, out_weight, up_weight, down_weight, vector_rows, qv_rows, up_row, masks):
    width = D // N_TENSOR
    inner = FF // N_TENSOR
    group_heads = width // HD
    pack_count = masks.shape[0]
    stream_low = low(stream)
    qkv_low = low(qkv_weight)
    out_low = low(out_weight)
    up_low = low(up_weight)
    down_low = low(down_weight)
    attn_total = jnp.zeros(stream.shape, jnp.float32)
    for group_index in range(N_TENSOR):
        start = group_index * width
        group_in = low_back(stream_low)
        project = jnp.einsum('td,dcn->tcn', group_in, qkv_low[:, :, start:start + width], precision=HIGH)
        queries = low_back(low(project[:, 0] + qv_rows[0, start:start + width]))
        key_rows = low_back(low(project[:, 1]))
        values = low_back(low(project[:, 2] + qv_rows[1, start:start + width]))
        shaped = [piece_array.reshape(pack_count, SEQ, group_heads, HD) for piece_array in (queries, key_rows, values)]
        attended = lax.map(jax.checkpoint(pack_attention), (shaped[0], shaped[1], shaped[2], masks))
        merged = low_back(low(attended.reshape(-1, width)))
        attn_total = attn_total + low(jnp.dot(merged, out_low[start:start + width], precision=HIGH))
    first_sum = stream + low_back(attn_total) + vector_rows[4]
    normed = layer_norm(first_sum, vector_rows[0], vector_rows[1])
    normed_low = low(normed)
    ffn_total = jnp.zeros(stream.shape, jnp.float32)
    for group_index in range(N_TENSOR):
        start = group_index * inner
        group_in = low_back(normed_low)
        hidden_pre = low_back(jnp.dot(group_in, up_low[:, start:start + inner], precision=HIGH) + up_row[start:start + inner])
        hidden_act = low(jax.nn.gelu(hidden_pre, approximate=False))
        ffn_total = ffn_total + low(jnp.dot(hidden_act, down_low[start:start + inner], precision=HIGH))
    second_sum = normed + low_back(ffn_total) + vector_rows[5]
    return layer_norm(second_sum, vector_rows[2], vector_rows[3])

def forward(stream, w_qkv, w_out, w_up, w_down, vectors, qv_bias, up_bias, masks):
    for layer_index in range(LAYERS):
        stream = encoder_layer(stream, w_qkv[layer_index], w_out[layer_index], w_up[layer_index], w_down[layer_index], vectors[layer_index], qv_bias[layer_index], up_bias[layer_index], masks)
    return stream

def adamw(weight, first, second, gradient, factor, rate, decay):
    clipped = gradient * factor
    new_first = BETA_ONE * first + (1.0 - BETA_ONE) * clipped
    new_second = BETA_TWO * second + (1.0 - BETA_TWO) * clipped * clipped
    first_hat = new_first / (1.0 - BETA_ONE ** STEP)
    second_hat = new_second / (1.0 - BETA_TWO ** STEP)
    new_weight = weight - rate * (first_hat / (jnp.sqrt(second_hat) + ADAM_EPS) + decay * weight)
    return (new_weight, new_first, new_second)

def reference(inputs, pair_lengths, out_grad, w_qkv, m_qkv, v_qkv, w_out, m_out, v_out, w_up, m_up, v_up, w_down, m_down, v_down, vectors, m_vectors, v_vectors, qv_bias, m_qv_bias, v_qv_bias, up_bias, m_up_bias, v_up_bias):
    rows = PACKS_DEV * SEQ
    blocks_in = inputs.astype(jnp.float32).reshape(N_DP, rows, D)
    blocks_cot = out_grad.astype(jnp.float32).reshape(N_DP, rows, D)
    blocks_len = pair_lengths.reshape(N_DP, PACKS_DEV, PAIRS)
    params = (w_qkv, w_out, w_up, w_down, vectors, qv_bias, up_bias)

    def block_step(total, item):
        stream, cotangent, lengths = item
        masks = jax.vmap(pair_mask)(lengths)

        def run(stream_in, *weights):
            return forward(stream_in, *weights, masks)
        result, pull = jax.vjp(run, stream, *params)
        grads = pull(cotangent)
        total = tuple((jnp.add(acc, part) for acc, part in zip(total, grads[1:])))
        return (total, (result.astype(jnp.bfloat16), grads[0]))
    zeros = tuple((jnp.zeros(param.shape, jnp.float32) for param in params))
    total, (results, in_grads) = lax.scan(block_step, zeros, (blocks_in, blocks_cot, blocks_len))
    squares = sum((jnp.sum(grad_part * grad_part) for grad_part in total))
    grad_norm = jnp.sqrt(squares)
    factor = jnp.minimum(1.0, CLIP_LIMIT / grad_norm)
    g_qkv, g_out, g_up, g_down, g_vec, g_qv, g_upb = total
    new_qkv = adamw(w_qkv, m_qkv, v_qkv, g_qkv, factor, LEARN_RATE, WEIGHT_DECAY)
    new_out = adamw(w_out, m_out, v_out, g_out, factor, LEARN_RATE, WEIGHT_DECAY)
    new_up = adamw(w_up, m_up, v_up, g_up, factor, LEARN_RATE, WEIGHT_DECAY)
    new_down = adamw(w_down, m_down, v_down, g_down, factor, LEARN_RATE, WEIGHT_DECAY)
    new_vec = adamw(vectors, m_vectors, v_vectors, g_vec, factor, VECTOR_RATE, 0.0)
    new_qv = adamw(qv_bias, m_qv_bias, v_qv_bias, g_qv, factor, VECTOR_RATE, 0.0)
    new_upb = adamw(up_bias, m_up_bias, v_up_bias, g_upb, factor, VECTOR_RATE, 0.0)
    return (results.reshape(TOKENS, D), in_grads.reshape(TOKENS, D), grad_norm, new_qkv[0], new_qkv[1], new_qkv[2], new_out[0], new_out[1], new_out[2], new_up[0], new_up[1], new_up[2], new_down[0], new_down[1], new_down[2], new_vec[0], new_vec[1], new_vec[2], new_qv[0], new_qv[1], new_qv[2], new_upb[0], new_upb[1], new_upb[2])
```

```python
import math
import types

import jax
import jax.numpy as jnp
from jax import lax
from jax.experimental import pallas as pl
from jax.experimental.pallas import tpu as pltpu
from jax.sharding import PartitionSpec as P

HD = 64
SEQ = 512
LAYERS = 2
STEP = 10


NORM_EPS = 1e-05
CLIP_LIMIT = 0.05
BETA_ONE = 0.9
BETA_TWO = 0.999
LEARN_RATE = 0.1
VECTOR_RATE = 1.0
WEIGHT_DECAY = 0.01
ADAM_EPS = 1e-08


def layer_norm(rows_in, gain, shift):
    center = rows_in - jnp.mean(rows_in, axis=-1, keepdims=True)
    spread = jnp.mean(center * center, axis=-1, keepdims=True)
    return center * lax.rsqrt(spread + NORM_EPS) * gain + shift


def gelu_exact(pre_values):
    return jax.nn.gelu(pre_values, approximate=False)


def pair_mask(lengths):
    ends = jnp.cumsum(lengths)
    positions = jnp.arange(SEQ, dtype=jnp.int32)
    pair_of = jnp.sum((positions[:, None] >= ends[None, :]).astype(jnp.int32), axis=1)
    return pair_of[:, None] == pair_of[None, :]


def pack_scores(queries, key_rows, masks):
    scores = jnp.einsum(
        "pqhe,pkhe->phqk", queries, key_rows, preferred_element_type=jnp.float32
    ) * HD ** (-0.5)
    return jnp.where(masks[:, None], scores, -1e30)


def attend(queries, key_rows, values, masks):
    scores = pack_scores(queries, key_rows, masks)
    top = jnp.max(scores, axis=-1, keepdims=True)
    weights = jnp.exp(scores - top)
    total = jnp.sum(weights, axis=-1, keepdims=True)
    probs = weights / total
    attended = jnp.einsum(
        "phqk,pkhe->pqhe", probs.astype(jnp.bfloat16), values, preferred_element_type=jnp.float32
    )
    return (attended, top + jnp.log(total))


def attend_back(queries, key_rows, values, grad_attended, log_total, masks):
    scores = pack_scores(queries, key_rows, masks)
    probs = jnp.exp(scores - log_total)
    grad_values = jnp.einsum(
        "phqk,pqhe->pkhe",
        probs.astype(jnp.bfloat16),
        grad_attended,
        preferred_element_type=jnp.float32,
    )
    grad_probs = jnp.einsum(
        "pqhe,pkhe->phqk", grad_attended, values, preferred_element_type=jnp.float32
    )
    row_dot = jnp.sum(grad_probs * probs, axis=-1, keepdims=True)
    grad_scores = (probs * (grad_probs - row_dot)).astype(jnp.bfloat16)
    grad_queries = jnp.einsum(
        "phqk,pkhe->pqhe", grad_scores, key_rows, preferred_element_type=jnp.float32
    ) * HD ** (-0.5)
    grad_keys = jnp.einsum(
        "phqk,pqhe->pkhe", grad_scores, queries, preferred_element_type=jnp.float32
    ) * HD ** (-0.5)
    return (
        grad_queries.astype(jnp.bfloat16),
        grad_keys.astype(jnp.bfloat16),
        grad_values.astype(jnp.bfloat16),
    )


def layer_forward(stream, qkv_w, out_w, up_w, down_w, vector_rows, qv_rows, up_row, masks):
    row_count = stream.shape[0]
    pack_count = masks.shape[0]
    width = out_w.shape[0]
    group_heads = width // HD
    stream_low = stream.astype(jnp.bfloat16)
    project = jnp.einsum("td,dcn->tcn", stream_low, qkv_w, preferred_element_type=jnp.float32)
    queries = (
        (project[:, 0] + qv_rows[0]).astype(jnp.bfloat16).reshape(pack_count, SEQ, group_heads, HD)
    )
    key_rows = project[:, 1].astype(jnp.bfloat16).reshape(pack_count, SEQ, group_heads, HD)
    values = (
        (project[:, 2] + qv_rows[1]).astype(jnp.bfloat16).reshape(pack_count, SEQ, group_heads, HD)
    )
    attended, log_total = attend(queries, key_rows, values, masks)
    merged = attended.reshape(row_count, width).astype(jnp.bfloat16)
    attn_part = jnp.dot(merged, out_w, preferred_element_type=jnp.float32)
    attn_summed = lax.psum(attn_part.astype(jnp.bfloat16), "tensor").astype(jnp.float32)
    first_sum = stream + attn_summed + vector_rows[4]
    normed = layer_norm(first_sum, vector_rows[0], vector_rows[1])
    normed_low = normed.astype(jnp.bfloat16)
    hidden_pre = jnp.dot(normed_low, up_w, preferred_element_type=jnp.float32) + up_row
    hidden_act = gelu_exact(hidden_pre).astype(jnp.bfloat16)
    ffn_part = jnp.dot(hidden_act, down_w, preferred_element_type=jnp.float32)
    ffn_summed = lax.psum(ffn_part.astype(jnp.bfloat16), "tensor").astype(jnp.float32)
    second_sum = normed + ffn_summed + vector_rows[5]
    result = layer_norm(second_sum, vector_rows[2], vector_rows[3])
    kept = (
        stream_low,
        queries,
        key_rows,
        values,
        log_total,
        merged,
        first_sum,
        normed_low,
        hidden_pre,
        hidden_act,
        second_sum,
    )
    return (result, kept)


def layer_backward(grad_out, kept, qkv_w, out_w, up_w, down_w, vector_rows, masks):
    (
        stream_low,
        queries,
        key_rows,
        values,
        log_total,
        merged,
        first_sum,
        normed_low,
        hidden_pre,
        hidden_act,
        second_sum,
    ) = kept
    row_count = stream_low.shape[0]
    width = out_w.shape[0]
    _, pull_second = jax.vjp(layer_norm, second_sum, vector_rows[2], vector_rows[3])
    grad_second, grad_gain_two, grad_shift_two = pull_second(grad_out)
    grad_down_bias = jnp.sum(grad_second, axis=0)
    low_second = grad_second.astype(jnp.bfloat16)
    grad_down = jnp.einsum("tf,td->fd", hidden_act, low_second, preferred_element_type=jnp.float32)
    grad_act = jnp.einsum("td,fd->tf", low_second, down_w, preferred_element_type=jnp.float32)
    _, pull_gelu = jax.vjp(gelu_exact, hidden_pre)
    grad_pre = pull_gelu(grad_act)[0].astype(jnp.bfloat16)
    grad_up_bias = jnp.sum(grad_pre.astype(jnp.float32), axis=0)
    grad_up = jnp.einsum("td,tf->df", normed_low, grad_pre, preferred_element_type=jnp.float32)
    back_normed = jnp.einsum("tf,df->td", grad_pre, up_w, preferred_element_type=jnp.float32)
    grad_normed = grad_second + lax.psum(back_normed.astype(jnp.bfloat16), "tensor").astype(
        jnp.float32
    )
    _, pull_first = jax.vjp(layer_norm, first_sum, vector_rows[0], vector_rows[1])
    grad_first, grad_gain_one, grad_shift_one = pull_first(grad_normed)
    grad_out_bias = jnp.sum(grad_first, axis=0)
    low_first = grad_first.astype(jnp.bfloat16)
    grad_outw = jnp.einsum("tn,td->nd", merged, low_first, preferred_element_type=jnp.float32)
    grad_merged = jnp.einsum(
        "td,nd->tn", low_first, out_w, preferred_element_type=jnp.float32
    ).astype(jnp.bfloat16)
    grad_queries, grad_keys, grad_values = attend_back(
        queries, key_rows, values, grad_merged.reshape(queries.shape), log_total, masks
    )
    grad_project = jnp.stack(
        (
            grad_queries.reshape(row_count, width),
            grad_keys.reshape(row_count, width),
            grad_values.reshape(row_count, width),
        ),
        axis=1,
    )
    grad_qv_bias = jnp.sum(grad_project[:, 0::2].astype(jnp.float32), axis=0)
    grad_qkv = jnp.einsum(
        "td,tcn->dcn", stream_low, grad_project, preferred_element_type=jnp.float32
    )
    back_stream = jnp.einsum("tcn,dcn->td", grad_project, qkv_w, preferred_element_type=jnp.float32)
    grad_stream = grad_first + lax.psum(back_stream.astype(jnp.bfloat16), "tensor").astype(
        jnp.float32
    )
    vector_grad = jnp.stack(
        (
            grad_gain_one,
            grad_shift_one,
            grad_gain_two,
            grad_shift_two,
            grad_out_bias,
            grad_down_bias,
        )
    )
    return (
        grad_stream,
        (grad_qkv, grad_outw, grad_up, grad_down),
        (vector_grad, grad_qv_bias, grad_up_bias),
    )


def adamw(weight, first, second, gradient, factor, rate, decay):
    clipped = gradient * factor
    new_first = BETA_ONE * first + (1.0 - BETA_ONE) * clipped
    new_second = BETA_TWO * second + (1.0 - BETA_TWO) * clipped * clipped
    first_hat = new_first / (1.0 - BETA_ONE**STEP)
    second_hat = new_second / (1.0 - BETA_TWO**STEP)
    new_weight = weight - rate * (first_hat / (jnp.sqrt(second_hat) + ADAM_EPS) + decay * weight)
    return (new_weight, new_first, new_second)


def body(
    inputs,
    pair_lengths,
    out_grad,
    w_qkv,
    m_qkv,
    v_qkv,
    w_out,
    m_out,
    v_out,
    w_up,
    m_up,
    v_up,
    w_down,
    m_down,
    v_down,
    vectors,
    m_vectors,
    v_vectors,
    qv_bias,
    m_qv_bias,
    v_qv_bias,
    up_bias,
    m_up_bias,
    v_up_bias,
):
    full_qkv, full_out, full_up, full_down = (
        lax.all_gather(w_qkv.astype(jnp.bfloat16), "dp", axis=1, tiled=True),
        lax.all_gather(w_out.astype(jnp.bfloat16), "dp", axis=1, tiled=True),
        lax.all_gather(w_up.astype(jnp.bfloat16), "dp", axis=1, tiled=True),
        lax.all_gather(w_down.astype(jnp.bfloat16), "dp", axis=1, tiled=True),
    )
    masks = jax.vmap(pair_mask)(pair_lengths)
    stream = inputs.astype(jnp.float32)
    kept_all = []
    for layer_index in range(LAYERS):
        stream, kept = layer_forward(
            stream,
            full_qkv[layer_index],
            full_out[layer_index],
            full_up[layer_index],
            full_down[layer_index],
            vectors[layer_index],
            qv_bias[layer_index],
            up_bias[layer_index],
            masks,
        )
        kept_all.append(kept)
    activations = stream.astype(jnp.bfloat16)
    grad_stream = out_grad.astype(jnp.float32)
    matrix_grads = [None] * LAYERS
    small_grads = [None] * LAYERS
    for layer_index in reversed(range(LAYERS)):
        grad_stream, mats, smalls = layer_backward(
            grad_stream,
            kept_all[layer_index],
            full_qkv[layer_index],
            full_out[layer_index],
            full_up[layer_index],
            full_down[layer_index],
            vectors[layer_index],
            masks,
        )
        matrix_grads[layer_index] = mats
        small_grads[layer_index] = smalls
    stacked = tuple(
        (
            jnp.stack([matrix_grads[layer_index][kind] for layer_index in range(LAYERS)])
            for kind in range(4)
        )
    )
    g_qkv, g_out, g_up, g_down = (
        lax.psum_scatter(stacked[0], "dp", scatter_dimension=1, tiled=True),
        lax.psum_scatter(stacked[1], "dp", scatter_dimension=1, tiled=True),
        lax.psum_scatter(stacked[2], "dp", scatter_dimension=1, tiled=True),
        lax.psum_scatter(stacked[3], "dp", scatter_dimension=1, tiled=True),
    )
    small_stacked = tuple(
        (
            jnp.stack([small_grads[layer_index][kind] for layer_index in range(LAYERS)])
            for kind in range(3)
        )
    )
    g_vec, g_qv, g_upb = lax.psum(small_stacked, "dp")
    data_count = lax.axis_size("dp")
    tensor_count = lax.axis_size("tensor")
    local_squares = (
        jnp.sum(g_qkv * g_qkv)
        + jnp.sum(g_out * g_out)
        + jnp.sum(g_up * g_up)
        + jnp.sum(g_down * g_down)
        + (jnp.sum(g_qv * g_qv) + jnp.sum(g_upb * g_upb)) / data_count
        + jnp.sum(g_vec * g_vec) / (data_count * tensor_count)
    )
    squares = lax.psum(local_squares, ("dp", "tensor"))
    grad_norm = jnp.sqrt(squares)
    factor = jnp.minimum(1.0, CLIP_LIMIT / grad_norm)
    new_qkv = adamw(w_qkv, m_qkv, v_qkv, g_qkv, factor, LEARN_RATE, WEIGHT_DECAY)
    new_out = adamw(w_out, m_out, v_out, g_out, factor, LEARN_RATE, WEIGHT_DECAY)
    new_up = adamw(w_up, m_up, v_up, g_up, factor, LEARN_RATE, WEIGHT_DECAY)
    new_down = adamw(w_down, m_down, v_down, g_down, factor, LEARN_RATE, WEIGHT_DECAY)
    new_vec = adamw(vectors, m_vectors, v_vectors, g_vec, factor, VECTOR_RATE, 0.0)
    new_qv = adamw(qv_bias, m_qv_bias, v_qv_bias, g_qv, factor, VECTOR_RATE, 0.0)
    new_upb = adamw(up_bias, m_up_bias, v_up_bias, g_upb, factor, VECTOR_RATE, 0.0)
    return (
        activations,
        grad_stream,
        grad_norm,
        new_qkv[0],
        new_qkv[1],
        new_qkv[2],
        new_out[0],
        new_out[1],
        new_out[2],
        new_up[0],
        new_up[1],
        new_up[2],
        new_down[0],
        new_down[1],
        new_down[2],
        new_vec[0],
        new_vec[1],
        new_vec[2],
        new_qv[0],
        new_qv[1],
        new_qv[2],
        new_upb[0],
        new_upb[1],
        new_upb[2],
    )


MESH = pl.DeviceIdType.MESH
F32, BF16 = jnp.float32, jnp.bfloat16
LINE = 4
DM = 768
KINDS = ("qkv", "out", "up", "down")
BLOCK = {"qkv": (96, 576), "out": (16, 1152), "up": (96, 768), "down": (96, 768)}
SPLIT = {"qkv": (0, 48, 80), "out": (1, 512, 1024), "up": (0, 48, 80), "down": (0, 32, 80)}
SEMS = 420
OWN, HALF = 384, 256


def dot(a, b):
    return jnp.dot(a, b, preferred_element_type=F32)


def dot_nt(a, b):
    return lax.dot_general(a, b, (((1,), (1,)), ((), ())), preferred_element_type=F32)


def dot_tn(a, b):
    return lax.dot_general(a, b, (((0,), (0,)), ((), ())), preferred_element_type=F32)


def flat(v):
    return v.reshape((-1, v.shape[-1]))


def gelu_and_slope(u):
    a = jnp.abs(u) * (1.0 / math.sqrt(2.0))
    t = 1.0 / (1.0 + 0.5 * a)
    poly = 0.17087277
    for coeff in (
        -0.82215223,
        1.48851587,
        -1.13520398,
        0.27886807,
        -0.18628806,
        0.09678418,
        0.37409196,
        1.00002368,
        -1.26551223,
    ):
        poly = poly * t + coeff
    bell = jnp.exp(-0.5 * u * u)
    tail = 0.5 * t * bell * jnp.exp(poly)
    below = jnp.where(u >= 0, 1.0 - tail, tail)
    return u * below, below + u * bell * (1.0 / math.sqrt(2.0 * math.pi))


def norm_stats(rows):
    center = rows - jnp.mean(rows, axis=-1, keepdims=True)
    spread = jnp.mean(center * center, axis=-1, keepdims=True)
    scale = lax.rsqrt(spread + NORM_EPS)
    return center * scale, scale


class Moves:
    def __init__(self, send, recv):
        self.send, self.recv, self.count, self.open = send, recv, 0, []

    def make(self, src, dst, device, lands, can_send=None, can_recv=None):
        index = self.count
        self.count += 1
        assert index < SEMS
        move = types.SimpleNamespace()

        def copy(src, dst):
            return pltpu.make_async_remote_copy(
                src_ref=src,
                dst_ref=dst,
                send_sem=self.send.at[index],
                recv_sem=self.recv.at[index],
                device_id=device,
                device_id_type=MESH,
            )

        def guarded(cond, act):
            if cond is None:
                act()
            else:
                pl.when(cond)(act)

        def start():
            guarded(can_send, lambda: copy(src(), dst()).start())
            self.open.append(move)

        move.start = start
        move.wait_recv = lambda: guarded(can_recv, lambda: copy(lands(), lands()).wait_recv())
        move.wait_send = lambda: guarded(can_send, lambda: copy(src(), src()).wait_send())
        return move

    def sent(self, *moves):
        for move in moves:
            move.wait_send()
            self.open.remove(move)

    def drain(self):
        for move in self.open:
            move.wait_send()
        self.open = []


def fused(names, *refs):
    k = types.SimpleNamespace(**dict(zip(names, refs)))
    dp, tensor = lax.axis_index("dp"), lax.axis_index("tensor")
    z, x, y, c = dp // 2, dp % 2, tensor // 2, tensor % 2
    core_dev = (dp, y * 2 + 1 - c)
    y_dev = (dp, (1 - y) * 2 + c)
    x_dev = (z * 2 + 1 - x, tensor)
    up_dev = ((z + 1) * 2 + x, tensor)
    down_dev = ((z - 1) * 2 + x, tensor)
    far_dev = ((z ^ 2) * 2 + x, tensor)
    near_dev = ((z ^ 1) * 2 + x, tensor)
    not_last, not_first = z <= LINE - 2, z >= 1

    barrier = pltpu.get_barrier_semaphore()
    for device in (core_dev, y_dev, x_dev, far_dev):
        pl.semaphore_signal(barrier, inc=1, device_id=device, device_id_type=MESH)

    @pl.when(not_last)
    def _():
        pl.semaphore_signal(barrier, inc=1, device_id=up_dev, device_id_type=MESH)

    @pl.when(not_first)
    def _():
        pl.semaphore_signal(barrier, inc=1, device_id=down_dev, device_id_type=MESH)

    moves = Moves(k.send, k.recv)
    weights = {"qkv": k.w_qkv, "out": k.w_out, "up": k.w_up, "down": k.w_down}

    def one(v):
        return (v, 1)

    both, line = (0, 2), (0, LINE)

    def part(kind, number):
        axis, first, second = SPLIT[kind]
        full = BLOCK[kind]
        low, high = {
            "first": (0, first),
            "second": (first, second),
            "early": (0, second),
            "late": (second, full[axis]),
        }[number]
        cut = [(0, full[0]), (0, full[1])]
        cut[axis] = (low, high - low)
        return tuple(cut)

    def part_shape(kind, number):
        return tuple(size for _, size in part(kind, number))

    def region(kind, layer, ys, zs, xs, number):
        rows, cols = part(kind, number)
        return weights[kind].at[(layer,) + tuple(pl.ds(*cut) for cut in (ys, zs, xs, rows, cols))]

    def swap(kind, layer, axis, number, ys, zs, xs):
        other_ys, other_xs = (one(1 - y), xs) if axis == "y" else (ys, one(1 - x))
        here = lambda: region(kind, layer, ys, zs, xs, number)
        return [
            moves.make(
                here,
                here,
                y_dev if axis == "y" else x_dev,
                lambda: region(kind, layer, other_ys, zs, other_xs, number),
            )
        ]

    def hop(kind, layer, step, number, ys, xs):
        at = lambda v: (lambda: region(kind, layer, ys, one(v), xs, number))
        return [
            moves.make(
                at(z - step + 1),
                at(z - step + 1),
                up_dev,
                at(z - step),
                (z >= step - 1) & not_last,
                z >= step,
            ),
            moves.make(
                at(z + step - 1),
                at(z + step - 1),
                down_dev,
                at(z + step),
                (z <= LINE - step) & not_first,
                z <= LINE - 1 - step,
            ),
        ]

    def gather_stages(kind, layer):
        a = (kind, layer)
        return [
            hop(*a, 1, "early", one(y), one(x)) + swap(*a, "x", "late", one(y), one(z), one(x)),
            hop(*a, 2, "early", one(y), one(x)) + swap(*a, "y", "late", one(y), one(z), both),
            hop(*a, 3, "early", one(y), one(x)) + hop(*a, 1, "late", both, both),
            swap(*a, "x", "first", one(y), line, one(x))
            + swap(*a, "y", "second", one(y), line, one(x))
            + hop(*a, 2, "late", both, both),
            swap(*a, "y", "first", one(y), line, both)
            + swap(*a, "x", "second", both, line, one(x))
            + hop(*a, 3, "late", both, both),
        ]

    gather_chunks = [
        (("qkv", 0), ("out", 0)),
        (("up", 0),),
        (("down", 0),),
        (("qkv", 1), ("out", 1)),
        (("up", 1),),
        (("down", 1),),
    ]
    gathers = []
    for chunk in gather_chunks:
        stages = [[] for _ in range(5)]
        for kind, layer in chunk:
            for stage, found in zip(stages, gather_stages(kind, layer)):
                stage.extend(found)
        gathers.append(stages)
    ticked = [0]

    def gather_tick():
        tick = ticked[0]
        ticked[0] += 1
        for stage in (4, 3, 2, 1, 0):
            chunk = tick - stage
            if 0 <= chunk < len(gathers):
                if stage:
                    for move in gathers[chunk][stage - 1]:
                        move.wait_recv()
                for move in gathers[chunk][stage]:
                    move.start()

    def need(chunk):
        while ticked[0] <= chunk + 5:
            gather_tick()
        for move in gathers[chunk][4]:
            move.wait_recv()

    def add_into(kind, layer, ys, zs, xs, number, buf):
        rows, cols = part(kind, number)
        count = (ys[1], zs[1], xs[1])

        @pl.loop(0, count[0] * count[1] * count[2])
        def _(i):
            yi, zi, xi = i // (count[1] * count[2]), (i // count[2]) % count[1], i % count[2]
            at = (layer, ys[0] + yi, zs[0] + zi, xs[0] + xi, pl.ds(*rows), pl.ds(*cols))
            total = weights[kind][at].astype(F32) + buf[yi, zi, xi].astype(F32)
            weights[kind][at] = total.astype(BF16)

    def scatter_swap(kind, layer, axis, number, ys, zs, xs, buf):
        away_ys, away_xs = (one(1 - y), xs) if axis == "y" else (ys, one(1 - x))
        stay_ys, stay_xs = (one(y), xs) if axis == "y" else (ys, one(x))
        landing = lambda: buf
        move = moves.make(
            lambda: region(kind, layer, away_ys, zs, away_xs, number),
            landing,
            y_dev if axis == "y" else x_dev,
            landing,
        )
        return [(move, lambda: add_into(kind, layer, stay_ys, zs, stay_xs, number, buf))]

    def scatter_hop(kind, layer, step, number, ys, xs, buf):
        found = []
        for way, device, goes, sends, comes, receives in (
            (0, up_dev, z + LINE - step, (z <= step - 1) & not_last, z + 3 - step, not_first & (z <= step)),
            (1, down_dev, z - LINE + step, (z >= LINE - step) & not_first, z - 3 + step, not_last & (z >= 3 - step)),
        ):
            landing = lambda way=way: buf.at[way, step - 1]
            move = moves.make(
                lambda goes=goes: region(kind, layer, ys, one(goes), xs, number),
                landing,
                device,
                landing,
                sends,
                receives,
            )

            def add(way=way, comes=comes, receives=receives):
                pl.when(receives)(
                    lambda: add_into(kind, layer, ys, one(comes), xs, number, buf.at[way, step - 1])
                )

            found.append((move, add))
        return found

    def scatter_stages(kind, layer):
        a = (kind, layer)
        r = {name: getattr(k, f"{name}_{kind}") for name in ("ry1", "rx1", "rx2", "ry2", "rz", "rz3", "ry3", "rx3")}
        return [
            scatter_swap(*a, "y", "first", both, line, both, r["ry1"])
            + scatter_swap(*a, "x", "second", both, line, both, r["rx2"])
            + scatter_hop(*a, 1, "late", both, both, r["rz3"]),
            scatter_swap(*a, "x", "first", one(y), line, both, r["rx1"])
            + scatter_swap(*a, "y", "second", both, line, one(x), r["ry2"])
            + scatter_hop(*a, 2, "late", both, both, r["rz3"]),
            scatter_hop(*a, 1, "early", one(y), one(x), r["rz"])
            + scatter_hop(*a, 3, "late", both, both, r["rz3"]),
            scatter_hop(*a, 2, "early", one(y), one(x), r["rz"])
            + scatter_swap(*a, "y", "late", both, one(z), both, r["ry3"]),
            scatter_hop(*a, 3, "early", one(y), one(x), r["rz"])
            + scatter_swap(*a, "x", "late", one(y), one(z), both, r["rx3"]),
        ]

    def finish(kind, layer):
        own = weights[kind].at[layer, y, z, x]
        for number in ("early", "late"):
            rows, cols = part(kind, number)
            total = own[pl.ds(*rows), pl.ds(*cols)].astype(F32)
            if kind == "qkv":
                for j in range(3):
                    k.g_qkv[layer, j, pl.ds(*rows), :] = total[:, j * 192 : (j + 1) * 192]
            elif kind == "out":
                if number == "early":
                    k.g_out[layer, 0:16, :] = total[:, 0:768]
                    k.g_out[layer, 16:24, 0:256] = total[0:8, 768:1024]
                    k.g_out[layer, 16:24, 384:640] = total[8:16, 768:1024]
                else:
                    k.g_out[layer, 16:24, 256:384] = total[0:8]
                    k.g_out[layer, 16:24, 640:768] = total[8:16]
            else:
                (k.g_up if kind == "up" else k.g_down)[layer, pl.ds(*rows), :] = total

    scatter_chunks = [
        (("down", 1),),
        (("up", 1),),
        (("out", 1), ("qkv", 1)),
        (("down", 0),),
        (("up", 0),),
        (("out", 0), ("qkv", 0)),
    ]
    scatters, scattered = {}, {}

    def scatter(chunk, stage):
        assert scattered.get(chunk, -1) == stage - 1
        scattered[chunk] = stage
        if stage == 0:
            scatters[chunk] = [[] for _ in range(5)]
            for kind, layer in scatter_chunks[chunk]:
                for into, found in zip(scatters[chunk], scatter_stages(kind, layer)):
                    into.extend(found)
        else:
            for move, add in scatters[chunk][stage - 1]:
                move.wait_recv()
                add()
        if stage < 5:
            for move, _ in scatters[chunk][stage]:
                move.start()
        else:
            for kind, layer in scatter_chunks[chunk]:
                finish(kind, layer)

    def small_step(layer, step):
        if step:
            small_move[layer].wait_recv()
            total = k.small[layer, step - 1] + k.small_in[layer, step - 1]
            if step == 1:
                row = lax.broadcasted_iota(jnp.int32, (16, DM), 0)
                total = jnp.where(row < 6, total, k.small[layer, 0])
            k.small[layer, step] = total
        if step < 5:
            device = (core_dev, x_dev, y_dev, near_dev, far_dev)[step]
            landing = lambda: k.small_in.at[layer, step]
            small_move[layer] = moves.make(lambda: k.small.at[layer, step], landing, device, landing)
            small_move[layer].start()

    small_move = {}

    pack_row = pl.multiple_of(y * (2 * SEQ), SEQ)
    own_a = pl.multiple_of(c * HALF, HALF)
    own_p = pl.multiple_of(SEQ + HALF * y + 128 * c, 128)
    loads = [
        pltpu.make_async_copy(k.wq_in, k.stage_q, k.local.at[0]),
        pltpu.make_async_copy(k.wu_in, k.sum2.at[0, pl.ds(0, 192)], k.local.at[1]),
        pltpu.make_async_copy(k.wd_in, k.sum2.at[0, pl.ds(192, 192)], k.local.at[2]),
        pltpu.make_async_copy(k.wo_in, k.sum2.at[1, pl.ds(0, 48)], k.local.at[3]),
    ]
    x_loads = [
        pltpu.make_async_copy(k.x_in.at[pl.ds(pack_row, SEQ)], k.x_buf.at[pl.ds(0, SEQ)], k.local.at[4]),
        pltpu.make_async_copy(k.x_in.at[pl.ds(SEQ, SEQ)], k.x_buf.at[pl.ds(SEQ, SEQ)], k.local.at[5]),
    ]
    in_a = pl.multiple_of(pack_row + own_a, HALF)
    e_loads = [
        pltpu.make_async_copy(k.e_in.at[pl.ds(in_a, HALF)], k.e_low.at[pl.ds(0, HALF)], k.local.at[6]),
        pltpu.make_async_copy(k.e_in.at[pl.ds(own_p, 128)], k.e_low.at[pl.ds(HALF, 128)], k.local.at[7]),
    ]
    for load in loads + x_loads + e_loads:
        load.start()

    k.bias[y, :, :] = jnp.zeros((8, DM), F32)
    for layer in range(LAYERS):
        k.bias[y, pl.ds(layer, 1), :] = k.upb_in[pl.ds(layer, 1), :]
        k.bias[y, pl.ds(2 + layer, 1), 0:192] = k.qvb_in[layer, 0:1, :]
        k.bias[y, pl.ds(2 + layer, 1), 384:576] = k.qvb_in[layer, 1:2, :]

    loads[0].wait()
    loads[3].wait()
    for layer in range(LAYERS):
        for j in range(3):
            k.w_qkv[layer, y, z, x, :, j * 192 : (j + 1) * 192] = k.stage_q[layer, j].astype(BF16)
        rows = k.sum2[1, pl.ds(layer * 24, 24), :]
        k.w_out[layer, y, z, x, :, 0:768] = rows[0:16].astype(BF16)
        k.w_out[layer, y, z, x, :, 768:1152] = jnp.concatenate([rows[16:24, 0:384], rows[16:24, 384:768]], axis=0).astype(BF16)
    loads[1].wait()
    loads[2].wait()
    for layer in range(LAYERS):
        k.w_up[layer, y, z, x] = k.sum2[0, pl.ds(layer * 96, 96), :].astype(BF16)
        k.w_down[layer, y, z, x] = k.sum2[0, pl.ds(192 + layer * 96, 96), :].astype(BF16)

    pl.semaphore_wait(barrier, 4 + not_last.astype(jnp.int32) + not_first.astype(jnp.int32))
    bias_move = moves.make(
        lambda: k.bias.at[pl.ds(y, 1)], lambda: k.bias.at[pl.ds(y, 1)], y_dev, lambda: k.bias.at[pl.ds(1 - y, 1)]
    )
    bias_move.start()
    gather_tick()

    for slot in range(2):
        pack = 1 if slot else 2 * y
        columns = lax.broadcasted_iota(jnp.int32, (8, SEQ), 1)
        rows = lax.broadcasted_iota(jnp.int32, (SEQ, 128), 0)
        pair_col, pair_row = jnp.zeros((8, SEQ), F32), jnp.zeros((SEQ, 128), F32)
        end = jnp.int32(0)
        for j in range(4):
            end = end + k.lens[pack, j]
            pair_col += jnp.where(columns >= end, 1.0, 0.0)
            pair_row += jnp.where(rows >= end, 1.0, 0.0)
        k.pair_col[slot] = pair_col
        k.pair_row[slot] = pair_row
    for layer in range(LAYERS):
        k.small[layer, 0] = jnp.zeros((16, DM), F32)
    gather_tick()

    for load in x_loads:
        load.wait()
    k.res[0:HALF, :] = k.x_buf[pl.ds(own_a, HALF), :].astype(F32)
    k.res[HALF:OWN, :] = k.x_buf[pl.ds(own_p, 128), :].astype(F32)
    bias_move.wait_recv()

    def gather_pair(buf, layer=None):
        at = lambda slot: (lambda: buf.at[pl.ds(slot, 1)])
        move = moves.make(at(c), at(c), core_dev, at(1 - c))
        move.start()
        return move

    def gather_rows(buf):
        rows = lambda start, size: (lambda: buf.at[pl.ds(pl.multiple_of(start, 128), size)])
        other_p = SEQ + HALF * (1 - y) + 128 * c
        mine = rows(own_p, 128)
        relayed = rows(other_p, 128)
        across = moves.make(mine, mine, y_dev, relayed)
        across.start()
        first = moves.make(rows(own_a, HALF), rows(own_a, HALF), core_dev, rows((1 - c) * HALF, HALF))
        first.start()
        second = moves.make(mine, mine, core_dev, rows(SEQ + HALF * y + 128 * (1 - c), 128))
        second.start()

        def relay():
            across.wait_recv()
            third = moves.make(relayed, relayed, core_dev, rows(SEQ + HALF * (1 - y) + 128 * (1 - c), 128))
            third.start()
            return third

        return across, first, second, relay

    def sum_rows(part_a, part_p):
        for other in range(2):
            start = pl.multiple_of(HALF * other + 128 * (1 - c), 128)
            k.ex_s[HALF + 128 * other : HALF + 128 * (other + 1), :] = part_p(start).astype(BF16)
        piece = lambda ref, start, size: (lambda: ref.at[pl.ds(start, size)])
        shared = moves.make(piece(k.ex_s, HALF, HALF), piece(k.ex_r, HALF, HALF), core_dev, piece(k.ex_r, HALF, HALF))
        shared.start()
        k.ex_s[0:HALF, :] = part_a(pl.multiple_of((1 - c) * HALF, HALF)).astype(BF16)
        whole = moves.make(piece(k.ex_s, 0, HALF), piece(k.ex_r, 0, HALF), core_dev, piece(k.ex_r, 0, HALF))
        whole.start()
        start = pl.multiple_of(HALF * (1 - y) + 128 * c, 128)
        away = part_p(start)
        shared.wait_recv()
        away = away + k.ex_r[pl.ds(pl.multiple_of(HALF + 128 * (1 - y), 128), 128), :].astype(F32)
        k.ey_s[...] = away.astype(BF16)
        across = moves.make(lambda: k.ey_s, lambda: k.ey_r, y_dev, lambda: k.ey_r)
        across.start()
        start = pl.multiple_of(HALF * y + 128 * c, 128)
        k.cur[HALF:OWN, :] = part_p(start) + k.ex_r[pl.ds(pl.multiple_of(HALF + 128 * y, 128), 128), :].astype(F32)
        k.cur[0:HALF, :] = part_a(own_a)
        whole.wait_recv()
        k.cur[0:HALF, :] += k.ex_r[0:HALF, :].astype(F32)
        across.wait_recv()
        k.cur[HALF:OWN, :] += k.ey_r[...].astype(F32)
        moves.sent(shared, whole, across)

    def sum_pair(fill):
        def to_send(cols, value):
            k.ex_s[0:OWN, cols] = value.astype(BF16)

        def to_keep(cols, value):
            k.cur[:, cols] = value

        fill(1 - c, to_send)
        move = moves.make(
            lambda: k.ex_s.at[pl.ds(0, OWN)], lambda: k.ex_r.at[pl.ds(0, OWN)], core_dev, lambda: k.ex_r.at[pl.ds(0, OWN)]
        )
        move.start()
        fill(c, to_keep)

        def end():
            move.wait_recv()
            k.cur[...] += k.ex_r[0:OWN, :].astype(F32)
            moves.sent(move)

        return end

    def spread(low, out, sems):
        piece = lambda ref, start, size: (lambda: ref.at[pl.ds(pl.multiple_of(start, 128), size)])
        locals_, started, relays = [], [], []
        other_a, other_p = (1 - y) * (2 * SEQ) + c * HALF, SEQ + HALF * (1 - y) + 128 * c
        for index, (start, size, at, far) in enumerate(((0, HALF, in_a, other_a), (HALF, 128, own_p, other_p))):
            copy = pltpu.make_async_copy(piece(low, start, size)(), piece(out, at, size)(), k.local.at[sems + index])
            copy.start()
            locals_.append(copy)
            across = moves.make(piece(low, start, size), piece(out, at, size), y_dev, piece(out, far, size))
            across.start()
            step = HALF if size == HALF else 128
            mate = at + (1 - 2 * c) * step
            beside = moves.make(piece(low, start, size), piece(out, at, size), core_dev, piece(out, mate, size))
            beside.start()
            started.append(beside)
            relays.append((across, far, far + (1 - 2 * c) * step, size))

        def relay():
            for across, far, mate, size in relays:
                across.wait_recv()
                move = moves.make(piece(out, far, size), piece(out, far, size), core_dev, piece(out, mate, size))
                move.start()
                started.append(move)

        def end():
            for copy in locals_:
                copy.wait()
            for move in started:
                move.wait_recv()

        return relay, end

    def save(slot, src, dst):
        copy = pltpu.make_async_copy(src, dst, k.local.at[slot])
        copy.start()
        return copy

    row_tiles = OWN // 128
    saves = []
    for layer in range(LAYERS):
        if layer == 1:
            k.x_buf[pl.ds(own_a, HALF), :] = k.res[0:HALF, :].astype(BF16)
            k.x_buf[pl.ds(own_p, 128), :] = k.res[HALF:OWN, :].astype(BF16)
            _, first, second, relay = gather_rows(k.x_buf)
            third = relay()
        need(3 * layer)
        if layer == 1:
            for move in (first, second, third):
                move.wait_recv()

        for group in range(2):
            for zi in range(LINE):
                for xi in range(2):
                    block = k.w_out[layer, group, zi, xi].astype(F32)
                    at = (zi * 2 + xi) * 24
                    k.unpack[at : at + 16, :] = block[:, 0:768]
                    k.unpack[at + 16 : at + 24, 0:384] = block[0:8, 768:1152]
                    k.unpack[at + 16 : at + 24, 384:768] = block[8:16, 768:1152]
            k.w_o[layer, group] = k.unpack[...].astype(BF16)

        @pl.loop(0, 6)
        def _(i):
            unit, half = i // 2, i % 2
            group = jnp.where(unit == 2, y, unit)
            start = pl.multiple_of(jnp.where(unit == 2, SEQ, 0) + half * HALF, HALF)
            made = dot(k.x_buf[pl.ds(start, HALF), :], flat(k.w_qkv[layer, group]))
            made = made + k.bias[group, 2 + layer : 3 + layer, 0:576]
            k.qkv[layer, unit, pl.ds(pl.multiple_of(half * HALF, HALF), HALF), :] = made.astype(BF16)

        if layer == 1:
            saves[0].wait()

        @pl.loop(0, 6)
        def _(i):
            unit, half = i // 2, i % 2
            slot = jnp.where(unit == 2, 1, 0)
            rows = pl.ds(pl.multiple_of(half * HALF, HALF), HALF)
            allowed = k.pair_row[slot, rows, 0:1] == k.pair_col[slot, 0:1, :]
            for head in range(3):
                low, high = head * HD, (head + 1) * HD
                queries = k.qkv[layer, unit, rows, low:high]
                key_rows = k.qkv[layer, unit, :, 192 + low : 192 + high]
                values = k.qkv[layer, unit, :, 384 + low : 384 + high]
                scores = jnp.where(allowed, dot_nt(queries, key_rows) * HD ** (-0.5), -1e30)
                top = jnp.max(scores, axis=-1, keepdims=True)
                probs = jnp.exp(scores - top)
                probs = (probs * (1.0 / jnp.sum(probs, axis=-1, keepdims=True))).astype(BF16)
                k.probs[unit * 3 + head, rows, :] = probs
                k.merged[layer, unit, rows, low:high] = dot(probs, values).astype(BF16)

        if layer == 0:
            saves.append(save(8, k.probs, k.probs_hbm))

        sum_rows(
            lambda start: dot(k.merged[layer, 0, pl.ds(start, HALF), :], k.w_o[layer, 0])
            + dot(k.merged[layer, 1, pl.ds(start, HALF), :], k.w_o[layer, 1]),
            lambda start: dot(k.merged[layer, 2, pl.ds(start, 128), :], k.w_o[layer, y]),
        )

        @pl.loop(0, row_tiles)
        def _(i):
            rows = pl.ds(pl.multiple_of(i * 128, 128), 128)
            total = k.res[rows, :] + k.cur[rows, :] + k.vec[layer, 4:5, :]
            k.sum1[layer, rows, :] = total
            normed = norm_stats(total)[0] * k.vec[layer, 0:1, :] + k.vec[layer, 1:2, :]
            k.res[rows, :] = normed
            k.nlow[layer, c, rows, :] = normed.astype(BF16)

        mate_rows = gather_pair(k.nlow.at[layer])
        need(3 * layer + 1)
        if layer == 1:
            saves[1].wait()
            saves[2].wait()
        for order in range(2):
            slot = c if order == 0 else 1 - c
            if order:
                mate_rows.wait_recv()

            @pl.loop(0, 6)
            def _(i):
                group, cols = i // 3, pl.ds(pl.multiple_of((i % 3) * 256, 256), 256)
                made = dot(k.nlow[layer, slot], flat(k.w_up[layer, group, :, :, :, cols]))
                made = made + k.bias[group, layer : layer + 1, cols]
                act, slope = gelu_and_slope(made)
                k.act[group, slot, :, cols] = act.astype(BF16)
                k.slope[group, slot, :, cols] = slope.astype(BF16)

        if layer == 0:
            saves.append(save(9, k.act, k.act_hbm))
            saves.append(save(10, k.slope, k.slope_hbm))
        need(3 * layer + 2)

        def down_rows(slot, store):
            @pl.loop(0, 3)
            def _(i):
                cols = pl.ds(pl.multiple_of(i * 256, 256), 256)
                made = dot(k.act[0, slot], flat(k.w_down[layer, 0, :, :, :, cols]))
                store(cols, made + dot(k.act[1, slot], flat(k.w_down[layer, 1, :, :, :, cols])))

        sum_pair(down_rows)()

        @pl.loop(0, row_tiles)
        def _(i):
            rows = pl.ds(pl.multiple_of(i * 128, 128), 128)
            total = k.res[rows, :] + k.cur[rows, :] + k.vec[layer, 5:6, :]
            k.sum2[layer, rows, :] = total
            k.res[rows, :] = norm_stats(total)[0] * k.vec[layer, 2:3, :] + k.vec[layer, 3:4, :]

    moves.drain()
    k.a_low[...] = k.res[...].astype(BF16)
    act_relay, act_end = spread(k.a_low, k.activations, 11)
    for load in e_loads:
        load.wait()
    k.res[...] = k.e_low[...].astype(F32)

    def norm_back(layer, sums, gain_row, bias_row, low_out):
        @pl.loop(0, row_tiles)
        def _(i):
            rows = pl.ds(pl.multiple_of(i * 128, 128), 128)
            e = k.res[rows, :]
            xhat, scale = norm_stats(sums[layer, rows, :])
            h = e * k.vec[layer, gain_row : gain_row + 1, :]
            mean_h = jnp.mean(h, axis=-1, keepdims=True)
            mean_hx = jnp.mean(h * xhat, axis=-1, keepdims=True)
            grad = scale * (h - mean_h - xhat * mean_hx)
            k.res[rows, :] = grad
            low_out(i, rows, grad.astype(BF16))
            acc = k.small.at[layer, 0]
            acc[gain_row : gain_row + 1, :] += jnp.sum(e * xhat, axis=0, keepdims=True)
            acc[gain_row + 1 : gain_row + 2, :] += jnp.sum(e, axis=0, keepdims=True)
            acc[bias_row : bias_row + 1, :] += jnp.sum(grad, axis=0, keepdims=True)

    restores = {}
    for layer in (1, 0):
        base = 0 if layer == 1 else 3

        def to_second(i, rows, low):
            k.lsec[c, rows, :] = low

        norm_back(layer, k.sum2, 2, 5, to_second)
        mate_rows = gather_pair(k.lsec)
        if layer == 0:
            scatter(0, 4)
            scatter(1, 3)
            scatter(2, 1)
            restores["act"].wait()
            restores["slope"].wait()
        for order in range(2):
            slot = c if order == 0 else 1 - c
            if order:
                mate_rows.wait_recv()
                moves.sent(mate_rows)

            @pl.loop(0, 4)
            def _(i):
                group, tile = i // 2, i % 2
                cols = pl.ds(pl.multiple_of(tile * OWN, OWN), OWN)
                back = dot_nt(k.lsec[slot], flat(k.w_down[layer, group, pl.ds(tile * 2, 2)]))
                grad = (back * k.slope[group, slot, :, cols].astype(F32)).astype(BF16)
                k.slope[group, slot, :, cols] = grad
                k.small[layer, 0, pl.ds(6 + group, 1), cols] += jnp.sum(grad.astype(F32), axis=0, keepdims=True)

        def normed_rows(slot, store):
            @pl.loop(0, 2)
            def _(tile):
                cols = pl.ds(pl.multiple_of(tile * OWN, OWN), OWN)
                made = dot_nt(k.slope[0, slot], flat(k.w_up[layer, 0, pl.ds(tile * 2, 2)]))
                store(cols, made + dot_nt(k.slope[1, slot], flat(k.w_up[layer, 1, pl.ds(tile * 2, 2)])))

        end_normed = sum_pair(normed_rows)

        @pl.loop(0, 4)
        def _(i):
            group, tile = i // 2, i % 2
            cols = pl.ds(pl.multiple_of(tile * OWN, OWN), OWN)
            made = dot_tn(flat(k.act[group, :, :, cols]), flat(k.lsec[...]))
            k.w_down[layer, group, pl.ds(tile * 2, 2)] = made.astype(BF16).reshape((2, 2, 96, 768))

        if layer == 0:
            scatter(0, 5)
            scatter(1, 4)
            scatter(2, 2)
        scatter(base, 0)
        if layer == 1:
            restores["act"] = save(9, k.act_hbm, k.act)
        end_normed()

        @pl.loop(0, row_tiles)
        def _(i):
            rows = pl.ds(pl.multiple_of(i * 128, 128), 128)
            k.res[rows, :] += k.cur[rows, :]

        def to_first(i, rows, low):
            start = jnp.where(i == 2, own_p, own_a + i * 128)
            k.lfirst[pl.ds(pl.multiple_of(start, 128), 128), :] = low

        norm_back(layer, k.sum1, 0, 4, to_first)
        across, first, second, relay = gather_rows(k.lfirst)

        @pl.loop(0, 4)
        def _(i):
            group, tile = i // 2, i % 2
            cols = pl.ds(pl.multiple_of(tile * OWN, OWN), OWN)
            made = dot_tn(flat(k.nlow[layer, :, :, cols]), flat(k.slope[group]))
            k.w_up[layer, group, pl.ds(tile * 2, 2)] = made.astype(BF16).reshape((2, 2, 96, 768))

        third = relay()
        if layer == 0:
            scatter(1, 5)
            scatter(2, 3)
            scatter(3, 1)
        scatter(base + 1, 0)
        if layer == 1:
            restores["slope"] = save(10, k.slope_hbm, k.slope)
            act_relay()
        for move in (first, second, third):
            move.wait_recv()
        moves.sent(across, first, second, third)

        @pl.loop(0, 6)
        def _(i):
            unit, half = i // 2, i % 2
            group = jnp.where(unit == 2, y, unit)
            start = pl.multiple_of(jnp.where(unit == 2, SEQ, 0) + half * HALF, HALF)
            rows = pl.ds(pl.multiple_of(half * HALF, HALF), HALF)
            k.dmerged[unit, rows, :] = dot_nt(k.lfirst[pl.ds(start, HALF), :], k.w_o[layer, group]).astype(BF16)

        for order in range(2):
            group = y if order == 0 else 1 - y
            made = dot_tn(k.merged[layer, group], k.lfirst[0:SEQ, :])
            if order == 0:
                made = made + dot_tn(k.merged[layer, 2], k.lfirst[SEQ : 2 * SEQ, :])
            for zi in range(LINE):
                for xi in range(2):
                    rows = made[(zi * 2 + xi) * 24 : (zi * 2 + xi + 1) * 24]
                    k.w_out[layer, group, zi, xi, :, 0:768] = rows[0:16].astype(BF16)
                    k.w_out[layer, group, zi, xi, :, 768:1152] = jnp.concatenate(
                        [rows[16:24, 0:384], rows[16:24, 384:768]], axis=0
                    ).astype(BF16)

        if layer == 0:
            restores["probs"].wait()

        @pl.loop(0, 3)
        def _(unit):
            group = jnp.where(unit == 2, y, unit)
            for head in range(3):
                low, high = head * HD, (head + 1) * HD
                key_rows = k.qkv[layer, unit, :, 192 + low : 192 + high]
                values = k.qkv[layer, unit, :, 384 + low : 384 + high]
                grad_keys = jnp.zeros((SEQ, HD), F32)
                grad_values = jnp.zeros((SEQ, HD), F32)
                for half in range(2):
                    rows = slice(half * HALF, (half + 1) * HALF)
                    queries = k.qkv[layer, unit, rows, low:high]
                    grad_out = k.dmerged[unit, rows, low:high]
                    probs = k.probs[unit * 3 + head, rows, :]
                    row_dot = jnp.sum(
                        grad_out.astype(F32) * k.merged[layer, unit, rows, low:high].astype(F32), axis=-1, keepdims=True
                    )
                    grad_probs = dot_nt(grad_out, values)
                    grad_scores = (probs.astype(F32) * (grad_probs - row_dot)).astype(BF16)
                    grad_values += dot_tn(probs, grad_out)
                    grad_keys += dot_tn(grad_scores, queries)
                    grad_queries = (dot(grad_scores, key_rows) * HD ** (-0.5)).astype(BF16)
                    k.qkv[layer, unit, rows, low:high] = grad_queries
                grad_keys = (grad_keys * HD ** (-0.5)).astype(BF16)
                k.qkv[layer, unit, :, 192 + low : 192 + high] = grad_keys
                k.qkv[layer, unit, :, 384 + low : 384 + high] = grad_values.astype(BF16)
            for j, row in ((0, 8), (2, 9)):
                sums = jnp.sum(k.qkv[layer, unit, :, j * 192 : (j + 1) * 192].astype(F32), axis=0, keepdims=True)
                k.small[layer, 0, pl.ds(row + 2 * group, 1), 0:192] += sums

            if layer == 1:
                pl.when(unit == 0)(lambda: scatter(0, 1))

                @pl.when(unit == 1)
                def _():
                    scatter(0, 2)
                    scatter(1, 1)

                @pl.when(unit == 2)
                def _():
                    scatter(0, 3)
                    scatter(1, 2)
            else:

                @pl.when(unit == 0)
                def _():
                    scatter(2, 4)
                    scatter(3, 2)
                    scatter(4, 1)

                @pl.when(unit == 1)
                def _():
                    scatter(2, 5)
                    scatter(3, 3)

                pl.when(unit == 2)(lambda: scatter(4, 2))

        small_step(layer, 0)
        if layer == 1:
            restores["probs"] = save(8, k.probs_hbm, k.probs)

        sum_rows(
            lambda start: dot_nt(k.qkv[layer, 0, pl.ds(start, HALF), :], flat(k.w_qkv[layer, 0]))
            + dot_nt(k.qkv[layer, 1, pl.ds(start, HALF), :], flat(k.w_qkv[layer, 1])),
            lambda start: dot_nt(k.qkv[layer, 2, pl.ds(start, 128), :], flat(k.w_qkv[layer, y])),
        )
        if layer == 0:
            x_load_again[0].wait()
            x_load_again[1].wait()
        for order in range(2):
            group = y if order == 0 else 1 - y

            @pl.loop(0, 2)
            def _(tile):
                cols = pl.ds(pl.multiple_of(tile * OWN, OWN), OWN)
                made = dot_tn(k.x_buf[0:SEQ, cols], k.qkv[layer, group])
                if order == 0:
                    made = made + dot_tn(k.x_buf[SEQ : 2 * SEQ, cols], k.qkv[layer, 2])
                k.w_qkv[layer, group, pl.ds(tile * 2, 2)] = made.astype(BF16).reshape((2, 2, 96, 576))

        scatter(base + 2, 0)
        if layer == 1:
            x_load_again = [
                pltpu.make_async_copy(k.x_in.at[pl.ds(pack_row, SEQ)], k.x_buf.at[pl.ds(0, SEQ)], k.local.at[4]),
                pltpu.make_async_copy(k.x_in.at[pl.ds(SEQ, SEQ)], k.x_buf.at[pl.ds(SEQ, SEQ)], k.local.at[5]),
            ]
            for load in x_load_again:
                load.start()
            act_end()
        small_step(layer, 1)

        @pl.loop(0, row_tiles)
        def _(i):
            rows = pl.ds(pl.multiple_of(i * 128, 128), 128)
            k.res[rows, :] += k.cur[rows, :]

    k.e_low[...] = k.res[...].astype(BF16)
    grad_relay, grad_end = spread(k.e_low, k.input_grad, 13)
    scatter(3, 4)
    scatter(4, 3)
    scatter(5, 1)
    for layer in range(LAYERS):
        small_step(layer, 2)
    scatter(3, 5)
    scatter(4, 4)
    scatter(5, 2)
    for layer in range(LAYERS):
        small_step(layer, 3)
    grad_relay()
    scatter(4, 5)
    scatter(5, 3)
    for layer in range(LAYERS):
        small_step(layer, 4)
    scatter(5, 4)
    for layer in range(LAYERS):
        small_step(layer, 5)
    small_squares = jnp.float32(0)
    for layer in range(LAYERS):
        total = k.small.at[layer, 5]
        rows = total[0:6, :]
        small_squares += jnp.sum(rows * rows) / (LINE * 8)
        k.small_out[layer, 0:6, :] = rows
        for row, source in ((6, 6 + y), (7, 8 + 2 * y), (8, 9 + 2 * y)):
            values = total[pl.ds(source, 1), :]
            small_squares += jnp.sum(values * values) / (LINE * 2)
            k.small_out[layer, row : row + 1, :] = values
        k.small_out[layer, 9:16, :] = jnp.zeros((7, DM), F32)
    grad_end()
    scatter(5, 5)
    squares = small_squares
    for ref in (k.g_qkv, k.g_out, k.g_up, k.g_down):
        for layer in range(LAYERS):
            values = ref[layer]
            squares += jnp.sum(values * values)
    k.sq[0] = jnp.full((8, 128), squares, F32)
    for step, device in enumerate((core_dev, x_dev, y_dev, near_dev, far_dev)):
        landing = lambda: k.sq_in.at[step]
        move = moves.make(lambda: k.sq.at[step], landing, device, landing)
        move.start()
        move.wait_recv()
        k.sq[step + 1] = k.sq[step] + k.sq_in[step]
    k.squares[...] = k.sq[5]
    moves.drain()


def kernel_call(inputs, out_grad, lens, w_q, w_o, w_u, w_d, vec, qvb, upb):
    any_ = pl.BlockSpec(memory_space=pl.ANY)
    vmem = pl.BlockSpec(memory_space=pltpu.VMEM)
    smem = pl.BlockSpec(memory_space=pltpu.SMEM)
    ins = [
        ("x_in", inputs, any_),
        ("e_in", out_grad, any_),
        ("lens", lens, smem),
        ("wq_in", w_q, any_),
        ("wo_in", w_o.reshape(LAYERS * 24, DM), any_),
        ("wu_in", w_u.reshape(LAYERS * 96, DM), any_),
        ("wd_in", w_d.reshape(LAYERS * 96, DM), any_),
        ("vec", vec, vmem),
        ("qvb_in", qvb, vmem),
        ("upb_in", upb, vmem),
    ]
    outs = [
        ("activations", (3 * SEQ, DM), BF16, any_),
        ("input_grad", (3 * SEQ, DM), BF16, any_),
        ("g_qkv", (LAYERS, 3, 96, 192), F32, vmem),
        ("g_out", (LAYERS, 24, DM), F32, vmem),
        ("g_up", (LAYERS, 96, DM), F32, vmem),
        ("g_down", (LAYERS, 96, DM), F32, vmem),
        ("small_out", (LAYERS, 16, DM), F32, vmem),
        ("squares", (8, 128), F32, vmem),
        ("probs_hbm", (9, SEQ, SEQ), BF16, any_),
        ("act_hbm", (2, 2, OWN, DM), BF16, any_),
        ("slope_hbm", (2, 2, OWN, DM), BF16, any_),
    ]
    scratch = [
        ("w_qkv", (LAYERS, 2, LINE, 2, 96, 576), BF16),
        ("w_out", (LAYERS, 2, LINE, 2, 16, 1152), BF16),
        ("w_up", (LAYERS, 2, LINE, 2, 96, 768), BF16),
        ("w_down", (LAYERS, 2, LINE, 2, 96, 768), BF16),
        ("w_o", (LAYERS, 2, 192, DM), BF16),
        ("unpack", (192, DM), F32),
        ("stage_q", (LAYERS, 3, 96, 192), F32),
        ("x_buf", (2 * SEQ, DM), BF16),
        ("qkv", (LAYERS, 3, SEQ, 576), BF16),
        ("probs", (9, SEQ, SEQ), BF16),
        ("merged", (LAYERS, 3, SEQ, 192), BF16),
        ("sum1", (LAYERS, OWN, DM), F32),
        ("sum2", (LAYERS, OWN, DM), F32),
        ("nlow", (LAYERS, 2, OWN, DM), BF16),
        ("act", (2, 2, OWN, DM), BF16),
        ("slope", (2, 2, OWN, DM), BF16),
        ("res", (OWN, DM), F32),
        ("cur", (OWN, DM), F32),
        ("a_low", (OWN, DM), BF16),
        ("e_low", (OWN, DM), BF16),
        ("lsec", (2, OWN, DM), BF16),
        ("lfirst", (2 * SEQ, DM), BF16),
        ("dmerged", (3, SEQ, 192), BF16),
        ("ex_s", (SEQ, DM), BF16),
        ("ex_r", (SEQ, DM), BF16),
        ("ey_s", (128, DM), BF16),
        ("ey_r", (128, DM), BF16),
        ("bias", (2, 8, DM), F32),
        ("pair_col", (2, 8, SEQ), F32),
        ("pair_row", (2, SEQ, 128), F32),
        ("small", (LAYERS, 6, 16, DM), F32),
        ("small_in", (LAYERS, 5, 16, DM), F32),
        ("sq", (6, 8, 128), F32),
        ("sq_in", (5, 8, 128), F32),
    ]
    for kind in KINDS:
        axis, first, second = SPLIT[kind]

        def cut(size):
            shape = list(BLOCK[kind])
            shape[axis] = size
            return tuple(shape)

        p_1, p_2 = cut(first), cut(second - first)
        p_12, p_3 = cut(second), cut(BLOCK[kind][axis] - second)
        scratch += [
            (f"ry1_{kind}", (1, LINE, 2) + p_1, BF16),
            (f"rx1_{kind}", (1, LINE, 1) + p_1, BF16),
            (f"rx2_{kind}", (2, LINE, 1) + p_2, BF16),
            (f"ry2_{kind}", (1, LINE, 1) + p_2, BF16),
            (f"rz_{kind}", (2, 3, 1, 1, 1) + p_12, BF16),
            (f"rz3_{kind}", (2, 3, 2, 1, 2) + p_3, BF16),
            (f"ry3_{kind}", (1, 1, 2) + p_3, BF16),
            (f"rx3_{kind}", (1, 1, 1) + p_3, BF16),
        ]
    names = [n for n, *_ in ins] + [n for n, *_ in outs] + [n for n, *_ in scratch] + ["send", "recv", "local"]
    made = pl.pallas_call(
        lambda *refs: fused(names, *refs),
        out_shape=[jax.ShapeDtypeStruct(shape, dtype) for _, shape, dtype, _ in outs],
        in_specs=[spec for *_, spec in ins],
        out_specs=[spec for *_, spec in outs],
        scratch_shapes=[pltpu.VMEM(shape, dtype) for _, shape, dtype in scratch]
        + [
            pltpu.SemaphoreType.DMA((SEMS,)),
            pltpu.SemaphoreType.DMA((SEMS,)),
            pltpu.SemaphoreType.DMA((16,)),
        ],
        compiler_params=pltpu.CompilerParams(
            collective_id=0, has_side_effects=True, vmem_limit_bytes=VMEM_BYTES
        ),
        name="encoder_step",
    )(*[value for _, value, _ in ins])
    return types.SimpleNamespace(**dict(zip([n for n, *_ in outs], made)))


VMEM_BYTES = 64 * 2**20 - 2**17


def kernel_body(
    inputs,
    pair_lengths,
    out_grad,
    w_qkv,
    m_qkv,
    v_qkv,
    w_out,
    m_out,
    v_out,
    w_up,
    m_up,
    v_up,
    w_down,
    m_down,
    v_down,
    vectors,
    m_vectors,
    v_vectors,
    qv_bias,
    m_qv_bias,
    v_qv_bias,
    up_bias,
    m_up_bias,
    v_up_bias,
):
    turn = lambda v: jnp.transpose(v, (0, 2, 1, 3))
    w_qkv, m_qkv, v_qkv = turn(w_qkv), turn(m_qkv), turn(v_qkv)
    made = kernel_call(inputs, out_grad, pair_lengths, w_qkv, w_out, w_up, w_down, vectors, qv_bias, up_bias)
    grad_norm = jnp.sqrt(made.squares[0, 0])
    factor = jnp.minimum(1.0, CLIP_LIMIT / grad_norm)
    new_qkv = adamw(w_qkv, m_qkv, v_qkv, made.g_qkv, factor, LEARN_RATE, WEIGHT_DECAY)
    new_out = adamw(w_out, m_out, v_out, made.g_out, factor, LEARN_RATE, WEIGHT_DECAY)
    new_up = adamw(w_up, m_up, v_up, made.g_up, factor, LEARN_RATE, WEIGHT_DECAY)
    new_down = adamw(w_down, m_down, v_down, made.g_down, factor, LEARN_RATE, WEIGHT_DECAY)
    small = made.small_out
    new_vec = adamw(vectors, m_vectors, v_vectors, small[:, 0:6], factor, VECTOR_RATE, 0.0)
    new_qv = adamw(qv_bias, m_qv_bias, v_qv_bias, small[:, 7:9, 0:192], factor, VECTOR_RATE, 0.0)
    new_upb = adamw(up_bias, m_up_bias, v_up_bias, small[:, 6], factor, VECTOR_RATE, 0.0)
    return (
        made.activations,
        made.input_grad.astype(F32),
        grad_norm,
        *[turn(v) for v in new_qkv],
        *new_out,
        *new_up,
        *new_down,
        *new_vec,
        *new_qv,
        *new_upb,
    )


def solution(mesh):
    rows, matrix = P("dp", None), P(None, ("tensor", "dp"), None)
    qkv, up = P(None, "dp", None, "tensor"), P(None, "dp", "tensor")
    heads, hidden = P(None, None, "tensor"), P(None, "tensor")
    weights = (qkv,) * 3 + (matrix,) * 3 + (up,) * 3 + (matrix,) * 3
    smalls = (P(),) * 3 + (heads,) * 3 + (hidden,) * 3
    fits = mesh.shape["dp"] == 2 * LINE and mesh.shape["tensor"] == 4
    return jax.shard_map(
        kernel_body if fits else body,
        mesh=mesh,
        in_specs=(rows, rows, rows) + weights + smalls,
        out_specs=(rows, rows, P()) + weights + smalls,
        check_vma=False,
    )
```

```python
import math
import types

import jax
import jax.numpy as jnp
from jax import lax
from jax.experimental import pallas as pl
from jax.experimental.pallas import tpu as pltpu
from jax.sharding import PartitionSpec as P

HD = 64
SEQ = 512
LAYERS = 2
STEP = 10


NORM_EPS = 1e-05
CLIP_LIMIT = 0.05
BETA_ONE = 0.9
BETA_TWO = 0.999
LEARN_RATE = 0.1
VECTOR_RATE = 1.0
WEIGHT_DECAY = 0.01
ADAM_EPS = 1e-08


def layer_norm(rows_in, gain, shift):
    center = rows_in - jnp.mean(rows_in, axis=-1, keepdims=True)
    spread = jnp.mean(center * center, axis=-1, keepdims=True)
    return center * lax.rsqrt(spread + NORM_EPS) * gain + shift


def gelu_exact(pre_values):
    return jax.nn.gelu(pre_values, approximate=False)


def pair_mask(lengths):
    ends = jnp.cumsum(lengths)
    positions = jnp.arange(SEQ, dtype=jnp.int32)
    pair_of = jnp.sum((positions[:, None] >= ends[None, :]).astype(jnp.int32), axis=1)
    return pair_of[:, None] == pair_of[None, :]


def pack_scores(queries, key_rows, masks):
    scores = jnp.einsum(
        "pqhe,pkhe->phqk", queries, key_rows, preferred_element_type=jnp.float32
    ) * HD ** (-0.5)
    return jnp.where(masks[:, None], scores, -1e30)


def attend(queries, key_rows, values, masks):
    scores = pack_scores(queries, key_rows, masks)
    top = jnp.max(scores, axis=-1, keepdims=True)
    weights = jnp.exp(scores - top)
    total = jnp.sum(weights, axis=-1, keepdims=True)
    probs = weights / total
    attended = jnp.einsum(
        "phqk,pkhe->pqhe", probs.astype(jnp.bfloat16), values, preferred_element_type=jnp.float32
    )
    return (attended, top + jnp.log(total))


def attend_back(queries, key_rows, values, grad_attended, log_total, masks):
    scores = pack_scores(queries, key_rows, masks)
    probs = jnp.exp(scores - log_total)
    grad_values = jnp.einsum(
        "phqk,pqhe->pkhe",
        probs.astype(jnp.bfloat16),
        grad_attended,
        preferred_element_type=jnp.float32,
    )
    grad_probs = jnp.einsum(
        "pqhe,pkhe->phqk", grad_attended, values, preferred_element_type=jnp.float32
    )
    row_dot = jnp.sum(grad_probs * probs, axis=-1, keepdims=True)
    grad_scores = (probs * (grad_probs - row_dot)).astype(jnp.bfloat16)
    grad_queries = jnp.einsum(
        "phqk,pkhe->pqhe", grad_scores, key_rows, preferred_element_type=jnp.float32
    ) * HD ** (-0.5)
    grad_keys = jnp.einsum(
        "phqk,pqhe->pkhe", grad_scores, queries, preferred_element_type=jnp.float32
    ) * HD ** (-0.5)
    return (
        grad_queries.astype(jnp.bfloat16),
        grad_keys.astype(jnp.bfloat16),
        grad_values.astype(jnp.bfloat16),
    )


def layer_forward(stream, qkv_w, out_w, up_w, down_w, vector_rows, qv_rows, up_row, masks):
    row_count = stream.shape[0]
    pack_count = masks.shape[0]
    width = out_w.shape[0]
    group_heads = width // HD
    stream_low = stream.astype(jnp.bfloat16)
    project = jnp.einsum("td,dcn->tcn", stream_low, qkv_w, preferred_element_type=jnp.float32)
    queries = (
        (project[:, 0] + qv_rows[0]).astype(jnp.bfloat16).reshape(pack_count, SEQ, group_heads, HD)
    )
    key_rows = project[:, 1].astype(jnp.bfloat16).reshape(pack_count, SEQ, group_heads, HD)
    values = (
        (project[:, 2] + qv_rows[1]).astype(jnp.bfloat16).reshape(pack_count, SEQ, group_heads, HD)
    )
    attended, log_total = attend(queries, key_rows, values, masks)
    merged = attended.reshape(row_count, width).astype(jnp.bfloat16)
    attn_part = jnp.dot(merged, out_w, preferred_element_type=jnp.float32)
    attn_summed = lax.psum(attn_part.astype(jnp.bfloat16), "tensor").astype(jnp.float32)
    first_sum = stream + attn_summed + vector_rows[4]
    normed = layer_norm(first_sum, vector_rows[0], vector_rows[1])
    normed_low = normed.astype(jnp.bfloat16)
    hidden_pre = jnp.dot(normed_low, up_w, preferred_element_type=jnp.float32) + up_row
    hidden_act = gelu_exact(hidden_pre).astype(jnp.bfloat16)
    ffn_part = jnp.dot(hidden_act, down_w, preferred_element_type=jnp.float32)
    ffn_summed = lax.psum(ffn_part.astype(jnp.bfloat16), "tensor").astype(jnp.float32)
    second_sum = normed + ffn_summed + vector_rows[5]
    result = layer_norm(second_sum, vector_rows[2], vector_rows[3])
    kept = (
        stream_low,
        queries,
        key_rows,
        values,
        log_total,
        merged,
        first_sum,
        normed_low,
        hidden_pre,
        hidden_act,
        second_sum,
    )
    return (result, kept)


def layer_backward(grad_out, kept, qkv_w, out_w, up_w, down_w, vector_rows, masks):
    (
        stream_low,
        queries,
        key_rows,
        values,
        log_total,
        merged,
        first_sum,
        normed_low,
        hidden_pre,
        hidden_act,
        second_sum,
    ) = kept
    row_count = stream_low.shape[0]
    width = out_w.shape[0]
    _, pull_second = jax.vjp(layer_norm, second_sum, vector_rows[2], vector_rows[3])
    grad_second, grad_gain_two, grad_shift_two = pull_second(grad_out)
    grad_down_bias = jnp.sum(grad_second, axis=0)
    low_second = grad_second.astype(jnp.bfloat16)
    grad_down = jnp.einsum("tf,td->fd", hidden_act, low_second, preferred_element_type=jnp.float32)
    grad_act = jnp.einsum("td,fd->tf", low_second, down_w, preferred_element_type=jnp.float32)
    _, pull_gelu = jax.vjp(gelu_exact, hidden_pre)
    grad_pre = pull_gelu(grad_act)[0].astype(jnp.bfloat16)
    grad_up_bias = jnp.sum(grad_pre.astype(jnp.float32), axis=0)
    grad_up = jnp.einsum("td,tf->df", normed_low, grad_pre, preferred_element_type=jnp.float32)
    back_normed = jnp.einsum("tf,df->td", grad_pre, up_w, preferred_element_type=jnp.float32)
    grad_normed = grad_second + lax.psum(back_normed.astype(jnp.bfloat16), "tensor").astype(
        jnp.float32
    )
    _, pull_first = jax.vjp(layer_norm, first_sum, vector_rows[0], vector_rows[1])
    grad_first, grad_gain_one, grad_shift_one = pull_first(grad_normed)
    grad_out_bias = jnp.sum(grad_first, axis=0)
    low_first = grad_first.astype(jnp.bfloat16)
    grad_outw = jnp.einsum("tn,td->nd", merged, low_first, preferred_element_type=jnp.float32)
    grad_merged = jnp.einsum(
        "td,nd->tn", low_first, out_w, preferred_element_type=jnp.float32
    ).astype(jnp.bfloat16)
    grad_queries, grad_keys, grad_values = attend_back(
        queries, key_rows, values, grad_merged.reshape(queries.shape), log_total, masks
    )
    grad_project = jnp.stack(
        (
            grad_queries.reshape(row_count, width),
            grad_keys.reshape(row_count, width),
            grad_values.reshape(row_count, width),
        ),
        axis=1,
    )
    grad_qv_bias = jnp.sum(grad_project[:, 0::2].astype(jnp.float32), axis=0)
    grad_qkv = jnp.einsum(
        "td,tcn->dcn", stream_low, grad_project, preferred_element_type=jnp.float32
    )
    back_stream = jnp.einsum("tcn,dcn->td", grad_project, qkv_w, preferred_element_type=jnp.float32)
    grad_stream = grad_first + lax.psum(back_stream.astype(jnp.bfloat16), "tensor").astype(
        jnp.float32
    )
    vector_grad = jnp.stack(
        (
            grad_gain_one,
            grad_shift_one,
            grad_gain_two,
            grad_shift_two,
            grad_out_bias,
            grad_down_bias,
        )
    )
    return (
        grad_stream,
        (grad_qkv, grad_outw, grad_up, grad_down),
        (vector_grad, grad_qv_bias, grad_up_bias),
    )


def adamw(weight, first, second, gradient, factor, rate, decay):
    clipped = gradient * factor
    new_first = BETA_ONE * first + (1.0 - BETA_ONE) * clipped
    new_second = BETA_TWO * second + (1.0 - BETA_TWO) * clipped * clipped
    first_hat = new_first / (1.0 - BETA_ONE**STEP)
    second_hat = new_second / (1.0 - BETA_TWO**STEP)
    new_weight = weight - rate * (first_hat / (jnp.sqrt(second_hat) + ADAM_EPS) + decay * weight)
    return (new_weight, new_first, new_second)


def body(
    inputs,
    pair_lengths,
    out_grad,
    w_qkv,
    m_qkv,
    v_qkv,
    w_out,
    m_out,
    v_out,
    w_up,
    m_up,
    v_up,
    w_down,
    m_down,
    v_down,
    vectors,
    m_vectors,
    v_vectors,
    qv_bias,
    m_qv_bias,
    v_qv_bias,
    up_bias,
    m_up_bias,
    v_up_bias,
):
    full_qkv, full_out, full_up, full_down = (
        lax.all_gather(w_qkv.astype(jnp.bfloat16), "dp", axis=1, tiled=True),
        lax.all_gather(w_out.astype(jnp.bfloat16), "dp", axis=1, tiled=True),
        lax.all_gather(w_up.astype(jnp.bfloat16), "dp", axis=1, tiled=True),
        lax.all_gather(w_down.astype(jnp.bfloat16), "dp", axis=1, tiled=True),
    )
    masks = jax.vmap(pair_mask)(pair_lengths)
    stream = inputs.astype(jnp.float32)
    kept_all = []
    for layer_index in range(LAYERS):
        stream, kept = layer_forward(
            stream,
            full_qkv[layer_index],
            full_out[layer_index],
            full_up[layer_index],
            full_down[layer_index],
            vectors[layer_index],
            qv_bias[layer_index],
            up_bias[layer_index],
            masks,
        )
        kept_all.append(kept)
    activations = stream.astype(jnp.bfloat16)
    grad_stream = out_grad.astype(jnp.float32)
    matrix_grads = [None] * LAYERS
    small_grads = [None] * LAYERS
    for layer_index in reversed(range(LAYERS)):
        grad_stream, mats, smalls = layer_backward(
            grad_stream,
            kept_all[layer_index],
            full_qkv[layer_index],
            full_out[layer_index],
            full_up[layer_index],
            full_down[layer_index],
            vectors[layer_index],
            masks,
        )
        matrix_grads[layer_index] = mats
        small_grads[layer_index] = smalls
    stacked = tuple(
        (
            jnp.stack([matrix_grads[layer_index][kind] for layer_index in range(LAYERS)])
            for kind in range(4)
        )
    )
    g_qkv, g_out, g_up, g_down = (
        lax.psum_scatter(stacked[0], "dp", scatter_dimension=1, tiled=True),
        lax.psum_scatter(stacked[1], "dp", scatter_dimension=1, tiled=True),
        lax.psum_scatter(stacked[2], "dp", scatter_dimension=1, tiled=True),
        lax.psum_scatter(stacked[3], "dp", scatter_dimension=1, tiled=True),
    )
    small_stacked = tuple(
        (
            jnp.stack([small_grads[layer_index][kind] for layer_index in range(LAYERS)])
            for kind in range(3)
        )
    )
    g_vec, g_qv, g_upb = lax.psum(small_stacked, "dp")
    data_count = lax.axis_size("dp")
    tensor_count = lax.axis_size("tensor")
    local_squares = (
        jnp.sum(g_qkv * g_qkv)
        + jnp.sum(g_out * g_out)
        + jnp.sum(g_up * g_up)
        + jnp.sum(g_down * g_down)
        + (jnp.sum(g_qv * g_qv) + jnp.sum(g_upb * g_upb)) / data_count
        + jnp.sum(g_vec * g_vec) / (data_count * tensor_count)
    )
    squares = lax.psum(local_squares, ("dp", "tensor"))
    grad_norm = jnp.sqrt(squares)
    factor = jnp.minimum(1.0, CLIP_LIMIT / grad_norm)
    new_qkv = adamw(w_qkv, m_qkv, v_qkv, g_qkv, factor, LEARN_RATE, WEIGHT_DECAY)
    new_out = adamw(w_out, m_out, v_out, g_out, factor, LEARN_RATE, WEIGHT_DECAY)
    new_up = adamw(w_up, m_up, v_up, g_up, factor, LEARN_RATE, WEIGHT_DECAY)
    new_down = adamw(w_down, m_down, v_down, g_down, factor, LEARN_RATE, WEIGHT_DECAY)
    new_vec = adamw(vectors, m_vectors, v_vectors, g_vec, factor, VECTOR_RATE, 0.0)
    new_qv = adamw(qv_bias, m_qv_bias, v_qv_bias, g_qv, factor, VECTOR_RATE, 0.0)
    new_upb = adamw(up_bias, m_up_bias, v_up_bias, g_upb, factor, VECTOR_RATE, 0.0)
    return (
        activations,
        grad_stream,
        grad_norm,
        new_qkv[0],
        new_qkv[1],
        new_qkv[2],
        new_out[0],
        new_out[1],
        new_out[2],
        new_up[0],
        new_up[1],
        new_up[2],
        new_down[0],
        new_down[1],
        new_down[2],
        new_vec[0],
        new_vec[1],
        new_vec[2],
        new_qv[0],
        new_qv[1],
        new_qv[2],
        new_upb[0],
        new_upb[1],
        new_upb[2],
    )


MESH = pl.DeviceIdType.MESH
F32, BF16 = jnp.float32, jnp.bfloat16
LINE = 4
DM = 768
QKV, OUT, UP, DOWN = KINDS = ("qkv", "out", "up", "down")
FIRST, SECOND, EARLY, LATE = range(4)
BLOCK = {QKV: (96, 576), OUT: (16, 1152), UP: (96, 768), DOWN: (96, 768)}
CUTS = (
    {QKV: (0, 48, 80), OUT: (1, 384, 1024), UP: (0, 32, 80), DOWN: (0, 32, 64)},
    {QKV: (0, 32, 80), OUT: (1, 384, 896), UP: (0, 32, 80), DOWN: (0, 16, 64)},
    {QKV: (0, 48, 96), OUT: (1, 512, 1152), UP: (0, 32, 80), DOWN: (0, 32, 64)},
)
G, L, F, S, M, R = range(6)
PLAN = {
    "f0s": ((G, 1, 0), (L, 3, 1), (L, 1, 1),),
    "need0": (
        (L, 4, 1),
        (G, 0, 1),
        (L, 2, 1),
        (L, 5, 1),
        (G, 4, 0),
        (G, 0, 2),
        (G, 1, 1),
        (G, 0, 3),
        (G, 1, 2),
        (G, 4, 1),
        (G, 1, 3),
        (G, 2, 0),
        (G, 0, 4),
        (G, 3, 0),
        (L, 4, 2),
        (G, 2, 1),
        (G, 3, 1),
        (G, 2, 2),
        (L, 1, 2),
        (G, 5, 0),
        (G, 1, 4),
        (G, 2, 3),
        (F, 0),
        (G, 3, 2),
        (G, 5, 1),
        (G, 4, 2),
        (L, 1, 3),
        (L, 3, 2),
        (L, 4, 3),
        (G, 3, 3),
    ),
    "f0a1": ((L, 2, 2), (L, 3, 3),),
    "f0p": ((L, 1, 4), (G, 4, 3),),
    "f0o": ((G, 2, 4), (L, 2, 3), (G, 3, 4),),
    "need1": ((F, 1),),
    "f0x": ((L, 2, 4), (G, 5, 2),),
    "f0v": ((F, 2),),
    "need3": ((L, 3, 4), (G, 5, 3), (L, 5, 2), (G, 4, 4), (F, 3),),
    "f1o": ((L, 4, 4), (F, 4), (L, 5, 4),),
    "need5": ((F, 5),),
    "b1m": ((S, 3, 1, 1),),
    "b1t": ((S, 2, 1, 1), (S, 3, 1, 2), (S, 1, 1, 1),),
    "b0s": ((S, 2, 1, 2),),
    "b0h": ((S, 3, 1, 3), (S, 1, 1, 2), (S, 2, 1, 3), (S, 3, 1, 4), (S, 0, 1, 1), (S, 1, 1, 3),),
    "b0w": ((M, 1, 1), (S, 2, 1, 4), (S, 3, 1, 5),),
    "b0n": ((S, 1, 1, 4), (S, 2, 1, 5),),
    "b0m": ((S, 0, 1, 2), (R, 0, 0), (S, 1, 1, 5), (S, 3, 0, 1), (S, 0, 1, 3),),
    "b0b": ((S, 2, 0, 1), (M, 1, 2), (S, 0, 1, 4),),
    "b0t": ((S, 1, 0, 1),),
    "b0q": ((S, 0, 1, 5),),
    "end": (
        (S, 1, 0, 2),
        (R, 0, 1),
        (S, 3, 0, 2),
        (S, 2, 0, 2),
        (S, 2, 0, 3),
        (M, 0, 1),
        (S, 0, 0, 1),
        (S, 1, 0, 3),
        (S, 3, 0, 3),
        (S, 2, 0, 4),
        (M, 1, 3),
        (M, 0, 2),
        (R, 1, 0),
        (S, 2, 0, 5),
        (S, 0, 0, 2),
        (S, 3, 0, 4),
        (S, 0, 0, 3),
        (M, 0, 3),
        (S, 0, 0, 4),
        (R, 1, 1),
        (S, 3, 0, 5),
        (S, 1, 0, 4),
        (S, 0, 0, 5),
        (S, 1, 0, 5),
    ),
    "f1p": ((L, 5, 3), (G, 5, 4),),
}
SEMS = 240
OWN, HALF = 384, 256


def dot(a, b):
    return jnp.dot(a, b, preferred_element_type=F32)


def dot_nt(a, b):
    return lax.dot_general(a, b, (((1,), (1,)), ((), ())), preferred_element_type=F32)


def dot_tn(a, b):
    return lax.dot_general(a, b, (((0,), (0,)), ((), ())), preferred_element_type=F32)


def flat(v):
    return v.reshape((-1, v.shape[-1]))


def gelu_and_slope(u):
    a = jnp.abs(u) * (1.0 / math.sqrt(2.0))
    t = 1.0 / (1.0 + 0.5 * a)
    poly = 0.17087277
    for coeff in (
        -0.82215223,
        1.48851587,
        -1.13520398,
        0.27886807,
        -0.18628806,
        0.09678418,
        0.37409196,
        1.00002368,
        -1.26551223,
    ):
        poly = poly * t + coeff
    bell = jnp.exp(-0.5 * u * u)
    tail = 0.5 * t * bell * jnp.exp(poly)
    below = jnp.where(u >= 0, 1.0 - tail, tail)
    return u * below, below + u * bell * (1.0 / math.sqrt(2.0 * math.pi))


def norm_stats(rows):
    center = rows - jnp.mean(rows, axis=-1, keepdims=True)
    spread = jnp.mean(center * center, axis=-1, keepdims=True)
    scale = lax.rsqrt(spread + NORM_EPS)
    return center * scale, scale


class Moves:
    def __init__(self, send, recv):
        self.send, self.recv, self.count, self.open = send, recv, 0, []
        self.again, self.log = [], []

    def make(self, src, dst, device, lands, can_send=None, can_recv=None):
        if self.again:
            index = self.again.pop(0)
        else:
            index = self.count
            self.count += 1
        assert index < SEMS
        self.log.append(index)
        move = types.SimpleNamespace(index=index)

        def copy(src, dst):
            return pltpu.make_async_remote_copy(
                src_ref=src,
                dst_ref=dst,
                send_sem=self.send.at[index],
                recv_sem=self.recv.at[index],
                device_id=device,
                device_id_type=MESH,
            )

        def guarded(cond, act):
            if cond is None:
                act()
            else:
                pl.when(cond)(act)

        def start():
            guarded(can_send, lambda: copy(src(), dst()).start())
            self.open.append(move)

        move.start = start
        move.wait_recv = lambda: guarded(can_recv, lambda: copy(lands(), lands()).wait_recv())
        move.wait_send = lambda: guarded(can_send, lambda: copy(src(), src()).wait_send())
        return move

    def sent(self, *moves):
        for move in moves:
            move.wait_send()
            self.open.remove(move)

    def drain_but(self, *moves):
        self.sent(*[move for move in self.open if move not in moves])

    def drain(self):
        for move in self.open:
            move.wait_send()
        self.open = []


def fused(names, *refs):
    k = types.SimpleNamespace(**dict(zip(names, refs)))
    dp, tensor = lax.axis_index("dp"), lax.axis_index("tensor")
    z, x, y, c = dp // 2, dp % 2, tensor // 2, tensor % 2
    core_dev = (dp, y * 2 + 1 - c)
    y_dev = (dp, (1 - y) * 2 + c)
    x_dev = (z * 2 + 1 - x, tensor)
    up_dev = ((z + 1) * 2 + x, tensor)
    down_dev = ((z - 1) * 2 + x, tensor)
    not_last, not_first = z <= LINE - 2, z >= 1

    plane_devs = [(z * 2 + (x ^ i // 4), (y ^ i // 2 % 2) * 2 + (c ^ i % 2)) for i in range(1, 8)]
    line_devs = [((z ^ i) * 2 + x, tensor) for i in range(1, LINE)]
    barrier = pltpu.get_barrier_semaphore()
    for device in plane_devs + line_devs:
        pl.semaphore_signal(barrier, inc=1, device_id=device, device_id_type=MESH)

    moves = Moves(k.send, k.recv)
    weights = {QKV: k.w_qkv, OUT: k.w_out, UP: k.w_up, DOWN: k.w_down}

    def one(v):
        return (v, 1)

    both, line = (0, 2), (0, LINE)

    def part(kind, number, cuts=0):
        axis, first, second = CUTS[cuts][kind]
        full = BLOCK[kind]
        low, high = ((0, first), (first, second), (0, second), (second, full[axis]))[number]
        cut = [(0, full[0]), (0, full[1])]
        cut[axis] = (low, high - low)
        return tuple(cut)

    def region(kind, layer, ys, zs, xs, number, cuts=0):
        rows, cols = part(kind, number, 2 if cuts == 0 and layer == 0 and kind in (QKV, OUT) else cuts)
        return weights[kind].at[(layer,) + tuple(pl.ds(*cut) for cut in (ys, zs, xs, rows, cols))]

    def swap(kind, layer, axis, number, ys, zs, xs):
        other_ys, other_xs = (one(1 - y), xs) if axis == "y" else (ys, one(1 - x))
        here = lambda: region(kind, layer, ys, zs, xs, number)
        return [
            moves.make(
                here,
                here,
                y_dev if axis == "y" else x_dev,
                lambda: region(kind, layer, other_ys, zs, other_xs, number),
            )
        ]

    def hop(kind, layer, step, number, ys, xs):
        at = lambda v: (lambda: region(kind, layer, ys, one(v), xs, number))
        return [
            moves.make(
                at(z - step + 1),
                at(z - step + 1),
                up_dev,
                at(z - step),
                (z >= step - 1) & not_last,
                z >= step,
            ),
            moves.make(
                at(z + step - 1),
                at(z + step - 1),
                down_dev,
                at(z + step),
                (z <= LINE - step) & not_first,
                z <= LINE - 1 - step,
            ),
        ]

    def gather_stages(kind, layer):
        a = (kind, layer)
        crosses = [
            swap(*a, "x", FIRST, one(y), line, one(x)) + swap(*a, "y", SECOND, one(y), line, one(x)),
            swap(*a, "y", FIRST, one(y), line, both) + swap(*a, "x", SECOND, both, line, one(x)),
        ]
        hops = [hop(*a, step, EARLY, one(y), one(x)) for step in (1, 2, 3)]
        if layer == 0 and kind in (QKV, OUT):
            return hops + crosses, [[]] * 5
        late = [swap(*a, "x", LATE, one(y), one(z), one(x)), swap(*a, "y", LATE, one(y), one(z), both)]
        return hops + crosses, late + [hop(*a, step, LATE, both, both) for step in (1, 2, 3)]

    gather_chunks = [
        ((QKV, 0), (OUT, 0)),
        ((UP, 0),),
        ((DOWN, 0),),
        ((QKV, 1), (OUT, 1)),
        ((UP, 1),),
        ((DOWN, 1),),
    ]
    earlies, lates, indices = [], [], {}
    for chunk in gather_chunks:
        early, late = [], []
        for kind, layer in chunk:
            start = moves.count
            for into, found in zip((early, late), gather_stages(kind, layer)):
                for stage, found_moves in enumerate(found):
                    if stage == len(into):
                        into.append([])
                    into[stage].extend(found_moves)
            indices[kind, layer] = list(range(start, moves.count))
        earlies.append(early)
        lates.append(late)

    def gather(stages, stage):
        if stage:
            for move in stages[stage - 1]:
                move.wait_recv()
        if stage < 5:
            for move in stages[stage]:
                move.start()

    def add_into(kind, layer, ys, zs, xs, number, buf, from_xs=0, from_ys=0):
        rows, cols = part(kind, number, 1)
        count = (ys[1], zs[1], xs[1])

        @pl.loop(0, count[0] * count[1] * count[2])
        def _(i):
            yi, zi, xi = i // (count[1] * count[2]), (i // count[2]) % count[1], i % count[2]
            at = (layer, ys[0] + yi, zs[0] + zi, xs[0] + xi, pl.ds(*rows), pl.ds(*cols))
            total = weights[kind][at].astype(F32) + buf[from_ys + yi, zi, from_xs + xi].astype(F32)
            weights[kind][at] = total.astype(BF16)

    def scatter_swap(kind, layer, axis, number, ys, zs, xs, buf):
        away_ys, away_xs = (one(1 - y), xs) if axis == "y" else (ys, one(1 - x))
        landing = lambda: buf
        return moves.make(
            lambda: region(kind, layer, away_ys, zs, away_xs, number, 1),
            landing,
            y_dev if axis == "y" else x_dev,
            landing,
        )

    def scatter_hop(kind, layer, step, number, ys, xs, buf):
        found = []
        for way, device, goes, sends, comes, receives in (
            (0, up_dev, z + LINE - step, (z <= step - 1) & not_last, z + 3 - step, not_first & (z <= step)),
            (1, down_dev, z - LINE + step, (z >= LINE - step) & not_first, z - 3 + step, not_last & (z >= 3 - step)),
        ):
            landing = lambda way=way: buf.at[way, step - 1]
            move = moves.make(
                lambda goes=goes: region(kind, layer, ys, one(goes), xs, number, 1),
                landing,
                device,
                landing,
                sends,
                receives,
            )

            def add(way=way, comes=comes, receives=receives):
                pl.when(receives)(
                    lambda: add_into(kind, layer, ys, one(comes), xs, number, buf.at[way, step - 1])
                )

            found.append((move, add))
        return found

    def scatter_stages(kind, layer):
        a = (kind, layer)
        r = types.SimpleNamespace(
            **{name[: -len(kind)]: ref for name, ref in vars(k).items() if name[0] == "r" and name.endswith(kind)}
        )
        first_y = scatter_swap(*a, "y", FIRST, both, line, both, r.ry1)
        second_x = scatter_swap(*a, "x", SECOND, both, line, both, r.rx2)
        first_x = scatter_swap(*a, "x", FIRST, one(y), line, both, r.rx1)
        second_y = scatter_swap(*a, "y", SECOND, both, line, one(x), r.ry2)
        late_y = scatter_swap(*a, "y", LATE, both, one(z), both, r.ry3)
        late_x = scatter_swap(*a, "x", LATE, one(y), one(z), both, r.rx3)
        early = [scatter_hop(*a, step, EARLY, one(y), one(x), r.rz) for step in (1, 2, 3)]
        late = [scatter_hop(*a, step, LATE, both, both, r.rz3) for step in (1, 2, 3)]

        def start(found):
            return [move.start for move, _ in found]

        def onward(found, then):
            steps = []
            for index, (move, add) in enumerate(found):
                steps += [move.wait_recv, add]
                if then:
                    steps.append(then[index][0].start)
            return steps

        stages = [
            [first_y.start, second_x.start] + start(late[0]),
            [
                first_y.wait_recv,
                lambda: add_into(*a, one(y), line, one(1 - x), FIRST, r.ry1, from_xs=1 - x),
                first_x.start,
                second_x.wait_recv,
                lambda: add_into(*a, one(1 - y), line, one(x), SECOND, r.rx2, from_ys=1 - y),
                second_y.start,
                lambda: add_into(*a, one(y), line, one(x), FIRST, r.ry1, from_xs=x),
                lambda: add_into(*a, one(y), line, one(x), SECOND, r.rx2, from_ys=y),
            ],
            [
                first_x.wait_recv,
                lambda: add_into(*a, one(y), line, one(x), FIRST, r.rx1),
                second_y.wait_recv,
                lambda: add_into(*a, one(y), line, one(x), SECOND, r.ry2),
            ]
            + start(early[0]),
        ]
        for index in range(len(early)):
            stages.append(onward(early[index], early[index + 1] if index + 1 < len(early) else None))
        for index in range(len(late)):
            stages[index + 1] += onward(late[index], late[index + 1] if index + 1 < len(late) else None)
        after = len(late)
        stages[after] += [late_y.start]
        stages[after + 1] += [
            late_y.wait_recv,
            lambda: add_into(*a, one(y), one(z), both, LATE, r.ry3),
            late_x.start,
        ]
        stages[after + 2] += [late_x.wait_recv, lambda: add_into(*a, one(y), one(z), one(x), LATE, r.rx3)]
        stages[-1].append(lambda: finish(kind, layer))
        return stages

    def finish(kind, layer):
        total = weights[kind][layer, y, z, x].astype(F32)
        size, width = BLOCK[kind]
        k.sq_rows[:, 0:width] += jnp.sum((total * total).reshape((size // 8, 8, width)), axis=0)
        if kind == QKV:
            for j in range(3):
                k.g_qkv[layer, j] = total[:, j * 192 : (j + 1) * 192]
        elif kind == OUT:
            k.g_out[layer, 0:16, :] = total[:, 0:768]
            k.g_out[layer, 16:24, 0:384] = total[0:8, 768:1152]
            k.g_out[layer, 16:24, 384:768] = total[8:16, 768:1152]
        else:
            (k.g_up if kind == UP else k.g_down)[layer] = total

    scatters, scattered, used = {}, {}, {}
    lenders = {DOWN: UP, UP: QKV, OUT: OUT, QKV: DOWN}

    def scatter(kind, layer, stage):
        chunk = (kind, layer)
        assert scattered.get(chunk, -1) == stage - 1
        scattered[chunk] = stage
        if stage == 0:
            if layer:
                moves.again = list(indices[lenders[kind], 0])
            else:
                assert scattered[kind, 1] == 5
                moves.sent(*[move for move in moves.open if move.index in used[kind]])
                moves.again = list(used[kind])
            before = len(moves.log)
            scatters[chunk] = scatter_stages(kind, layer)
            used[kind] = moves.log[before:]
            moves.again = []
        for act in scatters[chunk][stage]:
            act()

    def small_step(layer, step):
        if step:
            total = k.small[layer, step - 1]
            for index, move in small_moves[layer]:
                move.wait_recv()
                total = total + k.small_in[layer, index]
            if step == 1:
                row = lax.broadcasted_iota(jnp.int32, (16, DM), 0)
                total = jnp.where(row < 6, total, k.small[layer, 0])
            k.small[layer, step] = total
        if step < 3:
            devices = ((core_dev,), (x_dev, y_dev, (z * 2 + 1 - x, (1 - y) * 2 + c)), line_devs)[step]
            small_moves[layer] = []
            for i, device in enumerate(devices):
                index = (0, 1, 4)[step] + i
                landing = lambda index=index: k.small_in.at[layer, index]
                move = moves.make(lambda: k.small.at[layer, step], landing, device, landing)
                move.start()
                small_moves[layer].append((index, move))

    small_moves = {}

    spreads = {}

    def at(name):
        for what, *args in PLAN.get(name, ()):
            if what == G:
                gather(earlies[args[0]], args[1])
            elif what == L:
                gather(lates[args[0]], args[1])
            elif what == F:
                gather(earlies[args[0]], 5)
                gather(lates[args[0]], 5)
            elif what == S:
                scatter(KINDS[args[0]], args[1], args[2])
            elif what == M:
                small_step(*args)
            else:
                spreads[args[0]][args[1]]()

    pack_row = pl.multiple_of(y * (2 * SEQ), SEQ)
    own_a = pl.multiple_of(c * HALF, HALF)
    own_p = pl.multiple_of(SEQ + HALF * y + 128 * c, 128)
    loads = [
        pltpu.make_async_copy(k.wq_in, k.stage_q, k.local.at[0]),
        pltpu.make_async_copy(k.wu_in, k.sum1.at[0, pl.ds(0, 192)], k.local.at[1]),
        pltpu.make_async_copy(k.wd_in, k.sum1.at[0, pl.ds(192, 192)], k.local.at[2]),
        pltpu.make_async_copy(k.wo_in, k.sum1.at[1, pl.ds(0, 48)], k.local.at[3]),
    ]
    x_loads = [
        pltpu.make_async_copy(k.x_in.at[pl.ds(pack_row, SEQ)], k.x_buf.at[pl.ds(0, SEQ)], k.local.at[4]),
        pltpu.make_async_copy(k.x_in.at[pl.ds(SEQ, SEQ)], k.x_buf.at[pl.ds(SEQ, SEQ)], k.local.at[5]),
    ]
    in_a = pl.multiple_of(pack_row + own_a, HALF)
    e_loads = [
        pltpu.make_async_copy(k.e_in.at[pl.ds(in_a, HALF)], k.e_low.at[pl.ds(0, HALF)], k.local.at[6]),
        pltpu.make_async_copy(k.e_in.at[pl.ds(own_p, 128)], k.e_low.at[pl.ds(HALF, 128)], k.local.at[7]),
    ]
    for load in loads + x_loads + e_loads:
        load.start()

    k.bias[y, :, :] = jnp.zeros((8, DM), F32)
    for layer in range(LAYERS):
        k.bias[y, pl.ds(layer, 1), :] = k.upb_in[pl.ds(layer, 1), :]
        k.bias[y, pl.ds(2 + layer, 1), 0:192] = k.qvb_in[layer, 0:1, :]
        k.bias[y, pl.ds(2 + layer, 1), 384:576] = k.qvb_in[layer, 1:2, :]
    loads[0].wait()
    for layer in range(LAYERS):
        for j in range(3):
            k.w_qkv[layer, y, z, x, :, j * 192 : (j + 1) * 192] = k.stage_q[layer, j].astype(BF16)
    loads[3].wait()
    for layer in range(LAYERS):
        rows = k.sum1[1, pl.ds(layer * 24, 24), :]
        k.w_out[layer, y, z, x, :, 0:768] = rows[0:16].astype(BF16)
        k.w_out[layer, y, z, x, :, 768:1152] = jnp.concatenate([rows[16:24, 0:384], rows[16:24, 384:768]], axis=0).astype(BF16)
    loads[1].wait()
    loads[2].wait()
    for layer in range(LAYERS):
        k.w_up[layer, y, z, x] = k.sum1[0, pl.ds(layer * 96, 96), :].astype(BF16)
        k.w_down[layer, y, z, x] = k.sum1[0, pl.ds(192 + layer * 96, 96), :].astype(BF16)

    pl.semaphore_wait(barrier, len(plane_devs + line_devs))
    gather(lates[0], 0)
    gather(earlies[0], 0)
    for late in lates[1:]:
        gather(late, 0)
    bias_move = moves.make(
        lambda: k.bias.at[pl.ds(y, 1)], lambda: k.bias.at[pl.ds(y, 1)], y_dev, lambda: k.bias.at[pl.ds(1 - y, 1)]
    )
    bias_move.start()

    for slot in range(2):
        pack = 1 if slot else 2 * y
        columns = lax.broadcasted_iota(jnp.int32, (8, SEQ), 1)
        rows = lax.broadcasted_iota(jnp.int32, (SEQ, 128), 0)
        pair_col, pair_row = jnp.zeros((8, SEQ), F32), jnp.zeros((SEQ, 128), F32)
        end = jnp.int32(0)
        for j in range(4):
            end = end + k.lens[pack, j]
            pair_col += jnp.where(columns >= end, 1.0, 0.0)
            pair_row += jnp.where(rows >= end, 1.0, 0.0)
        k.pair_col[slot] = pair_col
        k.pair_row[slot] = pair_row
    for layer in range(LAYERS):
        k.small[layer, 0] = jnp.zeros((16, DM), F32)
    k.sq_rows[...] = jnp.zeros(k.sq_rows.shape, F32)

    for load in x_loads:
        load.wait()
    k.res[0:HALF, :] = k.x_buf[pl.ds(own_a, HALF), :].astype(F32)
    k.res[HALF:OWN, :] = k.x_buf[pl.ds(own_p, 128), :].astype(F32)
    bias_move.wait_recv()
    at("f0s")

    def gather_pair(buf, layer=None):
        at = lambda slot: (lambda: buf.at[pl.ds(slot, 1)])
        move = moves.make(at(c), at(c), core_dev, at(1 - c))
        move.start()
        return move

    def gather_chip(buf):
        found = []
        for mine, other, size in ((own_a, (1 - c) * HALF, HALF), (SEQ + 128 * c, SEQ + 128 * (1 - c), 128)):
            here = lambda mine=mine, size=size: buf.at[pl.ds(pl.multiple_of(mine, 128), size)]
            there = lambda other=other, size=size: buf.at[pl.ds(pl.multiple_of(other, 128), size)]
            found.append(moves.make(here, here, core_dev, there))
            found[-1].start()
        return found

    def gather_rows(buf):
        rows = lambda start, size: (lambda: buf.at[pl.ds(pl.multiple_of(start, 128), size)])
        other_p = SEQ + HALF * (1 - y) + 128 * c
        mine = rows(own_p, 128)
        relayed = rows(other_p, 128)
        across = moves.make(mine, mine, y_dev, relayed)
        across.start()
        first = moves.make(rows(own_a, HALF), rows(own_a, HALF), core_dev, rows((1 - c) * HALF, HALF))
        first.start()
        second = moves.make(mine, mine, core_dev, rows(SEQ + HALF * y + 128 * (1 - c), 128))
        second.start()

        def relay():
            across.wait_recv()
            third = moves.make(relayed, relayed, core_dev, rows(SEQ + HALF * (1 - y) + 128 * (1 - c), 128))
            third.start()
            return third

        return across, first, second, relay

    def sum_pair(fill):
        def to_send(rows, cols, value):
            k.ex_s[rows, cols] = value.astype(BF16)

        def to_keep(rows, cols, value):
            k.cur[rows, cols] = value

        fill(1 - c, to_send)
        move = moves.make(
            lambda: k.ex_s.at[pl.ds(0, OWN)], lambda: k.ex_r.at[pl.ds(0, OWN)], core_dev, lambda: k.ex_r.at[pl.ds(0, OWN)]
        )
        move.start()
        fill(c, to_keep)

        def end():
            move.wait_recv()
            k.cur[...] += k.ex_r[0:OWN, :].astype(F32)
            moves.sent(move)

        return end

    def fill_rows(part_a, part_p):
        def fill(slot, store):
            store(slice(0, HALF), slice(0, DM), part_a(slot))
            store(slice(HALF, OWN), slice(0, DM), part_p(slot))

        return fill

    def send_away(part):
        k.ex_s[OWN:SEQ, :] = part(1 - c).astype(BF16)
        piece = lambda ref: (lambda: ref.at[pl.ds(OWN, 128)])
        beside = moves.make(piece(k.ex_s), piece(k.ex_r), core_dev, piece(k.ex_r))
        beside.start()
        k.ey_f[...] = part(c)
        across = moves.make(lambda: k.ey_s, lambda: k.ey_r, y_dev, lambda: k.ey_r)

        def go():
            beside.wait_recv()
            k.ey_s[...] = (k.ey_f[...] + k.ex_r[OWN:SEQ, :].astype(F32)).astype(BF16)
            across.start()

        def end():
            across.wait_recv()
            k.cur[HALF:OWN, :] += k.ey_r[...].astype(F32)
            moves.sent(beside, across)

        return go, end

    def spread(low, out, sems):
        piece = lambda ref, start, size: (lambda: ref.at[pl.ds(pl.multiple_of(start, 128), size)])
        locals_, started, relays = [], [], []
        other_a, other_p = (1 - y) * (2 * SEQ) + c * HALF, SEQ + HALF * (1 - y) + 128 * c
        for index, (start, size, at, far) in enumerate(((0, HALF, in_a, other_a), (HALF, 128, own_p, other_p))):
            copy = pltpu.make_async_copy(piece(low, start, size)(), piece(out, at, size)(), k.local.at[sems + index])
            copy.start()
            locals_.append(copy)
            across = moves.make(piece(low, start, size), piece(out, at, size), y_dev, piece(out, far, size))
            across.start()
            step = HALF if size == HALF else 128
            mate = at + (1 - 2 * c) * step
            beside = moves.make(piece(low, start, size), piece(out, at, size), core_dev, piece(out, mate, size))
            beside.start()
            started.append(beside)
            relays.append((across, far, far + (1 - 2 * c) * step, size))

        def relay():
            for across, far, mate, size in relays:
                across.wait_recv()
                move = moves.make(piece(out, far, size), piece(out, far, size), core_dev, piece(out, mate, size))
                move.start()
                started.append(move)

        def end():
            for copy in locals_:
                copy.wait()
            for move in started:
                move.wait_recv()

        return relay, end

    def save(slot, src, dst):
        copy = pltpu.make_async_copy(src, dst, k.local.at[slot])
        copy.start()
        return copy

    def norm_grad(layer, e, xhat, scale, gain_row, bias_row, rows):
        h = e * k.vec[gain_row, layer : layer + 1, :]
        mean_h = jnp.mean(h, axis=-1, keepdims=True)
        mean_hx = jnp.mean(h * xhat, axis=-1, keepdims=True)
        grad = scale * (h - mean_h - xhat * mean_hx)
        k.res[rows, :] = grad
        acc = k.small.at[layer, 0]
        acc[gain_row : gain_row + 1, :] += jnp.sum(e * xhat, axis=0, keepdims=True)
        acc[gain_row + 1 : gain_row + 2, :] += jnp.sum(e, axis=0, keepdims=True)
        acc[bias_row : bias_row + 1, :] += jnp.sum(grad, axis=0, keepdims=True)

    row_tiles = OWN // 128
    saves = []
    for layer in range(LAYERS):
        if layer == 1:
            k.x_buf[pl.ds(own_a, HALF), :] = k.res[0:HALF, :].astype(BF16)
            k.x_buf[pl.ds(own_p, 128), :] = k.res[HALF:OWN, :].astype(BF16)
            _, first, second, relay = gather_rows(k.x_buf)
            at("f1s")
        place = "f" + str(layer)
        at("need" + str(3 * layer))
        if layer == 1:
            for move in (first, second):
                move.wait_recv()

        for group in range(2):
            for zi in range(LINE):
                for xi in range(2):
                    block = k.w_out[layer, group, zi, xi].astype(F32)
                    low = (zi * 2 + xi) * 24
                    k.unpack[low : low + 16, :] = block[:, 0:768]
                    k.unpack[low + 16 : low + 24, 0:384] = block[0:8, 768:1152]
                    k.unpack[low + 16 : low + 24, 384:768] = block[8:16, 768:1152]
            k.w_o[layer, group] = k.unpack[...].astype(BF16)

        shrink = jnp.where(lax.broadcasted_iota(jnp.int32, (1, 576), 1) < 192, HD ** (-0.5), 1.0)

        def project(group, start):
            rows = pl.ds(pl.multiple_of(start, HALF), HALF)
            made = dot(k.x_buf[rows, :], flat(k.w_qkv[layer, group]))
            made = (made + k.bias[group, 2 + layer : 3 + layer, 0:576]) * shrink
            k.qkv[layer, group, rows, :] = made.astype(BF16)

        def attend(group, tile, key_start, pair_start):
            slot = key_start // SEQ
            rows = pl.ds(pl.multiple_of(tile * HALF, HALF), HALF)
            from_rows = pl.ds(pl.multiple_of(key_start + pair_start, HALF), HALF)
            keys = pl.ds(key_start, SEQ)
            allowed = k.pair_row[slot, pl.ds(pl.multiple_of(pair_start, HALF), HALF), 0:1] == k.pair_col[slot, 0:1, :]
            for head in range(3):
                low, high = head * HD, (head + 1) * HD
                queries = k.qkv[layer, group, from_rows, low:high]
                key_rows = k.qkv[layer, group, keys, 192 + low : 192 + high]
                values = k.qkv[layer, group, keys, 384 + low : 384 + high]
                scores = jnp.where(allowed, dot_nt(queries, key_rows), -1e30)
                raised = jnp.exp(scores - jnp.max(scores, axis=-1, keepdims=True))
                probs = (raised * (1.0 / jnp.sum(raised, axis=-1, keepdims=True))).astype(BF16)
                k.probs[group, head, rows, :] = probs
                k.merged[layer, group, rows, low:high] = dot(probs, values).astype(BF16)

        if layer == 0:
            pl.loop(0, 8)(lambda i: project(i // 4, (i % 4) * HALF))
        else:
            pl.loop(0, 6)(lambda i: project(i // 3, jnp.where(i % 3 == 2, SEQ + HALF * y, (i % 3) * HALF)))
            saves[0].wait()
        at(place + "q")

        @pl.loop(0, 4)
        def _(i):
            attend(i // 2, i % 2, 0, (i % 2) * HALF)
            for turn in range(4):
                pl.when(i == turn)(lambda: at(place + "a" + str(turn)))

        if layer == 1:
            relay().wait_recv()
            pl.loop(0, 2)(lambda group: project(group, SEQ + HALF * (1 - y)))
        pl.loop(0, 2)(lambda group: attend(group, 2, SEQ, HALF * y))
        at(place + "p")
        if layer == 0:
            saves.append(save(8, k.probs, k.probs_hbm))

        def out_rows(start, size):
            rows = pl.ds(pl.multiple_of(start, 128), size)
            return dot(k.merged[layer, 0, rows, :], k.w_o[layer, 0]) + dot(k.merged[layer, 1, rows, :], k.w_o[layer, 1])

        end_out = sum_pair(
            fill_rows(lambda slot: out_rows(slot * HALF, HALF), lambda slot: out_rows(SEQ + 128 * slot, 128))
        )

        def first_norm(i):
            rows = pl.ds(pl.multiple_of(i * 128, 128), 128)
            total = k.res[rows, :] + k.cur[rows, :] + k.vec[4, layer : layer + 1, :]
            k.sum1[layer, rows, :] = total
            normed = norm_stats(total)[0] * k.vec[0, layer : layer + 1, :] + k.vec[1, layer : layer + 1, :]
            k.res[rows, :] = normed
            k.nlow[layer, c, rows, :] = normed.astype(BF16)

        at(place + "o")
        end_out()
        pl.loop(0, row_tiles)(first_norm)

        mate_rows = gather_pair(k.nlow.at[layer])
        at(place + "n")
        at("need" + str(3 * layer + 1))
        if layer == 1:
            saves[1].wait()
            saves[2].wait()
        for order in range(2):
            slot = c if order == 0 else 1 - c
            if order:
                mate_rows.wait_recv()

            @pl.loop(0, 6)
            def _(i):
                group, cols = i // 3, pl.ds(pl.multiple_of((i % 3) * 256, 256), 256)
                made = dot(k.nlow[layer, slot], flat(k.w_up[layer, group, :, :, :, cols]))
                made = made + k.bias[group, layer : layer + 1, cols]
                act, slope = gelu_and_slope(made)
                k.act[group, slot, :, cols] = act.astype(BF16)
                k.slope[group, slot, :, cols] = slope.astype(BF16)
                pl.when(i == 2)(lambda: at(place + "xw"[order]))

            at(place + "uv"[order])

        if layer == 0:
            saves.append(save(9, k.act, k.act_hbm))
            saves.append(save(10, k.slope, k.slope_hbm))
        at("need" + str(3 * layer + 2))

        def down_rows(slot, store):
            @pl.loop(0, 3)
            def _(i):
                cols = pl.ds(pl.multiple_of(i * 256, 256), 256)
                made = dot(k.act[0, slot], flat(k.w_down[layer, 0, :, :, :, cols]))
                store(slice(0, OWN), cols, made + dot(k.act[1, slot], flat(k.w_down[layer, 1, :, :, :, cols])))

        end_down = sum_pair(down_rows)
        at(place + "d")
        if layer == 1:
            for load in e_loads:
                load.wait()
        end_down()

        @pl.loop(0, row_tiles)
        def _(i):
            rows = pl.ds(pl.multiple_of(i * 128, 128), 128)
            total = k.res[rows, :] + k.cur[rows, :] + k.vec[5, layer : layer + 1, :]
            xhat, scale = norm_stats(total)
            result = xhat * k.vec[2, layer : layer + 1, :] + k.vec[3, layer : layer + 1, :]
            if layer == 0:
                k.sum2[rows, :] = total
                k.res[rows, :] = result
            else:
                k.a_low[rows, :] = result.astype(BF16)
                norm_grad(layer, k.e_low[rows, :].astype(F32), xhat, scale, 2, 5, rows)
                k.lsec[c, rows, :] = k.res[rows, :].astype(BF16)

    mate_rows = gather_pair(k.lsec)
    moves.drain_but(mate_rows)
    spreads[0] = spread(k.a_low, k.activations, 11)

    for layer in (1, 0):
        place = "b" + str(layer)
        if layer == 0:

            @pl.loop(0, row_tiles)
            def _(i):
                rows = pl.ds(pl.multiple_of(i * 128, 128), 128)
                xhat, scale = norm_stats(k.sum2[rows, :])
                norm_grad(layer, k.res[rows, :] + k.cur[rows, :], xhat, scale, 2, 5, rows)
                k.lsec[c, rows, :] = k.res[rows, :].astype(BF16)

            mate_rows = gather_pair(k.lsec)
            restore_act.wait()
            restore_slope.wait()
        at(place + "s")
        for order in range(2):
            slot = c if order == 0 else 1 - c
            if order:
                mate_rows.wait_recv()
                moves.sent(mate_rows)

            @pl.loop(0, 4)
            def _(i):
                group, tile = i // 2, i % 2
                cols = pl.ds(pl.multiple_of(tile * OWN, OWN), OWN)
                back = dot_nt(k.lsec[slot], flat(k.w_down[layer, group, pl.ds(tile * 2, 2)]))
                grad = (back * k.slope[group, slot, :, cols].astype(F32)).astype(BF16)
                k.slope[group, slot, :, cols] = grad
                k.small[layer, 0, pl.ds(6 + group, 1), cols] += jnp.sum(grad.astype(F32), axis=0, keepdims=True)

            at(place + "gh"[order])

        @pl.loop(0, 4)
        def _(i):
            group, tile = i // 2, i % 2
            cols = pl.ds(pl.multiple_of(tile * OWN, OWN), OWN)
            made = dot_tn(flat(k.act[group, :, :, cols]), flat(k.lsec[...]))
            k.w_down[layer, group, pl.ds(tile * 2, 2)] = made.astype(BF16).reshape((2, 2, 96, 768))

        at(place + "w")
        scatter(DOWN, layer, 0)
        if layer == 1:
            restore_act = save(9, k.act_hbm, k.act)

        def normed_rows(slot, store):
            @pl.loop(0, 2)
            def _(tile):
                cols = pl.ds(pl.multiple_of(tile * OWN, OWN), OWN)
                made = dot_nt(k.slope[0, slot], flat(k.w_up[layer, 0, pl.ds(tile * 2, 2)]))
                store(slice(0, OWN), cols, made + dot_nt(k.slope[1, slot], flat(k.w_up[layer, 1, pl.ds(tile * 2, 2)])))

        end_normed = sum_pair(normed_rows)
        at(place + "n")
        end_normed()

        @pl.loop(0, row_tiles)
        def _(i):
            rows = pl.ds(pl.multiple_of(i * 128, 128), 128)
            xhat, scale = norm_stats(k.sum1[layer, rows, :])
            norm_grad(layer, k.res[rows, :] + k.cur[rows, :], xhat, scale, 0, 4, rows)
            start = jnp.where(i == 2, SEQ + 128 * c, own_a + i * 128)
            k.lfirst[pl.ds(pl.multiple_of(start, 128), 128), :] = k.res[rows, :].astype(BF16)

        mate_firsts = gather_chip(k.lfirst)
        at(place + "f")

        @pl.loop(0, 4)
        def _(i):
            group, tile = i // 2, i % 2
            cols = pl.ds(pl.multiple_of(tile * OWN, OWN), OWN)
            made = dot_tn(flat(k.nlow[layer, :, :, cols]), flat(k.slope[group]))
            k.w_up[layer, group, pl.ds(tile * 2, 2)] = made.astype(BF16).reshape((2, 2, 96, 768))

        at(place + "u")
        scatter(UP, layer, 0)
        if layer == 1:
            restore_slope = save(10, k.slope_hbm, k.slope)
        for move in mate_firsts:
            move.wait_recv()
        moves.sent(*mate_firsts)

        @pl.loop(0, 6)
        def _(i):
            group, rows = i // 3, pl.ds(pl.multiple_of((i % 3) * HALF, HALF), HALF)
            k.dmerged[group, rows, :] = dot_nt(k.lfirst[rows, :], k.w_o[layer, group]).astype(BF16)

        for group in range(2):
            made = dot_tn(k.merged[layer, group], k.lfirst[...])
            for zi in range(LINE):
                for xi in range(2):
                    rows = made[(zi * 2 + xi) * 24 : (zi * 2 + xi + 1) * 24]
                    k.w_out[layer, group, zi, xi, :, 0:768] = rows[0:16].astype(BF16)
                    k.w_out[layer, group, zi, xi, :, 768:1152] = jnp.concatenate(
                        [rows[16:24, 0:384], rows[16:24, 384:768]], axis=0
                    ).astype(BF16)

        at(place + "m")
        scatter(OUT, layer, 0)
        if layer == 0:
            restore_probs.wait()

        def attend_back(group, key_start, tiles):
            keys = pl.ds(key_start, SEQ)
            for head in range(3):
                low, high = head * HD, (head + 1) * HD
                key_rows = k.qkv[layer, group, keys, 192 + low : 192 + high]
                values = k.qkv[layer, group, keys, 384 + low : 384 + high]
                grad_keys = jnp.zeros((HD, SEQ), F32)
                grad_values = jnp.zeros((HD, SEQ), F32)
                for start, from_start in tiles:
                    rows, from_rows = pl.ds(start, HALF), pl.ds(pl.multiple_of(from_start, HALF), HALF)
                    queries = k.qkv[layer, group, from_rows, low:high]
                    grad_out = k.dmerged[group, rows, low:high]
                    probs = k.probs[group, head, rows, :]
                    row_dot = jnp.sum(
                        grad_out.astype(F32) * k.merged[layer, group, rows, low:high].astype(F32), axis=-1, keepdims=True
                    )
                    grad_probs = dot_nt(grad_out, values)
                    grad_scores = (probs.astype(F32) * (grad_probs - row_dot)).astype(BF16)
                    grad_values += dot(grad_out.astype(F32).T.astype(BF16), probs)
                    grad_keys += dot(queries.astype(F32).T.astype(BF16), grad_scores)
                    grad_queries = (dot(grad_scores, key_rows) * HD ** (-0.5)).astype(BF16)
                    k.qkv[layer, group, from_rows, low:high] = grad_queries
                k.qkv[layer, group, keys, 192 + low : 192 + high] = grad_keys.T.astype(BF16)
                k.qkv[layer, group, keys, 384 + low : 384 + high] = grad_values.T.astype(BF16)

        def stream_rows(start, size):
            rows = pl.ds(pl.multiple_of(start, 128), size)
            made = dot_nt(k.qkv[layer, 0, rows, :], flat(k.w_qkv[layer, 0]))
            return made + dot_nt(k.qkv[layer, 1, rows, :], flat(k.w_qkv[layer, 1]))

        @pl.loop(0, 2)
        def _(group):
            attend_back(group, SEQ, ((SEQ, SEQ + HALF * y),))
            other = pl.ds(pl.multiple_of(SEQ + HALF * (1 - y), HALF), HALF)
            k.qkv[layer, group, other, 0:192] = jnp.zeros((HALF, 192), BF16)

        away_go, away_end = send_away(lambda slot: stream_rows(SEQ + HALF * (1 - y) + 128 * slot, 128))
        at(place + "p")

        @pl.loop(0, 2)
        def _(group):
            attend_back(group, 0, ((0, 0), (HALF, HALF)))
            for j, row in ((0, 8), (2, 9)):
                sums = jnp.sum(k.qkv[layer, group, :, j * 192 : (j + 1) * 192].astype(F32), axis=0, keepdims=True)
                k.small[layer, 0, pl.ds(row + 2 * group, 1), 0:192] += sums

            @pl.when(group == 0)
            def _():
                away_go()
                at(place + "a")

            pl.when(group == 1)(lambda: at(place + "b"))

        small_step(layer, 0)
        if layer == 1:
            restore_probs = save(8, k.probs_hbm, k.probs)

        end_stream = sum_pair(
            fill_rows(
                lambda slot: stream_rows(slot * HALF, HALF), lambda slot: stream_rows(SEQ + HALF * y + 128 * slot, 128)
            )
        )
        at(place + "t")
        if layer == 0:
            for load in x_load_again:
                load.wait()

        @pl.loop(0, 4)
        def _(i):
            group, tile = i // 2, i % 2
            cols = pl.ds(pl.multiple_of(tile * OWN, OWN), OWN)
            made = dot_tn(k.x_buf[:, cols], k.qkv[layer, group])
            k.w_qkv[layer, group, pl.ds(tile * 2, 2)] = made.astype(BF16).reshape((2, 2, 96, 576))

        at(place + "q")
        scatter(QKV, layer, 0)
        if layer == 1:
            x_load_again = [
                pltpu.make_async_copy(k.x_in.at[pl.ds(pack_row, SEQ)], k.x_buf.at[pl.ds(0, SEQ)], k.local.at[4]),
                pltpu.make_async_copy(k.x_in.at[pl.ds(SEQ, SEQ)], k.x_buf.at[pl.ds(SEQ, SEQ)], k.local.at[5]),
            ]
            for load in x_load_again:
                load.start()
        end_stream()
        away_end()

    k.e_low[...] = (k.res[...] + k.cur[...]).astype(BF16)
    spreads[1] = spread(k.e_low, k.input_grad, 13)
    at("end")
    for layer in range(LAYERS):
        total = k.small.at[layer, 3]
        for row, source, share in [(row, row, LINE * 8) for row in range(6)] + [
            (6, 6 + y, LINE * 2),
            (7, 8 + 2 * y, LINE * 2),
            (8, 9 + 2 * y, LINE * 2),
        ]:
            values = total[pl.ds(source, 1), :]
            k.sq_rows[0:1, 0:DM] += values * values * (1.0 / share)
            if row < 6:
                k.vec_out[row, layer : layer + 1, :] = values
            elif row == 6:
                k.upb_out[layer : layer + 1, :] = values
            else:
                k.qvb_out[layer, row - 7 : row - 6, :] = values[:, 0:192]
    squares = jnp.sum(k.sq_rows[...], axis=0, keepdims=True)
    k.sq[0] = jnp.broadcast_to(jnp.sum(squares, axis=1, keepdims=True), (8, 128))
    for step, (devices, landing) in enumerate(((plane_devs, k.sq_plane), (line_devs, k.sq_line))):
        sent = []
        for index, device in enumerate(devices):
            lands = lambda index=index: landing.at[index]
            sent.append(moves.make(lambda: k.sq.at[step], lands, device, lands))
            sent[-1].start()
        total = k.sq[step]
        for index, move in enumerate(sent):
            move.wait_recv()
            total = total + landing[index]
        k.sq[step + 1] = total
    k.squares[...] = k.sq[2]
    moves.drain()


def kernel_call(inputs, out_grad, lens, w_q, w_o, w_u, w_d, vec, qvb, upb):
    any_ = pl.BlockSpec(memory_space=pl.ANY)
    vmem = pl.BlockSpec(memory_space=pltpu.VMEM)
    smem = pl.BlockSpec(memory_space=pltpu.SMEM)
    ins = dict(
        x_in=(inputs, any_),
        e_in=(out_grad, any_),
        lens=(lens, smem),
        wq_in=(w_q, any_),
        wo_in=(w_o.reshape(LAYERS * 24, DM), any_),
        wu_in=(w_u.reshape(LAYERS * 96, DM), any_),
        wd_in=(w_d.reshape(LAYERS * 96, DM), any_),
        vec=(vec, vmem),
        qvb_in=(qvb, vmem),
        upb_in=(upb, vmem),
    )
    outs = dict(
        activations=((3 * SEQ, DM), BF16, any_),
        input_grad=((3 * SEQ, DM), BF16, any_),
        g_qkv=((LAYERS, 3, 96, 192), F32, vmem),
        g_out=((LAYERS, 24, DM), F32, vmem),
        g_up=((LAYERS, 96, DM), F32, vmem),
        g_down=((LAYERS, 96, DM), F32, vmem),
        vec_out=((6, LAYERS, DM), F32, vmem),
        qvb_out=((LAYERS, 2, 192), F32, vmem),
        upb_out=((LAYERS, DM), F32, vmem),
        squares=((8, 128), F32, vmem),
        probs_hbm=((2, 3, 2 * OWN, SEQ), BF16, any_),
        act_hbm=((2, 2, OWN, DM), BF16, any_),
        slope_hbm=((2, 2, OWN, DM), BF16, any_),
    )
    scratch = dict(
        w_qkv=((LAYERS, 2, LINE, 2, 96, 576), BF16),
        w_out=((LAYERS, 2, LINE, 2, 16, 1152), BF16),
        w_up=((LAYERS, 2, LINE, 2, 96, 768), BF16),
        w_down=((LAYERS, 2, LINE, 2, 96, 768), BF16),
        w_o=((LAYERS, 2, 192, DM), BF16),
        unpack=((192, DM), F32),
        stage_q=((LAYERS, 3, 96, 192), F32),
        x_buf=((2 * SEQ, DM), BF16),
        qkv=((LAYERS, 2, 2 * SEQ, 576), BF16),
        probs=((2, 3, 2 * OWN, SEQ), BF16),
        merged=((LAYERS, 2, 2 * OWN, 192), BF16),
        sum1=((LAYERS, OWN, DM), F32),
        sum2=((OWN, DM), F32),
        nlow=((LAYERS, 2, OWN, DM), BF16),
        act=((2, 2, OWN, DM), BF16),
        slope=((2, 2, OWN, DM), BF16),
        res=((OWN, DM), F32),
        cur=((OWN, DM), F32),
        a_low=((OWN, DM), BF16),
        e_low=((OWN, DM), BF16),
        lsec=((2, OWN, DM), BF16),
        lfirst=((2 * OWN, DM), BF16),
        dmerged=((2, 2 * OWN, 192), BF16),
        ex_s=((SEQ, DM), BF16),
        ex_r=((SEQ, DM), BF16),
        ey_s=((128, DM), BF16),
        ey_r=((128, DM), BF16),
        ey_f=((128, DM), F32),
        bias=((2, 8, DM), F32),
        pair_col=((2, 8, SEQ), F32),
        pair_row=((2, SEQ, 128), F32),
        small=((LAYERS, 4, 16, DM), F32),
        small_in=((LAYERS, 7, 16, DM), F32),
        sq_rows=((8, 1152), F32),
        sq=((3, 8, 128), F32),
        sq_plane=((7, 8, 128), F32),
        sq_line=((LINE - 1, 8, 128), F32),
    )
    landings = {}
    for kind in KINDS:
        axis, first, second = CUTS[1][kind]

        def cut(size):
            shape = list(BLOCK[kind])
            shape[axis] = size
            return tuple(shape)

        p_1, p_2 = cut(first), cut(second - first)
        p_12, p_3 = cut(second), cut(BLOCK[kind][axis] - second)
        landings[kind] = dict(
            ry1=(1, LINE, 2) + p_1,
            rx1=(1, LINE, 1) + p_1,
            rx2=(2, LINE, 1) + p_2,
            ry2=(1, LINE, 1) + p_2,
            rz=(2, 3, 1, 1, 1) + p_12,
            rz3=(2, 3, 2, 1, 2) + p_3,
            ry3=(1, 1, 2) + p_3,
            rx3=(1, 1, 1) + p_3,
        )
    scratch.update({name + kind: (shape, BF16) for kind in KINDS for name, shape in landings[kind].items()})
    names = [*ins, *outs, *scratch, "send", "recv", "local"]
    made = pl.pallas_call(
        lambda *refs: fused(names, *refs),
        out_shape=[jax.ShapeDtypeStruct(shape, dtype) for shape, dtype, _ in outs.values()],
        in_specs=[spec for _, spec in ins.values()],
        out_specs=[spec for *_, spec in outs.values()],
        scratch_shapes=[pltpu.VMEM(shape, dtype) for shape, dtype in scratch.values()]
        + [
            pltpu.SemaphoreType.DMA((SEMS,)),
            pltpu.SemaphoreType.DMA((SEMS,)),
            pltpu.SemaphoreType.DMA((16,)),
        ],
        compiler_params=pltpu.CompilerParams(
            collective_id=0, has_side_effects=True, vmem_limit_bytes=VMEM_BYTES
        ),
        name="encoder_step",
    )(*[value for value, _ in ins.values()])
    return types.SimpleNamespace(**dict(zip(outs, made)))


VMEM_BYTES = 64 * 2**20 - 2**17


def update_kernel(names, *refs):
    k = types.SimpleNamespace(**dict(zip(names, refs)))
    norm = jnp.sqrt(k.squares[0:1, 0:1])
    factor = jnp.minimum(1.0, CLIP_LIMIT / norm)

    def update(name, rate, decay):
        made = adamw(*[vars(k)[part + name][...] for part in "wmvg"], factor, rate, decay)
        for part, value in zip("wmv", made):
            vars(k)["new" + part + name][...] = value

    for name in (QKV, UP, DOWN):
        update(name, LEARN_RATE, WEIGHT_DECAY)

    @pl.when(pl.program_id(1) == 0)
    def _():
        update(OUT, LEARN_RATE, WEIGHT_DECAY)

    @pl.when((pl.program_id(0) == 0) & (pl.program_id(1) == 0))
    def _():
        for name in ("vec", "qvb", "upb"):
            update(name, VECTOR_RATE, 0.0)
        k.norm[...] = norm

    k.new_input_grad[...] = k.input_grad[...].astype(F32)
    k.new_activations[...] = k.activations[...]


def update_call(weights, squares, activations, input_grad):
    blocks = dict(
        qkv=pl.BlockSpec((1, 3, 48, 192), lambda i, j: (i, 0, j, 0)),
        out=pl.BlockSpec((1, 24, DM), lambda i, j: (i, 0, 0)),
        up=pl.BlockSpec((1, 48, DM), lambda i, j: (i, j, 0)),
        down=pl.BlockSpec((1, 48, DM), lambda i, j: (i, j, 0)),
        vec=pl.BlockSpec((6, LAYERS, DM), lambda i, j: (0, 0, 0)),
        qvb=pl.BlockSpec((LAYERS, 2, 192), lambda i, j: (0, 0, 0)),
        upb=pl.BlockSpec((LAYERS, DM), lambda i, j: (0, 0)),
    )
    whole = pl.BlockSpec((8, 128), lambda i, j: (0, 0))
    rows = pl.BlockSpec((OWN, DM), lambda i, j: (i * 2 + j, 0))
    ins = dict(squares=(squares, whole), activations=(activations, rows), input_grad=(input_grad, rows))
    outs = dict(
        norm=(jax.ShapeDtypeStruct((1, 1), F32), F32, pl.BlockSpec((1, 1), lambda i, j: (0, 0))), new_activations=(activations, BF16, rows), new_input_grad=(input_grad, F32, rows)
    )
    for name, arrays in weights.items():
        for part, value in zip("wmvg", arrays):
            ins[part + name] = (value, blocks[name])
            if part != "g":
                outs["new" + part + name] = (value, F32, blocks[name])
    names = [*ins, *outs]
    made = pl.pallas_call(
        lambda *refs: update_kernel(names, *refs),
        grid=(LAYERS, 2),
        out_shape=[jax.ShapeDtypeStruct(like.shape, dtype) for like, dtype, _ in outs.values()],
        in_specs=[spec for _, spec in ins.values()],
        out_specs=[spec for *_, spec in outs.values()],
        name="update",
    )(*[value for value, _ in ins.values()])
    return types.SimpleNamespace(**dict(zip(outs, made)))


def kernel_body(
    inputs,
    pair_lengths,
    out_grad,
    w_qkv,
    m_qkv,
    v_qkv,
    w_out,
    m_out,
    v_out,
    w_up,
    m_up,
    v_up,
    w_down,
    m_down,
    v_down,
    vectors,
    m_vectors,
    v_vectors,
    qv_bias,
    m_qv_bias,
    v_qv_bias,
    up_bias,
    m_up_bias,
    v_up_bias,
):
    turn = lambda v: jnp.transpose(v, (0, 2, 1, 3))
    swap = lambda v: jnp.transpose(v, (1, 0, 2))
    w_qkv, m_qkv, v_qkv = turn(w_qkv), turn(m_qkv), turn(v_qkv)
    vectors, m_vectors, v_vectors = swap(vectors), swap(m_vectors), swap(v_vectors)
    made = kernel_call(inputs, out_grad, pair_lengths, w_qkv, w_out, w_up, w_down, vectors, qv_bias, up_bias)
    weights = dict(
        qkv=(w_qkv, m_qkv, v_qkv, made.g_qkv),
        out=(w_out, m_out, v_out, made.g_out),
        up=(w_up, m_up, v_up, made.g_up),
        down=(w_down, m_down, v_down, made.g_down),
        vec=(vectors, m_vectors, v_vectors, made.vec_out),
        qvb=(qv_bias, m_qv_bias, v_qv_bias, made.qvb_out),
        upb=(up_bias, m_up_bias, v_up_bias, made.upb_out),
    )
    new = update_call(weights, made.squares, made.activations, made.input_grad)
    parts = lambda name: [vars(new)["new" + part + name] for part in "wmv"]
    return (
        new.new_activations,
        new.new_input_grad,
        new.norm.reshape(()),
        *[turn(v) for v in parts(QKV)],
        *parts(OUT),
        *parts(UP),
        *parts(DOWN),
        *[swap(v) for v in parts("vec")],
        *parts("qvb"),
        *parts("upb"),
    )


def solution(mesh):
    rows, matrix = P("dp", None), P(None, ("tensor", "dp"), None)
    qkv, up = P(None, "dp", None, "tensor"), P(None, "dp", "tensor")
    heads, hidden = P(None, None, "tensor"), P(None, "tensor")
    weights = (qkv,) * 3 + (matrix,) * 3 + (up,) * 3 + (matrix,) * 3
    smalls = (P(),) * 3 + (heads,) * 3 + (hidden,) * 3
    fits = mesh.shape["dp"] == 2 * LINE and mesh.shape["tensor"] == 4
    return jax.shard_map(
        kernel_body if fits else body,
        mesh=mesh,
        in_specs=(rows, rows, rows) + weights + smalls,
        out_specs=(rows, rows, P()) + weights + smalls,
        check_vma=False,
    )
```

```python
import math
import types

import jax
import jax.numpy as jnp
from jax import lax
from jax.experimental import pallas as pl
from jax.experimental.pallas import tpu as pltpu
from jax.sharding import PartitionSpec as P

HD = 64
SEQ = 512
LAYERS = 2
STEP = 10


NORM_EPS = 1e-05
CLIP_LIMIT = 0.05
BETA_ONE = 0.9
BETA_TWO = 0.999
LEARN_RATE = 0.1
VECTOR_RATE = 1.0
WEIGHT_DECAY = 0.01
ADAM_EPS = 1e-08


def layer_norm(rows_in, gain, shift):
    center = rows_in - jnp.mean(rows_in, axis=-1, keepdims=True)
    spread = jnp.mean(center * center, axis=-1, keepdims=True)
    return center * lax.rsqrt(spread + NORM_EPS) * gain + shift


def gelu_exact(pre_values):
    return jax.nn.gelu(pre_values, approximate=False)


def pair_mask(lengths):
    ends = jnp.cumsum(lengths)
    positions = jnp.arange(SEQ, dtype=jnp.int32)
    pair_of = jnp.sum((positions[:, None] >= ends[None, :]).astype(jnp.int32), axis=1)
    return pair_of[:, None] == pair_of[None, :]


def pack_scores(queries, key_rows, masks):
    scores = jnp.einsum(
        "pqhe,pkhe->phqk", queries, key_rows, preferred_element_type=jnp.float32
    ) * HD ** (-0.5)
    return jnp.where(masks[:, None], scores, -1e30)


def attend(queries, key_rows, values, masks):
    scores = pack_scores(queries, key_rows, masks)
    top = jnp.max(scores, axis=-1, keepdims=True)
    weights = jnp.exp(scores - top)
    total = jnp.sum(weights, axis=-1, keepdims=True)
    probs = weights / total
    attended = jnp.einsum(
        "phqk,pkhe->pqhe", probs.astype(jnp.bfloat16), values, preferred_element_type=jnp.float32
    )
    return (attended, top + jnp.log(total))


def attend_back(queries, key_rows, values, grad_attended, log_total, masks):
    scores = pack_scores(queries, key_rows, masks)
    probs = jnp.exp(scores - log_total)
    grad_values = jnp.einsum(
        "phqk,pqhe->pkhe",
        probs.astype(jnp.bfloat16),
        grad_attended,
        preferred_element_type=jnp.float32,
    )
    grad_probs = jnp.einsum(
        "pqhe,pkhe->phqk", grad_attended, values, preferred_element_type=jnp.float32
    )
    row_dot = jnp.sum(grad_probs * probs, axis=-1, keepdims=True)
    grad_scores = (probs * (grad_probs - row_dot)).astype(jnp.bfloat16)
    grad_queries = jnp.einsum(
        "phqk,pkhe->pqhe", grad_scores, key_rows, preferred_element_type=jnp.float32
    ) * HD ** (-0.5)
    grad_keys = jnp.einsum(
        "phqk,pqhe->pkhe", grad_scores, queries, preferred_element_type=jnp.float32
    ) * HD ** (-0.5)
    return (
        grad_queries.astype(jnp.bfloat16),
        grad_keys.astype(jnp.bfloat16),
        grad_values.astype(jnp.bfloat16),
    )


def layer_forward(stream, qkv_w, out_w, up_w, down_w, vector_rows, qv_rows, up_row, masks):
    row_count = stream.shape[0]
    pack_count = masks.shape[0]
    width = out_w.shape[0]
    group_heads = width // HD
    stream_low = stream.astype(jnp.bfloat16)
    project = jnp.einsum("td,dcn->tcn", stream_low, qkv_w, preferred_element_type=jnp.float32)
    queries = (
        (project[:, 0] + qv_rows[0]).astype(jnp.bfloat16).reshape(pack_count, SEQ, group_heads, HD)
    )
    key_rows = project[:, 1].astype(jnp.bfloat16).reshape(pack_count, SEQ, group_heads, HD)
    values = (
        (project[:, 2] + qv_rows[1]).astype(jnp.bfloat16).reshape(pack_count, SEQ, group_heads, HD)
    )
    attended, log_total = attend(queries, key_rows, values, masks)
    merged = attended.reshape(row_count, width).astype(jnp.bfloat16)
    attn_part = jnp.dot(merged, out_w, preferred_element_type=jnp.float32)
    attn_summed = lax.psum(attn_part.astype(jnp.bfloat16), "tensor").astype(jnp.float32)
    first_sum = stream + attn_summed + vector_rows[4]
    normed = layer_norm(first_sum, vector_rows[0], vector_rows[1])
    normed_low = normed.astype(jnp.bfloat16)
    hidden_pre = jnp.dot(normed_low, up_w, preferred_element_type=jnp.float32) + up_row
    hidden_act = gelu_exact(hidden_pre).astype(jnp.bfloat16)
    ffn_part = jnp.dot(hidden_act, down_w, preferred_element_type=jnp.float32)
    ffn_summed = lax.psum(ffn_part.astype(jnp.bfloat16), "tensor").astype(jnp.float32)
    second_sum = normed + ffn_summed + vector_rows[5]
    result = layer_norm(second_sum, vector_rows[2], vector_rows[3])
    kept = (
        stream_low,
        queries,
        key_rows,
        values,
        log_total,
        merged,
        first_sum,
        normed_low,
        hidden_pre,
        hidden_act,
        second_sum,
    )
    return (result, kept)


def layer_backward(grad_out, kept, qkv_w, out_w, up_w, down_w, vector_rows, masks):
    (
        stream_low,
        queries,
        key_rows,
        values,
        log_total,
        merged,
        first_sum,
        normed_low,
        hidden_pre,
        hidden_act,
        second_sum,
    ) = kept
    row_count = stream_low.shape[0]
    width = out_w.shape[0]
    _, pull_second = jax.vjp(layer_norm, second_sum, vector_rows[2], vector_rows[3])
    grad_second, grad_gain_two, grad_shift_two = pull_second(grad_out)
    grad_down_bias = jnp.sum(grad_second, axis=0)
    low_second = grad_second.astype(jnp.bfloat16)
    grad_down = jnp.einsum("tf,td->fd", hidden_act, low_second, preferred_element_type=jnp.float32)
    grad_act = jnp.einsum("td,fd->tf", low_second, down_w, preferred_element_type=jnp.float32)
    _, pull_gelu = jax.vjp(gelu_exact, hidden_pre)
    grad_pre = pull_gelu(grad_act)[0].astype(jnp.bfloat16)
    grad_up_bias = jnp.sum(grad_pre.astype(jnp.float32), axis=0)
    grad_up = jnp.einsum("td,tf->df", normed_low, grad_pre, preferred_element_type=jnp.float32)
    back_normed = jnp.einsum("tf,df->td", grad_pre, up_w, preferred_element_type=jnp.float32)
    grad_normed = grad_second + lax.psum(back_normed.astype(jnp.bfloat16), "tensor").astype(
        jnp.float32
    )
    _, pull_first = jax.vjp(layer_norm, first_sum, vector_rows[0], vector_rows[1])
    grad_first, grad_gain_one, grad_shift_one = pull_first(grad_normed)
    grad_out_bias = jnp.sum(grad_first, axis=0)
    low_first = grad_first.astype(jnp.bfloat16)
    grad_outw = jnp.einsum("tn,td->nd", merged, low_first, preferred_element_type=jnp.float32)
    grad_merged = jnp.einsum(
        "td,nd->tn", low_first, out_w, preferred_element_type=jnp.float32
    ).astype(jnp.bfloat16)
    grad_queries, grad_keys, grad_values = attend_back(
        queries, key_rows, values, grad_merged.reshape(queries.shape), log_total, masks
    )
    grad_project = jnp.stack(
        (
            grad_queries.reshape(row_count, width),
            grad_keys.reshape(row_count, width),
            grad_values.reshape(row_count, width),
        ),
        axis=1,
    )
    grad_qv_bias = jnp.sum(grad_project[:, 0::2].astype(jnp.float32), axis=0)
    grad_qkv = jnp.einsum(
        "td,tcn->dcn", stream_low, grad_project, preferred_element_type=jnp.float32
    )
    back_stream = jnp.einsum("tcn,dcn->td", grad_project, qkv_w, preferred_element_type=jnp.float32)
    grad_stream = grad_first + lax.psum(back_stream.astype(jnp.bfloat16), "tensor").astype(
        jnp.float32
    )
    vector_grad = jnp.stack(
        (
            grad_gain_one,
            grad_shift_one,
            grad_gain_two,
            grad_shift_two,
            grad_out_bias,
            grad_down_bias,
        )
    )
    return (
        grad_stream,
        (grad_qkv, grad_outw, grad_up, grad_down),
        (vector_grad, grad_qv_bias, grad_up_bias),
    )


def adamw(weight, first, second, gradient, factor, rate, decay):
    clipped = gradient * factor
    new_first = BETA_ONE * first + (1.0 - BETA_ONE) * clipped
    new_second = BETA_TWO * second + (1.0 - BETA_TWO) * clipped * clipped
    first_hat = new_first / (1.0 - BETA_ONE**STEP)
    second_hat = new_second / (1.0 - BETA_TWO**STEP)
    new_weight = weight - rate * (first_hat / (jnp.sqrt(second_hat) + ADAM_EPS) + decay * weight)
    return (new_weight, new_first, new_second)


def body(
    inputs,
    pair_lengths,
    out_grad,
    w_qkv,
    m_qkv,
    v_qkv,
    w_out,
    m_out,
    v_out,
    w_up,
    m_up,
    v_up,
    w_down,
    m_down,
    v_down,
    vectors,
    m_vectors,
    v_vectors,
    qv_bias,
    m_qv_bias,
    v_qv_bias,
    up_bias,
    m_up_bias,
    v_up_bias,
):
    full_qkv, full_out, full_up, full_down = (
        lax.all_gather(w_qkv.astype(jnp.bfloat16), "dp", axis=1, tiled=True),
        lax.all_gather(w_out.astype(jnp.bfloat16), "dp", axis=1, tiled=True),
        lax.all_gather(w_up.astype(jnp.bfloat16), "dp", axis=1, tiled=True),
        lax.all_gather(w_down.astype(jnp.bfloat16), "dp", axis=1, tiled=True),
    )
    masks = jax.vmap(pair_mask)(pair_lengths)
    stream = inputs.astype(jnp.float32)
    kept_all = []
    for layer_index in range(LAYERS):
        stream, kept = layer_forward(
            stream,
            full_qkv[layer_index],
            full_out[layer_index],
            full_up[layer_index],
            full_down[layer_index],
            vectors[layer_index],
            qv_bias[layer_index],
            up_bias[layer_index],
            masks,
        )
        kept_all.append(kept)
    activations = stream.astype(jnp.bfloat16)
    grad_stream = out_grad.astype(jnp.float32)
    matrix_grads = [None] * LAYERS
    small_grads = [None] * LAYERS
    for layer_index in reversed(range(LAYERS)):
        grad_stream, mats, smalls = layer_backward(
            grad_stream,
            kept_all[layer_index],
            full_qkv[layer_index],
            full_out[layer_index],
            full_up[layer_index],
            full_down[layer_index],
            vectors[layer_index],
            masks,
        )
        matrix_grads[layer_index] = mats
        small_grads[layer_index] = smalls
    stacked = tuple(
        (
            jnp.stack([matrix_grads[layer_index][kind] for layer_index in range(LAYERS)])
            for kind in range(4)
        )
    )
    g_qkv, g_out, g_up, g_down = (
        lax.psum_scatter(stacked[0], "dp", scatter_dimension=1, tiled=True),
        lax.psum_scatter(stacked[1], "dp", scatter_dimension=1, tiled=True),
        lax.psum_scatter(stacked[2], "dp", scatter_dimension=1, tiled=True),
        lax.psum_scatter(stacked[3], "dp", scatter_dimension=1, tiled=True),
    )
    small_stacked = tuple(
        (
            jnp.stack([small_grads[layer_index][kind] for layer_index in range(LAYERS)])
            for kind in range(3)
        )
    )
    g_vec, g_qv, g_upb = lax.psum(small_stacked, "dp")
    data_count = lax.axis_size("dp")
    tensor_count = lax.axis_size("tensor")
    local_squares = (
        jnp.sum(g_qkv * g_qkv)
        + jnp.sum(g_out * g_out)
        + jnp.sum(g_up * g_up)
        + jnp.sum(g_down * g_down)
        + (jnp.sum(g_qv * g_qv) + jnp.sum(g_upb * g_upb)) / data_count
        + jnp.sum(g_vec * g_vec) / (data_count * tensor_count)
    )
    squares = lax.psum(local_squares, ("dp", "tensor"))
    grad_norm = jnp.sqrt(squares)
    factor = jnp.minimum(1.0, CLIP_LIMIT / grad_norm)
    new_qkv = adamw(w_qkv, m_qkv, v_qkv, g_qkv, factor, LEARN_RATE, WEIGHT_DECAY)
    new_out = adamw(w_out, m_out, v_out, g_out, factor, LEARN_RATE, WEIGHT_DECAY)
    new_up = adamw(w_up, m_up, v_up, g_up, factor, LEARN_RATE, WEIGHT_DECAY)
    new_down = adamw(w_down, m_down, v_down, g_down, factor, LEARN_RATE, WEIGHT_DECAY)
    new_vec = adamw(vectors, m_vectors, v_vectors, g_vec, factor, VECTOR_RATE, 0.0)
    new_qv = adamw(qv_bias, m_qv_bias, v_qv_bias, g_qv, factor, VECTOR_RATE, 0.0)
    new_upb = adamw(up_bias, m_up_bias, v_up_bias, g_upb, factor, VECTOR_RATE, 0.0)
    return (
        activations,
        grad_stream,
        grad_norm,
        new_qkv[0],
        new_qkv[1],
        new_qkv[2],
        new_out[0],
        new_out[1],
        new_out[2],
        new_up[0],
        new_up[1],
        new_up[2],
        new_down[0],
        new_down[1],
        new_down[2],
        new_vec[0],
        new_vec[1],
        new_vec[2],
        new_qv[0],
        new_qv[1],
        new_qv[2],
        new_upb[0],
        new_upb[1],
        new_upb[2],
    )


MESH = pl.DeviceIdType.MESH
F32, BF16 = jnp.float32, jnp.bfloat16
LINE = 4
DM = 768
QKV, OUT, UP, DOWN = KINDS = ("qkv", "out", "up", "down")
FIRST, SECOND, EARLY, LATE = range(4)
BLOCK = {QKV: (96, 576), OUT: (16, 1152), UP: (96, 768), DOWN: (96, 768)}
CUTS = (
    {QKV: (0, 48, 80), OUT: (1, 384, 1024), UP: (0, 32, 80), DOWN: (0, 32, 64)},
    {QKV: (0, 32, 80), OUT: (1, 384, 896), UP: (0, 32, 80), DOWN: (0, 16, 64)},
    {QKV: (0, 48, 96), OUT: (1, 512, 1152), UP: (0, 32, 80), DOWN: (0, 32, 64)},
)
G, L, F, S, M, R = range(6)
PLAN = {
    "need0": (
        (G, 1, 0),
        (L, 4, 1),
        (L, 2, 1),
        (G, 0, 1),
        (L, 1, 1),
        (L, 5, 1),
        (G, 2, 0),
        (G, 0, 2),
        (G, 1, 1),
        (L, 3, 1),
        (G, 0, 3),
        (G, 1, 2),
        (L, 2, 2),
        (G, 2, 1),
        (G, 1, 3),
        (L, 1, 2),
        (G, 4, 0),
        (G, 0, 5),
        (G, 0, 4),
        (G, 5, 0),
        (G, 2, 2),
        (G, 3, 0),
        (L, 1, 3),
        (G, 3, 1),
        (G, 2, 3),
        (G, 1, 5),
        (G, 1, 4),
        (G, 3, 2),
        (L, 3, 2),
        (L, 5, 2),
        (L, 1, 4),
        (G, 3, 3),
        (F, 0),
        (L, 2, 3),
        (G, 4, 1),
        (G, 2, 4),
        (L, 4, 2),
    ),
    "f0a2": ((L, 3, 3),),
    "f0o": ((G, 2, 5), (L, 2, 4), (G, 3, 5), (G, 5, 1), (F, 1), (G, 4, 2), (L, 5, 3), (G, 3, 4),),
    "f0v": ((F, 2),),
    "f0d": ((G, 5, 2), (G, 4, 3),),
    "need3": ((L, 3, 4), (F, 3), (L, 4, 3), (G, 5, 3), (L, 5, 4),),
    "f1q": ((G, 4, 5),),
    "f1a0": ((G, 4, 4),),
    "need5": ((F, 5),),
    "b1s": ((R, 0, 0),),
    "b1p": ((S, 3, 1, 6),),
    "b1a": ((S, 3, 1, 2),),
    "b1q": ((S, 3, 1, 1), (S, 2, 1, 2), (S, 2, 1, 6), (S, 2, 1, 1), (S, 3, 1, 8),),
    "b0s": ((S, 3, 1, 3), (S, 1, 1, 6),),
    "b0w": (
        (S, 2, 1, 3),
        (S, 3, 1, 5),
        (S, 3, 1, 9),
        (S, 2, 1, 7),
        (S, 1, 1, 2),
        (S, 0, 1, 7),
        (S, 1, 1, 1),
        (S, 2, 1, 4),
        (S, 1, 1, 7),
        (S, 0, 1, 2),
        (S, 0, 1, 1),
        (S, 3, 1, 10),
    ),
    "b0u": (
        (S, 1, 1, 3),
        (S, 1, 1, 8),
        (S, 0, 1, 8),
        (S, 2, 1, 8),
        (S, 0, 1, 3),
        (S, 1, 1, 4),
        (S, 2, 1, 5),
        (S, 1, 1, 9),
        (S, 0, 1, 4),
        (S, 2, 1, 9),
        (M, 1, 1),
        (S, 1, 1, 5),
        (S, 0, 1, 9),
        (S, 3, 0, 2),
        (S, 3, 0, 6),
        (S, 3, 0, 1),
        (R, 0, 1),
        (S, 0, 1, 5),
        (S, 2, 1, 10),
        (S, 1, 1, 10),
    ),
    "b0p": ((S, 3, 0, 3),),
    "b0a": ((S, 0, 1, 10),),
    "end": (
        (R, 0, 2),
        (S, 2, 0, 6),
        (S, 3, 0, 4),
        (S, 2, 0, 1),
        (S, 2, 0, 2),
        (M, 0, 1),
        (S, 1, 0, 1),
        (S, 1, 0, 6),
        (M, 1, 2),
        (S, 1, 0, 2),
        (S, 3, 0, 5),
        (S, 0, 0, 2),
        (S, 0, 0, 1),
        (S, 0, 0, 6),
        (M, 1, 3),
        (S, 3, 0, 7),
        (S, 2, 0, 3),
        (S, 1, 0, 3),
        (R, 1, 0),
        (S, 2, 0, 7),
        (S, 0, 0, 3),
        (S, 0, 0, 7),
        (S, 2, 0, 4),
        (S, 1, 0, 7),
        (S, 1, 0, 4),
        (S, 0, 0, 8),
        (M, 0, 2),
        (S, 0, 0, 4),
        (S, 1, 0, 8),
        (S, 2, 0, 5),
        (S, 2, 0, 8),
        (S, 3, 0, 8),
        (R, 1, 1),
        (S, 1, 0, 5),
        (S, 2, 0, 9),
        (S, 1, 0, 9),
        (S, 0, 0, 5),
        (M, 0, 3),
        (S, 0, 0, 9),
        (S, 3, 0, 9),
        (S, 0, 0, 10),
        (R, 1, 2),
        (S, 2, 0, 10),
        (S, 1, 0, 10),
        (S, 3, 0, 10),
    ),
    "b1b": ((S, 3, 1, 7),),
    "b0h": ((S, 3, 1, 4), (S, 0, 1, 6),),
    "f1o": ((L, 4, 4), (G, 5, 4), (G, 5, 5),),
    "f1n": ((F, 4),),
}
SEMS = 205
OWN, HALF = 384, 256


def dot(a, b):
    return jnp.dot(a, b, preferred_element_type=F32)


def dot_nt(a, b):
    return lax.dot_general(a, b, (((1,), (1,)), ((), ())), preferred_element_type=F32)


def dot_tn(a, b):
    return lax.dot_general(a, b, (((0,), (0,)), ((), ())), preferred_element_type=F32)


def flat(v):
    return v.reshape((-1, v.shape[-1]))


def gelu_and_slope(u):
    a = jnp.abs(u) * (1.0 / math.sqrt(2.0))
    t = 1.0 / (1.0 + 0.5 * a)
    poly = 0.17087277
    for coeff in (
        -0.82215223,
        1.48851587,
        -1.13520398,
        0.27886807,
        -0.18628806,
        0.09678418,
        0.37409196,
        1.00002368,
        -1.26551223,
    ):
        poly = poly * t + coeff
    bell = jnp.exp(-0.5 * u * u)
    tail = 0.5 * t * bell * jnp.exp(poly)
    below = jnp.where(u >= 0, 1.0 - tail, tail)
    return u * below, below + u * bell * (1.0 / math.sqrt(2.0 * math.pi))


def norm_stats(rows):
    center = rows - jnp.mean(rows, axis=-1, keepdims=True)
    spread = jnp.mean(center * center, axis=-1, keepdims=True)
    scale = lax.rsqrt(spread + NORM_EPS)
    return center * scale, scale


class Moves:
    def __init__(self, send, recv):
        self.send, self.recv, self.count, self.open = send, recv, 0, []
        self.again, self.log = [], []

    def make(self, src, dst, device, lands, can_send=None, can_recv=None):
        if self.again:
            index = self.again.pop(0)
        else:
            index = self.count
            self.count += 1
        assert index < SEMS
        self.log.append(index)
        move = types.SimpleNamespace(index=index)

        def copy(src, dst):
            return pltpu.make_async_remote_copy(
                src_ref=src,
                dst_ref=dst,
                send_sem=self.send.at[index],
                recv_sem=self.recv.at[index],
                device_id=device,
                device_id_type=MESH,
            )

        def guarded(cond, act):
            if cond is None:
                act()
            else:
                pl.when(cond)(act)

        def start():
            guarded(can_send, lambda: copy(src(), dst()).start())
            self.open.append(move)

        move.start = start
        move.wait_recv = lambda: guarded(can_recv, lambda: copy(lands(), lands()).wait_recv())
        move.wait_send = lambda: guarded(can_send, lambda: copy(src(), src()).wait_send())
        return move

    def sent(self, *moves):
        for move in moves:
            move.wait_send()
            self.open.remove(move)

    def drain_but(self, *moves):
        self.sent(*[move for move in self.open if move not in moves])

    def drain(self):
        for move in self.open:
            move.wait_send()
        self.open = []


def fused(names, *refs):
    k = types.SimpleNamespace(**dict(zip(names, refs)))
    dp, tensor = lax.axis_index("dp"), lax.axis_index("tensor")
    z, x, y, c = dp // 2, dp % 2, tensor // 2, tensor % 2
    core_dev = (dp, y * 2 + 1 - c)
    y_dev = (dp, (1 - y) * 2 + c)
    x_dev = (z * 2 + 1 - x, tensor)
    up_dev = ((z + 1) * 2 + x, tensor)
    down_dev = ((z - 1) * 2 + x, tensor)
    xy_dev = (z * 2 + 1 - x, (1 - y) * 2 + c)
    not_last, not_first = z <= LINE - 2, z >= 1

    pack_row = pl.multiple_of(y * (2 * SEQ), SEQ)
    own_a = pl.multiple_of(c * HALF, HALF)
    own_p = pl.multiple_of(SEQ + HALF * y + 128 * c, 128)
    loads = [
        pltpu.make_async_copy(k.wq_in, k.stage_q, k.local.at[0]),
        pltpu.make_async_copy(k.wu_in, k.sum1.at[0, pl.ds(0, 192)], k.local.at[1]),
        pltpu.make_async_copy(k.wd_in, k.sum1.at[0, pl.ds(192, 192)], k.local.at[2]),
        pltpu.make_async_copy(k.wo_in, k.sum1.at[1, pl.ds(0, 48)], k.local.at[3]),
    ]
    x_loads = [
        pltpu.make_async_copy(k.x_in.at[pl.ds(pack_row, SEQ)], k.x_buf.at[pl.ds(0, SEQ)], k.local.at[4]),
        pltpu.make_async_copy(k.x_in.at[pl.ds(SEQ, SEQ)], k.x_buf.at[pl.ds(SEQ, SEQ)], k.local.at[5]),
    ]
    in_a = pl.multiple_of(pack_row + own_a, HALF)
    e_loads = [
        pltpu.make_async_copy(k.e_in.at[pl.ds(in_a, HALF)], k.e_low.at[pl.ds(0, HALF)], k.local.at[6]),
        pltpu.make_async_copy(k.e_in.at[pl.ds(own_p, 128)], k.e_low.at[pl.ds(HALF, 128)], k.local.at[7]),
    ]
    for load in loads + x_loads + e_loads:
        load.start()

    plane_devs = [(z * 2 + (x ^ i // 4), (y ^ i // 2 % 2) * 2 + (c ^ i % 2)) for i in range(1, 8)]
    line_devs = [((z ^ i) * 2 + x, tensor) for i in range(1, LINE)]
    barrier = pltpu.get_barrier_semaphore()
    for device in plane_devs + line_devs:
        pl.semaphore_signal(barrier, inc=1, device_id=device, device_id_type=MESH)

    moves = Moves(k.send, k.recv)
    weights = {QKV: k.w_qkv, OUT: k.w_out, UP: k.w_up, DOWN: k.w_down}

    def one(v):
        return (v, 1)

    both, line = (0, 2), (0, LINE)

    def part(kind, number, cuts=0):
        axis, first, second = CUTS[cuts][kind]
        full = BLOCK[kind]
        low, high = ((0, first), (first, second), (0, second), (second, full[axis]))[number]
        cut = [(0, full[0]), (0, full[1])]
        cut[axis] = (low, high - low)
        return tuple(cut)

    def region(kind, layer, ys, zs, xs, number, cuts=0):
        rows, cols = part(kind, number, 2 if cuts == 0 and layer == 0 and kind in (QKV, OUT) else cuts)
        return weights[kind].at[(layer,) + tuple(pl.ds(*cut) for cut in (ys, zs, xs, rows, cols))]

    def swap(kind, layer, axis, number, ys, zs, xs):
        other_ys, other_xs = (one(1 - y), xs) if axis == "y" else (ys, one(1 - x))
        here = lambda: region(kind, layer, ys, zs, xs, number)
        return [
            moves.make(
                here,
                here,
                y_dev if axis == "y" else x_dev,
                lambda: region(kind, layer, other_ys, zs, other_xs, number),
            )
        ]

    def hop(kind, layer, step, number, ys, xs):
        at = lambda v: (lambda: region(kind, layer, ys, one(v), xs, number))
        return [
            moves.make(
                at(z - step + 1),
                at(z - step + 1),
                up_dev,
                at(z - step),
                (z >= step - 1) & not_last,
                z >= step,
            ),
            moves.make(
                at(z + step - 1),
                at(z + step - 1),
                down_dev,
                at(z + step),
                (z <= LINE - step) & not_first,
                z <= LINE - 1 - step,
            ),
        ]

    def gather_steps(kind, layer):
        a = (kind, layer)
        hops = [hop(*a, step, EARLY, one(y), one(x)) for step in (1, 2, 3)]
        first_x = swap(*a, "x", FIRST, one(y), line, one(x))
        second_y = swap(*a, "y", SECOND, one(y), line, one(x))
        first_y = swap(*a, "y", FIRST, one(y), line, both)
        second_x = swap(*a, "x", SECOND, both, line, one(x))
        early = [
            ([], hops[0]),
            (hops[0], hops[1]),
            (hops[1], hops[2]),
            (hops[2], first_x + second_y),
            (first_x, first_y),
            (second_y, second_x),
            (first_y + second_x, []),
        ]
        if layer == 0 and kind in (QKV, OUT):
            return early, [([], [])] * 6
        late_x = swap(*a, "x", LATE, one(y), one(z), one(x))
        late_y = swap(*a, "y", LATE, one(y), one(z), both)
        hops = [hop(*a, step, LATE, both, both) for step in (1, 2, 3)]
        return early, [([], late_x), (late_x, late_y), (late_y, hops[0]), (hops[0], hops[1]), (hops[1], hops[2]), (hops[2], [])]

    gather_chunks = [
        ((QKV, 0), (OUT, 0)),
        ((UP, 0),),
        ((DOWN, 0),),
        ((QKV, 1), (OUT, 1)),
        ((UP, 1),),
        ((DOWN, 1),),
    ]
    gathers, indices = [], {}
    for chunk in gather_chunks:
        gathers.append([])
        for kind, layer in chunk:
            start = moves.count
            gathers[-1].append(gather_steps(kind, layer))
            indices[kind, layer] = list(range(start, moves.count))

    def gather(chunk, late, step):
        for steps in gathers[chunk]:
            for move in steps[late][step][0]:
                move.wait_recv()
        for steps in gathers[chunk]:
            for move in steps[late][step][1]:
                move.start()

    def add_into(kind, layer, ys, zs, xs, number, buf, from_xs=0, from_ys=0):
        rows, cols = part(kind, number, 1)
        count = (ys[1], zs[1], xs[1])

        @pl.loop(0, count[0] * count[1] * count[2])
        def _(i):
            yi, zi, xi = i // (count[1] * count[2]), (i // count[2]) % count[1], i % count[2]
            at = (layer, ys[0] + yi, zs[0] + zi, xs[0] + xi, pl.ds(*rows), pl.ds(*cols))
            weights[kind][at] = weights[kind][at] + buf[from_ys + yi, zi, from_xs + xi]

    def scatter_swap(kind, layer, axis, number, ys, zs, xs, buf):
        away_ys, away_xs = (one(1 - y), xs) if axis == "y" else (ys, one(1 - x))
        landing = lambda: buf
        return moves.make(
            lambda: region(kind, layer, away_ys, zs, away_xs, number, 1),
            landing,
            y_dev if axis == "y" else x_dev,
            landing,
        )

    def scatter_hop(kind, layer, step, number, ys, xs, buf):
        found = []
        for way, device, goes, sends, comes, receives in (
            (0, up_dev, z + LINE - step, (z <= step - 1) & not_last, z + 3 - step, not_first & (z <= step)),
            (1, down_dev, z - LINE + step, (z >= LINE - step) & not_first, z - 3 + step, not_last & (z >= 3 - step)),
        ):
            landing = lambda way=way: buf.at[way, step - 1]
            move = moves.make(
                lambda goes=goes: region(kind, layer, ys, one(goes), xs, number, 1),
                landing,
                device,
                landing,
                sends,
                receives,
            )

            def add(way=way, comes=comes, receives=receives):
                pl.when(receives)(
                    lambda: add_into(kind, layer, ys, one(comes), xs, number, buf.at[way, step - 1])
                )

            found.append((move, add))
        return found

    def scatter_steps(kind, layer):
        a = (kind, layer)
        r = types.SimpleNamespace(
            **{name[: -len(kind)]: ref for name, ref in vars(k).items() if name[0] == "r" and name.endswith(kind)}
        )
        first_y = scatter_swap(*a, "y", FIRST, both, line, both, r.ry1)
        second_x = scatter_swap(*a, "x", SECOND, both, line, both, r.rx2)
        first_x = scatter_swap(*a, "x", FIRST, one(y), line, both, r.rx1)
        second_y = scatter_swap(*a, "y", SECOND, both, line, one(x), r.ry2)
        late_y = scatter_swap(*a, "y", LATE, both, one(z), both, r.ry3)
        late_x = scatter_swap(*a, "x", LATE, one(y), one(z), both, r.rx3)
        early = [scatter_hop(*a, step, EARLY, one(y), one(x), r.rz) for step in (1, 2, 3)]
        late = [scatter_hop(*a, step, LATE, both, both, r.rz3) for step in (1, 2, 3)]

        def starts(found):
            return [move.start for move, _ in found]

        def onward(found, then):
            steps = []
            for index, (move, add) in enumerate(found):
                steps += [move.wait_recv, add]
                if then:
                    steps.append(then[index][0].start)
            return steps

        return [
            [first_y.start, second_x.start] + starts(late[0]),
            [
                first_y.wait_recv,
                lambda: add_into(*a, one(y), line, one(1 - x), FIRST, r.ry1, from_xs=1 - x),
                first_x.start,
                lambda: add_into(*a, one(y), line, one(x), FIRST, r.ry1, from_xs=x),
            ],
            [
                second_x.wait_recv,
                lambda: add_into(*a, one(1 - y), line, one(x), SECOND, r.rx2, from_ys=1 - y),
                second_y.start,
                lambda: add_into(*a, one(y), line, one(x), SECOND, r.rx2, from_ys=y),
            ],
            [
                first_x.wait_recv,
                lambda: add_into(*a, one(y), line, one(x), FIRST, r.rx1),
                second_y.wait_recv,
                lambda: add_into(*a, one(y), line, one(x), SECOND, r.ry2),
            ]
            + starts(early[0]),
            onward(early[0], early[1]),
            onward(early[1], early[2]),
            onward(late[0], late[1]),
            onward(late[1], late[2]),
            onward(late[2], None) + [late_y.start],
            [late_y.wait_recv, lambda: add_into(*a, one(y), one(z), both, LATE, r.ry3), late_x.start],
            onward(early[2], None)
            + [
                late_x.wait_recv,
                lambda: add_into(*a, one(y), one(z), one(x), LATE, r.rx3),
                lambda: finish(kind, layer),
            ],
        ]

    def finish(kind, layer):
        total = weights[kind][layer, y, z, x].astype(F32)
        size, width = BLOCK[kind]
        k.sq_rows[:, 0:width] += jnp.sum((total * total).reshape((size // 8, 8, width)), axis=0)
        if kind == QKV:
            for j in range(3):
                k.g_qkv[layer, j] = total[:, j * 192 : (j + 1) * 192]
        elif kind == OUT:
            k.g_out[layer, 0:16, :] = total[:, 0:768]
            k.g_out[layer, 16:24, 0:384] = total[0:8, 768:1152]
            k.g_out[layer, 16:24, 384:768] = total[8:16, 768:1152]
        else:
            (k.g_up if kind == UP else k.g_down)[layer] = total

    scatters, used = {}, {}
    lenders = {DOWN: UP, UP: QKV, OUT: OUT, QKV: DOWN}

    def scatter(kind, layer, step):
        chunk = (kind, layer)
        if step == 0:
            if layer:
                moves.again = list(indices[lenders[kind], 0])
            else:
                moves.sent(*[move for move in moves.open if move.index in used[kind]])
                moves.again = list(used[kind])
            before = len(moves.log)
            scatters[chunk] = scatter_steps(kind, layer)
            used[kind] = moves.log[before:]
            moves.again = []
        for act in scatters[chunk][step]:
            act()

    def small_step(layer, step):
        if step:
            total = k.small[layer, step - 1]
            for index, move in small_moves[layer]:
                move.wait_recv()
                total = total + k.small_in[layer, index]
            if step == 1:
                row = lax.broadcasted_iota(jnp.int32, (16, DM), 0)
                total = jnp.where(row < 6, total, k.small[layer, 0])
            k.small[layer, step] = total
        if step < 3:
            devices = ((core_dev,), (x_dev, y_dev, xy_dev), line_devs)[step]
            small_moves[layer] = []
            for i, device in enumerate(devices):
                index = (0, 1, 4)[step] + i
                landing = lambda index=index: k.small_in.at[layer, index]
                move = moves.make(lambda: k.small.at[layer, step], landing, device, landing)
                move.start()
                small_moves[layer].append((index, move))

    small_moves = {}

    spreads = {}

    def at(name):
        for what, *args in PLAN.get(name, ()):
            if what == G:
                gather(args[0], 0, args[1])
            elif what == L:
                gather(args[0], 1, args[1])
            elif what == F:
                gather(args[0], 0, 6)
                gather(args[0], 1, 5)
            elif what == S:
                scatter(KINDS[args[0]], args[1], args[2])
            elif what == M:
                small_step(*args)
            else:
                spreads[args[0]][args[1]]()


    k.small[0, 0] = jnp.zeros((16, DM), F32)
    clear = pltpu.make_async_copy(k.small.at[0, 0], k.small.at[1, 0], k.local.at[15])
    clear.start()
    clear.wait()

    for slot in range(2):
        pack = 1 if slot else 2 * y
        columns = lax.broadcasted_iota(jnp.int32, (8, SEQ), 1)
        rows = lax.broadcasted_iota(jnp.int32, (SEQ, 128), 0)
        pair_col, pair_row = jnp.zeros((8, SEQ), F32), jnp.zeros((SEQ, 128), F32)
        end = jnp.int32(0)
        for j in range(4):
            end = end + k.lens[pack, j]
            pair_col += jnp.where(columns >= end, 1.0, 0.0)
            pair_row += jnp.where(rows >= end, 1.0, 0.0)
        k.pair_col[slot] = pair_col
        k.pair_row[slot] = pair_row
    k.sq_rows[...] = jnp.zeros(k.sq_rows.shape, F32)

    k.bias[y, :, :] = jnp.zeros((8, DM), F32)
    for layer in range(LAYERS):
        k.bias[y, pl.ds(layer, 1), :] = k.upb_in[pl.ds(layer, 1), :]
        k.bias[y, pl.ds(2 + layer, 1), 0:192] = k.qvb_in[layer, 0:1, :]
        k.bias[y, pl.ds(2 + layer, 1), 384:576] = k.qvb_in[layer, 1:2, :]
    loads[0].wait()
    for layer in range(LAYERS):
        for j in range(3):
            k.w_qkv[layer, y, z, x, :, j * 192 : (j + 1) * 192] = k.stage_q[layer, j].astype(BF16)
    loads[3].wait()
    for layer in range(LAYERS):
        rows = k.sum1[1, pl.ds(layer * 24, 24), :]
        k.w_out[layer, y, z, x, :, 0:768] = rows[0:16].astype(BF16)
        k.w_out[layer, y, z, x, :, 768:1152] = jnp.concatenate([rows[16:24, 0:384], rows[16:24, 384:768]], axis=0).astype(BF16)
    loads[1].wait()
    loads[2].wait()
    for layer in range(LAYERS):
        k.w_up[layer, y, z, x] = k.sum1[0, pl.ds(layer * 96, 96), :].astype(BF16)
        k.w_down[layer, y, z, x] = k.sum1[0, pl.ds(192 + layer * 96, 96), :].astype(BF16)

    pl.semaphore_wait(barrier, len(plane_devs + line_devs))
    gather(0, 0, 0)
    for chunk in range(1, len(gathers)):
        gather(chunk, 1, 0)
    bias_move = moves.make(
        lambda: k.bias.at[pl.ds(y, 1)], lambda: k.bias.at[pl.ds(y, 1)], y_dev, lambda: k.bias.at[pl.ds(1 - y, 1)]
    )
    bias_move.start()

    for load in x_loads:
        load.wait()
    k.res[0:HALF, :] = k.x_buf[pl.ds(own_a, HALF), :].astype(F32)
    k.res[HALF:OWN, :] = k.x_buf[pl.ds(own_p, 128), :].astype(F32)
    bias_move.wait_recv()
    at("f0s")

    def gather_pair(buf, layer=None):
        at = lambda slot: (lambda: buf.at[pl.ds(slot, 1)])
        move = moves.make(at(c), at(c), core_dev, at(1 - c))
        move.start()
        return move

    def gather_chip(buf):
        found = []
        for mine, other, size in ((own_a, (1 - c) * HALF, HALF), (SEQ + 128 * c, SEQ + 128 * (1 - c), 128)):
            here = lambda mine=mine, size=size: buf.at[pl.ds(pl.multiple_of(mine, 128), size)]
            there = lambda other=other, size=size: buf.at[pl.ds(pl.multiple_of(other, 128), size)]
            found.append(moves.make(here, here, core_dev, there))
            found[-1].start()
        return found

    def gather_rows(buf):
        rows = lambda start, size: (lambda: buf.at[pl.ds(pl.multiple_of(start, 128), size)])
        other_p = SEQ + HALF * (1 - y) + 128 * c
        mine = rows(own_p, 128)
        far = lambda: k.x_far
        across = moves.make(mine, far, y_dev, far)
        across.start()
        first = moves.make(rows(own_a, HALF), rows(own_a, HALF), core_dev, rows((1 - c) * HALF, HALF))
        first.start()
        second = moves.make(mine, mine, core_dev, rows(SEQ + HALF * y + 128 * (1 - c), 128))
        second.start()

        def relay():
            across.wait_recv()
            buf[pl.ds(pl.multiple_of(other_p, 128), 128), :] = k.x_far[...]
            third = moves.make(far, rows(other_p, 128), core_dev, rows(SEQ + HALF * (1 - y) + 128 * (1 - c), 128))
            third.start()
            return third

        return across, first, second, relay

    def sum_pair(fill):
        def to_send(rows, cols, value):
            k.ex_s[rows, cols] = value.astype(BF16)

        def to_keep(rows, cols, value):
            k.cur[rows, cols] = value

        fill(1 - c, to_send)
        move = moves.make(
            lambda: k.ex_s.at[pl.ds(0, OWN)], lambda: k.ex_r.at[pl.ds(0, OWN)], core_dev, lambda: k.ex_r.at[pl.ds(0, OWN)]
        )
        move.start()
        fill(c, to_keep)

        def end():
            move.wait_recv()
            k.cur[...] += k.ex_r[0:OWN, :].astype(F32)
            moves.sent(move)

        return end

    def fill_rows(part_a, part_p):
        def fill(slot, store):
            store(slice(0, HALF), slice(0, DM), part_a(slot))
            store(slice(HALF, OWN), slice(0, DM), part_p(slot))

        return fill

    def send_away(part):
        k.ex_s[OWN:SEQ, :] = part(1 - c).astype(BF16)
        piece = lambda ref: (lambda: ref.at[pl.ds(OWN, 128)])
        beside = moves.make(piece(k.ex_s), piece(k.ex_r), core_dev, piece(k.ex_r))
        beside.start()
        k.ey_f[...] = part(c)
        across = moves.make(lambda: k.ey_s, lambda: k.ey_r, y_dev, lambda: k.ey_r)

        def go():
            beside.wait_recv()
            k.ey_s[...] = (k.ey_f[...] + k.ex_r[OWN:SEQ, :].astype(F32)).astype(BF16)
            across.start()

        def end():
            across.wait_recv()
            k.cur[HALF:OWN, :] += k.ey_r[...].astype(F32)
            moves.sent(beside, across)

        return go, end

    def spread(low, out, sems):
        piece = lambda ref, start, size: (lambda: ref.at[pl.ds(pl.multiple_of(start, 128), size)])
        other_a, other_p = (1 - y) * (2 * SEQ) + c * HALF, SEQ + HALF * (1 - y) + 128 * c
        copies, across, beside, relays = [], [], [], []
        for index, (start, size, mine, far) in enumerate(((0, HALF, in_a, other_a), (HALF, 128, own_p, other_p))):
            toward = (1 - 2 * c) * size
            own, there = piece(low, start, size), piece(out, mine, size)
            copies.append(
                lambda own=own, there=there, index=index: pltpu.make_async_copy(own(), there(), k.local.at[sems + index])
            )
            across.append(moves.make(own, there, y_dev, piece(out, far, size)))
            beside.append(moves.make(own, there, core_dev, piece(out, mine + toward, size)))
            far_rows = piece(out, far, size)
            relays.append(moves.make(far_rows, far_rows, core_dev, piece(out, far + toward, size)))

        def begin():
            for copy in copies:
                copy().start()
            for move in across + beside:
                move.start()

        def relay():
            for arrived, move in zip(across, relays):
                arrived.wait_recv()
                move.start()

        def end():
            for copy in copies:
                copy().wait()
            for move in beside + relays:
                move.wait_recv()

        return begin, relay, end

    def save(slot, src, dst):
        copy = pltpu.make_async_copy(src, dst, k.local.at[slot])
        copy.start()
        return copy

    def norm_grad(layer, e, xhat, scale, gain_row, bias_row, rows):
        h = e * k.vec[gain_row, layer : layer + 1, :]
        mean_h = jnp.mean(h, axis=-1, keepdims=True)
        mean_hx = jnp.mean(h * xhat, axis=-1, keepdims=True)
        grad = scale * (h - mean_h - xhat * mean_hx)
        k.res[rows, :] = grad
        acc = k.small.at[layer, 0]
        acc[gain_row : gain_row + 1, :] += jnp.sum(e * xhat, axis=0, keepdims=True)
        acc[gain_row + 1 : gain_row + 2, :] += jnp.sum(e, axis=0, keepdims=True)
        acc[bias_row : bias_row + 1, :] += jnp.sum(grad, axis=0, keepdims=True)

    row_tiles = OWN // 128
    saves = []
    for layer in range(LAYERS):
        if layer == 1:
            k.x_buf[pl.ds(own_a, HALF), :] = k.res[0:HALF, :].astype(BF16)
            k.x_buf[pl.ds(own_p, 128), :] = k.res[HALF:OWN, :].astype(BF16)
            _, first, second, relay = gather_rows(k.x_buf)
            at("f1s")
        place = "f" + str(layer)
        at("need" + str(3 * layer))
        if layer == 1:
            for move in (first, second):
                move.wait_recv()

        for group in range(2):
            for zi in range(LINE):
                for xi in range(2):
                    block = k.w_out[layer, group, zi, xi].astype(F32)
                    low = (zi * 2 + xi) * 24
                    k.unpack[low : low + 16, :] = block[:, 0:768]
                    k.unpack[low + 16 : low + 24, 0:384] = block[0:8, 768:1152]
                    k.unpack[low + 16 : low + 24, 384:768] = block[8:16, 768:1152]
            k.w_o[layer, group] = k.unpack[...].astype(BF16)

        shrink = jnp.where(lax.broadcasted_iota(jnp.int32, (1, 576), 1) < 192, HD ** (-0.5), 1.0)

        def project(group, start):
            rows = pl.ds(pl.multiple_of(start, HALF), HALF)
            made = dot(k.x_buf[rows, :], flat(k.w_qkv[layer, group]))
            made = (made + k.bias[group, 2 + layer : 3 + layer, 0:576]) * shrink
            k.qkv[layer, group, rows, :] = made.astype(BF16)

        def attend(group, tile, key_start, pair_start):
            slot = key_start // SEQ
            rows = pl.ds(pl.multiple_of(tile * HALF, HALF), HALF)
            from_rows = pl.ds(pl.multiple_of(key_start + pair_start, HALF), HALF)
            keys = pl.ds(key_start, SEQ)
            allowed = k.pair_row[slot, pl.ds(pl.multiple_of(pair_start, HALF), HALF), 0:1] == k.pair_col[slot, 0:1, :]
            for head in range(3):
                low, high = head * HD, (head + 1) * HD
                queries = k.qkv[layer, group, from_rows, low:high]
                key_rows = k.qkv[layer, group, keys, 192 + low : 192 + high]
                values = k.qkv[layer, group, keys, 384 + low : 384 + high]
                scores = jnp.where(allowed, dot_nt(queries, key_rows), -1e30)
                raised = jnp.exp(scores - jnp.max(scores, axis=-1, keepdims=True))
                probs = (raised * (1.0 / jnp.sum(raised, axis=-1, keepdims=True))).astype(BF16)
                k.probs[group, head, rows, :] = probs
                k.merged[layer, group, rows, low:high] = dot(probs, values).astype(BF16)

        if layer == 0:
            pl.loop(0, 8)(lambda i: project(i // 4, (i % 4) * HALF))
        else:
            pl.loop(0, 6)(lambda i: project(i // 3, jnp.where(i % 3 == 2, SEQ + HALF * y, (i % 3) * HALF)))
            saves[0].wait()
        at(place + "q")

        @pl.loop(0, 4)
        def _(i):
            attend(i // 2, i % 2, 0, (i % 2) * HALF)
            for turn in range(4):
                pl.when(i == turn)(lambda: at(place + "a" + str(turn)))

        if layer == 1:
            relay().wait_recv()
            pl.loop(0, 2)(lambda group: project(group, SEQ + HALF * (1 - y)))
        pl.loop(0, 2)(lambda group: attend(group, 2, SEQ, HALF * y))
        at(place + "p")
        if layer == 0:
            saves.append(save(8, k.probs, k.probs_hbm))

        def out_rows(start, size):
            rows = pl.ds(pl.multiple_of(start, 128), size)
            return dot(k.merged[layer, 0, rows, :], k.w_o[layer, 0]) + dot(k.merged[layer, 1, rows, :], k.w_o[layer, 1])

        end_out = sum_pair(
            fill_rows(lambda slot: out_rows(slot * HALF, HALF), lambda slot: out_rows(SEQ + 128 * slot, 128))
        )

        def first_norm(i):
            rows = pl.ds(pl.multiple_of(i * 128, 128), 128)
            total = k.res[rows, :] + k.cur[rows, :] + k.vec[4, layer : layer + 1, :]
            k.sum1[layer, rows, :] = total
            normed = norm_stats(total)[0] * k.vec[0, layer : layer + 1, :] + k.vec[1, layer : layer + 1, :]
            k.res[rows, :] = normed
            k.nlow[layer, c, rows, :] = normed.astype(BF16)

        at(place + "o")
        end_out()
        pl.loop(0, row_tiles)(first_norm)

        mate_rows = gather_pair(k.nlow.at[layer])
        at(place + "n")
        at("need" + str(3 * layer + 1))
        if layer == 1:
            saves[1].wait()
            saves[2].wait()
        for order in range(2):
            slot = c if order == 0 else 1 - c
            if order:
                mate_rows.wait_recv()

            @pl.loop(0, 6)
            def _(i):
                group, cols = i // 3, pl.ds(pl.multiple_of((i % 3) * 256, 256), 256)
                made = dot(k.nlow[layer, slot], flat(k.w_up[layer, group, :, :, :, cols]))
                made = made + k.bias[group, layer : layer + 1, cols]
                act, slope = gelu_and_slope(made)
                k.act[group, slot, :, cols] = act.astype(BF16)
                k.slope[group, slot, :, cols] = slope.astype(BF16)
                pl.when(i == 2)(lambda: at(place + "xw"[order]))

            at(place + "uv"[order])

        if layer == 0:
            saves.append(save(9, k.act, k.act_hbm))
            saves.append(save(10, k.slope, k.slope_hbm))
        at("need" + str(3 * layer + 2))

        def down_rows(slot, store):
            @pl.loop(0, 3)
            def _(i):
                cols = pl.ds(pl.multiple_of(i * 256, 256), 256)
                made = dot(k.act[0, slot], flat(k.w_down[layer, 0, :, :, :, cols]))
                store(slice(0, OWN), cols, made + dot(k.act[1, slot], flat(k.w_down[layer, 1, :, :, :, cols])))

        end_down = sum_pair(down_rows)
        at(place + "d")
        if layer == 1:
            for load in e_loads:
                load.wait()
        end_down()

        @pl.loop(0, row_tiles)
        def _(i):
            rows = pl.ds(pl.multiple_of(i * 128, 128), 128)
            total = k.res[rows, :] + k.cur[rows, :] + k.vec[5, layer : layer + 1, :]
            xhat, scale = norm_stats(total)
            result = xhat * k.vec[2, layer : layer + 1, :] + k.vec[3, layer : layer + 1, :]
            if layer == 0:
                k.sum2[rows, :] = total
                k.res[rows, :] = result
            else:
                k.a_low[rows, :] = result.astype(BF16)
                norm_grad(layer, k.e_low[rows, :].astype(F32), xhat, scale, 2, 5, rows)
                k.lsec[c, rows, :] = k.res[rows, :].astype(BF16)

    mate_rows = gather_pair(k.lsec)
    moves.drain_but(mate_rows)
    spreads[0] = spread(k.a_low, k.activations, 11)

    for layer in (1, 0):
        place = "b" + str(layer)
        if layer == 0:

            @pl.loop(0, row_tiles)
            def _(i):
                rows = pl.ds(pl.multiple_of(i * 128, 128), 128)
                xhat, scale = norm_stats(k.sum2[rows, :])
                norm_grad(layer, k.res[rows, :] + k.cur[rows, :], xhat, scale, 2, 5, rows)
                k.lsec[c, rows, :] = k.res[rows, :].astype(BF16)

            mate_rows = gather_pair(k.lsec)
            restore_act.wait()
            restore_slope.wait()
        at(place + "s")
        for order in range(2):
            slot = c if order == 0 else 1 - c
            if order:
                mate_rows.wait_recv()
                moves.sent(mate_rows)

            @pl.loop(0, 4)
            def _(i):
                group, tile = i // 2, i % 2
                cols = pl.ds(pl.multiple_of(tile * OWN, OWN), OWN)
                back = dot_nt(k.lsec[slot], flat(k.w_down[layer, group, pl.ds(tile * 2, 2)]))
                grad = (back * k.slope[group, slot, :, cols].astype(F32)).astype(BF16)
                k.slope[group, slot, :, cols] = grad
                k.small[layer, 0, pl.ds(6 + group, 1), cols] += jnp.sum(grad.astype(F32), axis=0, keepdims=True)

            at(place + "gh"[order])

        @pl.loop(0, 4)
        def _(i):
            group, tile = i // 2, i % 2
            cols = pl.ds(pl.multiple_of(tile * OWN, OWN), OWN)
            made = dot_tn(flat(k.act[group, :, :, cols]), flat(k.lsec[...]))
            k.w_down[layer, group, pl.ds(tile * 2, 2)] = made.astype(BF16).reshape((2, 2, 96, 768))

        at(place + "w")
        scatter(DOWN, layer, 0)
        if layer == 1:
            restore_act = save(9, k.act_hbm, k.act)

        def normed_rows(slot, store):
            @pl.loop(0, 2)
            def _(tile):
                cols = pl.ds(pl.multiple_of(tile * OWN, OWN), OWN)
                made = dot_nt(k.slope[0, slot], flat(k.w_up[layer, 0, pl.ds(tile * 2, 2)]))
                store(slice(0, OWN), cols, made + dot_nt(k.slope[1, slot], flat(k.w_up[layer, 1, pl.ds(tile * 2, 2)])))

        end_normed = sum_pair(normed_rows)
        at(place + "n")
        end_normed()

        @pl.loop(0, row_tiles)
        def _(i):
            rows = pl.ds(pl.multiple_of(i * 128, 128), 128)
            xhat, scale = norm_stats(k.sum1[layer, rows, :])
            norm_grad(layer, k.res[rows, :] + k.cur[rows, :], xhat, scale, 0, 4, rows)
            start = jnp.where(i == 2, SEQ + 128 * c, own_a + i * 128)
            k.lfirst[pl.ds(pl.multiple_of(start, 128), 128), :] = k.res[rows, :].astype(BF16)

        mate_firsts = gather_chip(k.lfirst)
        at(place + "f")

        @pl.loop(0, 4)
        def _(i):
            group, tile = i // 2, i % 2
            cols = pl.ds(pl.multiple_of(tile * OWN, OWN), OWN)
            made = dot_tn(flat(k.nlow[layer, :, :, cols]), flat(k.slope[group]))
            k.w_up[layer, group, pl.ds(tile * 2, 2)] = made.astype(BF16).reshape((2, 2, 96, 768))

        at(place + "u")
        scatter(UP, layer, 0)
        if layer == 1:
            restore_slope = save(10, k.slope_hbm, k.slope)
        for move in mate_firsts:
            move.wait_recv()
        moves.sent(*mate_firsts)

        @pl.loop(0, 6)
        def _(i):
            group, rows = i // 3, pl.ds(pl.multiple_of((i % 3) * HALF, HALF), HALF)
            k.dmerged[group, rows, :] = dot_nt(k.lfirst[rows, :], k.w_o[layer, group]).astype(BF16)

        for group in range(2):
            made = dot_tn(k.merged[layer, group], k.lfirst[...])
            for zi in range(LINE):
                for xi in range(2):
                    rows = made[(zi * 2 + xi) * 24 : (zi * 2 + xi + 1) * 24]
                    k.w_out[layer, group, zi, xi, :, 0:768] = rows[0:16].astype(BF16)
                    k.w_out[layer, group, zi, xi, :, 768:1152] = jnp.concatenate(
                        [rows[16:24, 0:384], rows[16:24, 384:768]], axis=0
                    ).astype(BF16)

        at(place + "m")
        scatter(OUT, layer, 0)
        if layer == 0:
            restore_probs.wait()

        def attend_back(group, key_start, tiles):
            keys = pl.ds(key_start, SEQ)
            for head in range(3):
                low, high = head * HD, (head + 1) * HD
                key_rows = k.qkv[layer, group, keys, 192 + low : 192 + high]
                values = k.qkv[layer, group, keys, 384 + low : 384 + high]
                grad_keys = jnp.zeros((HD, SEQ), F32)
                grad_values = jnp.zeros((HD, SEQ), F32)
                for start, from_start in tiles:
                    rows, from_rows = pl.ds(start, HALF), pl.ds(pl.multiple_of(from_start, HALF), HALF)
                    queries = k.qkv[layer, group, from_rows, low:high]
                    grad_out = k.dmerged[group, rows, low:high]
                    probs = k.probs[group, head, rows, :]
                    row_dot = jnp.sum(
                        grad_out.astype(F32) * k.merged[layer, group, rows, low:high].astype(F32), axis=-1, keepdims=True
                    )
                    grad_probs = dot_nt(grad_out, values)
                    grad_scores = (probs.astype(F32) * (grad_probs - row_dot)).astype(BF16)
                    grad_values += dot(grad_out.astype(F32).T.astype(BF16), probs)
                    grad_keys += dot(queries.astype(F32).T.astype(BF16), grad_scores)
                    grad_queries = (dot(grad_scores, key_rows) * HD ** (-0.5)).astype(BF16)
                    k.qkv[layer, group, from_rows, low:high] = grad_queries
                k.qkv[layer, group, keys, 192 + low : 192 + high] = grad_keys.T.astype(BF16)
                k.qkv[layer, group, keys, 384 + low : 384 + high] = grad_values.T.astype(BF16)

        def stream_rows(start, size):
            rows = pl.ds(pl.multiple_of(start, 128), size)
            made = dot_nt(k.qkv[layer, 0, rows, :], flat(k.w_qkv[layer, 0]))
            return made + dot_nt(k.qkv[layer, 1, rows, :], flat(k.w_qkv[layer, 1]))

        @pl.loop(0, 2)
        def _(group):
            attend_back(group, SEQ, ((SEQ, SEQ + HALF * y),))
            other = pl.ds(pl.multiple_of(SEQ + HALF * (1 - y), HALF), HALF)
            k.qkv[layer, group, other, 0:192] = jnp.zeros((HALF, 192), BF16)

        away_go, away_end = send_away(lambda slot: stream_rows(SEQ + HALF * (1 - y) + 128 * slot, 128))
        at(place + "p")

        @pl.loop(0, 2)
        def _(group):
            attend_back(group, 0, ((0, 0), (HALF, HALF)))
            for j, row in ((0, 8), (2, 9)):
                sums = jnp.sum(k.qkv[layer, group, :, j * 192 : (j + 1) * 192].astype(F32), axis=0, keepdims=True)
                k.small[layer, 0, pl.ds(row + 2 * group, 1), 0:192] += sums

            @pl.when(group == 0)
            def _():
                away_go()
                at(place + "a")

            pl.when(group == 1)(lambda: at(place + "b"))

        small_step(layer, 0)
        if layer == 1:
            restore_probs = save(8, k.probs_hbm, k.probs)

        end_stream = sum_pair(
            fill_rows(
                lambda slot: stream_rows(slot * HALF, HALF), lambda slot: stream_rows(SEQ + HALF * y + 128 * slot, 128)
            )
        )
        at(place + "t")
        if layer == 0:
            for load in x_load_again:
                load.wait()

        @pl.loop(0, 4)
        def _(i):
            group, tile = i // 2, i % 2
            cols = pl.ds(pl.multiple_of(tile * OWN, OWN), OWN)
            made = dot_tn(k.x_buf[:, cols], k.qkv[layer, group])
            k.w_qkv[layer, group, pl.ds(tile * 2, 2)] = made.astype(BF16).reshape((2, 2, 96, 576))

        at(place + "q")
        scatter(QKV, layer, 0)
        if layer == 1:
            x_load_again = [
                pltpu.make_async_copy(k.x_in.at[pl.ds(pack_row, SEQ)], k.x_buf.at[pl.ds(0, SEQ)], k.local.at[4]),
                pltpu.make_async_copy(k.x_in.at[pl.ds(SEQ, SEQ)], k.x_buf.at[pl.ds(SEQ, SEQ)], k.local.at[5]),
            ]
            for load in x_load_again:
                load.start()
        end_stream()
        away_end()

    k.e_low[...] = (k.res[...] + k.cur[...]).astype(BF16)
    spreads[1] = spread(k.e_low, k.input_grad, 13)
    at("end")
    for layer in range(LAYERS):
        total = k.small.at[layer, 3]
        for row, source, share in [(row, row, LINE * 8) for row in range(6)] + [
            (6, 6 + y, LINE * 2),
            (7, 8 + 2 * y, LINE * 2),
            (8, 9 + 2 * y, LINE * 2),
        ]:
            values = total[pl.ds(source, 1), :]
            k.sq_rows[0:1, 0:DM] += values * values * (1.0 / share)
            if row < 6:
                k.vec_out[row, layer : layer + 1, :] = values
            elif row == 6:
                k.upb_out[layer : layer + 1, :] = values
            else:
                k.qvb_out[layer, row - 7 : row - 6, :] = values[:, 0:192]
    squares = jnp.sum(k.sq_rows[...], axis=0, keepdims=True)
    k.sq[0] = jnp.broadcast_to(jnp.sum(squares, axis=1, keepdims=True), (8, 128))
    for step, (devices, landing) in enumerate(((plane_devs, k.sq_plane), (line_devs, k.sq_line))):
        sent = []
        for index, device in enumerate(devices):
            lands = lambda index=index: landing.at[index]
            sent.append(moves.make(lambda: k.sq.at[step], lands, device, lands))
            sent[-1].start()
        total = k.sq[step]
        for index, move in enumerate(sent):
            move.wait_recv()
            total = total + landing[index]
        k.sq[step + 1] = total
    k.squares[...] = k.sq[2]
    moves.drain()


def kernel_call(inputs, out_grad, lens, w_q, w_o, w_u, w_d, vec, qvb, upb):
    any_ = pl.BlockSpec(memory_space=pl.ANY)
    vmem = pl.BlockSpec(memory_space=pltpu.VMEM)
    smem = pl.BlockSpec(memory_space=pltpu.SMEM)
    ins = dict(
        x_in=(inputs, any_),
        e_in=(out_grad, any_),
        lens=(lens, smem),
        wq_in=(w_q, any_),
        wo_in=(w_o.reshape(LAYERS * 24, DM), any_),
        wu_in=(w_u.reshape(LAYERS * 96, DM), any_),
        wd_in=(w_d.reshape(LAYERS * 96, DM), any_),
        vec=(vec, vmem),
        qvb_in=(qvb, vmem),
        upb_in=(upb, vmem),
    )
    outs = dict(
        activations=((3 * SEQ, DM), BF16, any_),
        input_grad=((3 * SEQ, DM), BF16, any_),
        g_qkv=((LAYERS, 3, 96, 192), F32, vmem),
        g_out=((LAYERS, 24, DM), F32, vmem),
        g_up=((LAYERS, 96, DM), F32, vmem),
        g_down=((LAYERS, 96, DM), F32, vmem),
        vec_out=((6, LAYERS, DM), F32, vmem),
        qvb_out=((LAYERS, 2, 192), F32, vmem),
        upb_out=((LAYERS, DM), F32, vmem),
        squares=((8, 128), F32, vmem),
        probs_hbm=((2, 3, 2 * OWN, SEQ), BF16, any_),
        act_hbm=((2, 2, OWN, DM), BF16, any_),
        slope_hbm=((2, 2, OWN, DM), BF16, any_),
    )
    scratch = dict(
        w_qkv=((LAYERS, 2, LINE, 2, 96, 576), BF16),
        w_out=((LAYERS, 2, LINE, 2, 16, 1152), BF16),
        w_up=((LAYERS, 2, LINE, 2, 96, 768), BF16),
        w_down=((LAYERS, 2, LINE, 2, 96, 768), BF16),
        w_o=((LAYERS, 2, 192, DM), BF16),
        unpack=((192, DM), F32),
        stage_q=((LAYERS, 3, 96, 192), F32),
        x_buf=((2 * SEQ, DM), BF16),
        qkv=((LAYERS, 2, 2 * SEQ, 576), BF16),
        probs=((2, 3, 2 * OWN, SEQ), BF16),
        merged=((LAYERS, 2, 2 * OWN, 192), BF16),
        sum1=((LAYERS, OWN, DM), F32),
        sum2=((OWN, DM), F32),
        nlow=((LAYERS, 2, OWN, DM), BF16),
        act=((2, 2, OWN, DM), BF16),
        slope=((2, 2, OWN, DM), BF16),
        res=((OWN, DM), F32),
        cur=((OWN, DM), F32),
        a_low=((OWN, DM), BF16),
        e_low=((OWN, DM), BF16),
        lsec=((2, OWN, DM), BF16),
        lfirst=((2 * OWN, DM), BF16),
        dmerged=((2, 2 * OWN, 192), BF16),
        ex_s=((SEQ, DM), BF16),
        ex_r=((SEQ, DM), BF16),
        x_far=((128, DM), BF16),
        ey_s=((128, DM), BF16),
        ey_r=((128, DM), BF16),
        ey_f=((128, DM), F32),
        bias=((2, 8, DM), F32),
        pair_col=((2, 8, SEQ), F32),
        pair_row=((2, SEQ, 128), F32),
        small=((LAYERS, 4, 16, DM), F32),
        small_in=((LAYERS, 7, 16, DM), F32),
        sq_rows=((8, 1152), F32),
        sq=((3, 8, 128), F32),
        sq_plane=((7, 8, 128), F32),
        sq_line=((LINE - 1, 8, 128), F32),
    )
    landings = {}
    for kind in KINDS:
        axis, first, second = CUTS[1][kind]

        def cut(size):
            shape = list(BLOCK[kind])
            shape[axis] = size
            return tuple(shape)

        p_1, p_2 = cut(first), cut(second - first)
        p_12, p_3 = cut(second), cut(BLOCK[kind][axis] - second)
        landings[kind] = dict(
            ry1=(1, LINE, 2) + p_1,
            rx1=(1, LINE, 1) + p_1,
            rx2=(2, LINE, 1) + p_2,
            ry2=(1, LINE, 1) + p_2,
            rz=(2, 3, 1, 1, 1) + p_12,
            rz3=(2, 3, 2, 1, 2) + p_3,
            ry3=(1, 1, 2) + p_3,
            rx3=(1, 1, 1) + p_3,
        )
    scratch.update({name + kind: (shape, BF16) for kind in KINDS for name, shape in landings[kind].items()})
    names = [*ins, *outs, *scratch, "send", "recv", "local"]
    made = pl.pallas_call(
        lambda *refs: fused(names, *refs),
        out_shape=[jax.ShapeDtypeStruct(shape, dtype) for shape, dtype, _ in outs.values()],
        in_specs=[spec for _, spec in ins.values()],
        out_specs=[spec for *_, spec in outs.values()],
        scratch_shapes=[pltpu.VMEM(shape, dtype) for shape, dtype in scratch.values()]
        + [
            pltpu.SemaphoreType.DMA((SEMS,)),
            pltpu.SemaphoreType.DMA((SEMS,)),
            pltpu.SemaphoreType.DMA((16,)),
        ],
        compiler_params=pltpu.CompilerParams(
            collective_id=0, has_side_effects=True, vmem_limit_bytes=VMEM_BYTES
        ),
        name="encoder_step",
    )(*[value for value, _ in ins.values()])
    return types.SimpleNamespace(**dict(zip(outs, made)))


VMEM_BYTES = 64 * 2**20 - 2**17
UPDATE_VMEM_BYTES = VMEM_BYTES


def update_kernel(names, *refs):
    k = types.SimpleNamespace(**dict(zip(names, refs)))
    norm = jnp.sqrt(k.squares[0:1, 0:1])
    factor = jnp.minimum(1.0, CLIP_LIMIT / norm)

    def update(name, rate, decay):
        made = adamw(*[vars(k)[part + name][...] for part in "wmvg"], factor, rate, decay)
        for part, value in zip("wmv", made):
            vars(k)["new" + part + name][...] = value

    for name in KINDS:
        update(name, LEARN_RATE, WEIGHT_DECAY)

    @pl.when(pl.program_id(0) == 0)
    def _():
        for name in ("vec", "qvb", "upb"):
            update(name, VECTOR_RATE, 0.0)
        k.norm[...] = norm

    k.new_input_grad[...] = k.input_grad[...].astype(F32)
    k.new_activations[...] = k.activations[...]


def update_call(weights, squares, activations, input_grad):
    blocks = dict(
        qkv=pl.BlockSpec((1, 3, 96, 192), lambda i: (i, 0, 0, 0)),
        out=pl.BlockSpec((1, 24, DM), lambda i: (i, 0, 0)),
        up=pl.BlockSpec((1, 96, DM), lambda i: (i, 0, 0)),
        down=pl.BlockSpec((1, 96, DM), lambda i: (i, 0, 0)),
        vec=pl.BlockSpec((6, LAYERS, DM), lambda i: (0, 0, 0)),
        qvb=pl.BlockSpec((LAYERS, 2, 192), lambda i: (0, 0, 0)),
        upb=pl.BlockSpec((LAYERS, DM), lambda i: (0, 0)),
    )
    whole = pl.BlockSpec((8, 128), lambda i: (0, 0))
    rows = pl.BlockSpec((2 * OWN, DM), lambda i: (i, 0))
    ins = dict(squares=(squares, whole), activations=(activations, rows), input_grad=(input_grad, rows))
    outs = dict(
        norm=(jax.ShapeDtypeStruct((1, 1), F32), F32, pl.BlockSpec((1, 1), lambda i: (0, 0))), new_activations=(activations, BF16, rows), new_input_grad=(input_grad, F32, rows)
    )
    for name, arrays in weights.items():
        for part, value in zip("wmvg", arrays):
            ins[part + name] = (value, blocks[name])
            if part != "g":
                outs["new" + part + name] = (value, F32, blocks[name])
    names = [*ins, *outs]
    made = pl.pallas_call(
        lambda *refs: update_kernel(names, *refs),
        grid=(LAYERS,),
        out_shape=[jax.ShapeDtypeStruct(like.shape, dtype) for like, dtype, _ in outs.values()],
        in_specs=[spec for _, spec in ins.values()],
        out_specs=[spec for *_, spec in outs.values()],
        compiler_params=pltpu.CompilerParams(vmem_limit_bytes=UPDATE_VMEM_BYTES),
        name="update",
    )(*[value for value, _ in ins.values()])
    return types.SimpleNamespace(**dict(zip(outs, made)))


def kernel_body(
    inputs,
    pair_lengths,
    out_grad,
    w_qkv,
    m_qkv,
    v_qkv,
    w_out,
    m_out,
    v_out,
    w_up,
    m_up,
    v_up,
    w_down,
    m_down,
    v_down,
    vectors,
    m_vectors,
    v_vectors,
    qv_bias,
    m_qv_bias,
    v_qv_bias,
    up_bias,
    m_up_bias,
    v_up_bias,
):
    turn = lambda v: jnp.transpose(v, (0, 2, 1, 3))
    swap = lambda v: jnp.transpose(v, (1, 0, 2))
    w_qkv, m_qkv, v_qkv = turn(w_qkv), turn(m_qkv), turn(v_qkv)
    vectors, m_vectors, v_vectors = swap(vectors), swap(m_vectors), swap(v_vectors)
    made = kernel_call(inputs, out_grad, pair_lengths, w_qkv, w_out, w_up, w_down, vectors, qv_bias, up_bias)
    weights = dict(
        qkv=(w_qkv, m_qkv, v_qkv, made.g_qkv),
        out=(w_out, m_out, v_out, made.g_out),
        up=(w_up, m_up, v_up, made.g_up),
        down=(w_down, m_down, v_down, made.g_down),
        vec=(vectors, m_vectors, v_vectors, made.vec_out),
        qvb=(qv_bias, m_qv_bias, v_qv_bias, made.qvb_out),
        upb=(up_bias, m_up_bias, v_up_bias, made.upb_out),
    )
    new = update_call(weights, made.squares, made.activations, made.input_grad)
    parts = lambda name: [vars(new)["new" + part + name] for part in "wmv"]
    return (
        new.new_activations,
        new.new_input_grad,
        new.norm.reshape(()),
        *[turn(v) for v in parts(QKV)],
        *parts(OUT),
        *parts(UP),
        *parts(DOWN),
        *[swap(v) for v in parts("vec")],
        *parts("qvb"),
        *parts("upb"),
    )


def solution(mesh):
    rows, matrix = P("dp", None), P(None, ("tensor", "dp"), None)
    qkv, up = P(None, "dp", None, "tensor"), P(None, "dp", "tensor")
    heads, hidden = P(None, None, "tensor"), P(None, "tensor")
    weights = (qkv,) * 3 + (matrix,) * 3 + (up,) * 3 + (matrix,) * 3
    smalls = (P(),) * 3 + (heads,) * 3 + (hidden,) * 3
    fits = mesh.shape["dp"] == 2 * LINE and mesh.shape["tensor"] == 4
    return jax.shard_map(
        kernel_body if fits else body,
        mesh=mesh,
        in_specs=(rows, rows, rows) + weights + smalls,
        out_specs=(rows, rows, P()) + weights + smalls,
        check_vma=False,
    )
```

```python
import math
import types

import jax
import jax.numpy as jnp
from jax import lax
from jax.experimental import pallas as pl
from jax.experimental.pallas import tpu as pltpu
from jax.sharding import PartitionSpec as P

HD = 64
SEQ = 512
LAYERS = 2
STEP = 10


NORM_EPS = 1e-05
CLIP_LIMIT = 0.05
BETA_ONE = 0.9
BETA_TWO = 0.999
LEARN_RATE = 0.1
VECTOR_RATE = 1.0
WEIGHT_DECAY = 0.01
ADAM_EPS = 1e-08


def layer_norm(rows_in, gain, shift):
    center = rows_in - jnp.mean(rows_in, axis=-1, keepdims=True)
    spread = jnp.mean(center * center, axis=-1, keepdims=True)
    return center * lax.rsqrt(spread + NORM_EPS) * gain + shift


def gelu_exact(pre_values):
    return jax.nn.gelu(pre_values, approximate=False)


def pair_mask(lengths):
    ends = jnp.cumsum(lengths)
    positions = jnp.arange(SEQ, dtype=jnp.int32)
    pair_of = jnp.sum((positions[:, None] >= ends[None, :]).astype(jnp.int32), axis=1)
    return pair_of[:, None] == pair_of[None, :]


def pack_scores(queries, key_rows, masks):
    scores = jnp.einsum(
        "pqhe,pkhe->phqk", queries, key_rows, preferred_element_type=jnp.float32
    ) * HD ** (-0.5)
    return jnp.where(masks[:, None], scores, -1e30)


def attend(queries, key_rows, values, masks):
    scores = pack_scores(queries, key_rows, masks)
    top = jnp.max(scores, axis=-1, keepdims=True)
    weights = jnp.exp(scores - top)
    total = jnp.sum(weights, axis=-1, keepdims=True)
    probs = weights / total
    attended = jnp.einsum(
        "phqk,pkhe->pqhe", probs.astype(jnp.bfloat16), values, preferred_element_type=jnp.float32
    )
    return (attended, top + jnp.log(total))


def attend_back(queries, key_rows, values, grad_attended, log_total, masks):
    scores = pack_scores(queries, key_rows, masks)
    probs = jnp.exp(scores - log_total)
    grad_values = jnp.einsum(
        "phqk,pqhe->pkhe",
        probs.astype(jnp.bfloat16),
        grad_attended,
        preferred_element_type=jnp.float32,
    )
    grad_probs = jnp.einsum(
        "pqhe,pkhe->phqk", grad_attended, values, preferred_element_type=jnp.float32
    )
    row_dot = jnp.sum(grad_probs * probs, axis=-1, keepdims=True)
    grad_scores = (probs * (grad_probs - row_dot)).astype(jnp.bfloat16)
    grad_queries = jnp.einsum(
        "phqk,pkhe->pqhe", grad_scores, key_rows, preferred_element_type=jnp.float32
    ) * HD ** (-0.5)
    grad_keys = jnp.einsum(
        "phqk,pqhe->pkhe", grad_scores, queries, preferred_element_type=jnp.float32
    ) * HD ** (-0.5)
    return (
        grad_queries.astype(jnp.bfloat16),
        grad_keys.astype(jnp.bfloat16),
        grad_values.astype(jnp.bfloat16),
    )


def layer_forward(stream, qkv_w, out_w, up_w, down_w, vector_rows, qv_rows, up_row, masks):
    row_count = stream.shape[0]
    pack_count = masks.shape[0]
    width = out_w.shape[0]
    group_heads = width // HD
    stream_low = stream.astype(jnp.bfloat16)
    project = jnp.einsum("td,dcn->tcn", stream_low, qkv_w, preferred_element_type=jnp.float32)
    queries = (
        (project[:, 0] + qv_rows[0]).astype(jnp.bfloat16).reshape(pack_count, SEQ, group_heads, HD)
    )
    key_rows = project[:, 1].astype(jnp.bfloat16).reshape(pack_count, SEQ, group_heads, HD)
    values = (
        (project[:, 2] + qv_rows[1]).astype(jnp.bfloat16).reshape(pack_count, SEQ, group_heads, HD)
    )
    attended, log_total = attend(queries, key_rows, values, masks)
    merged = attended.reshape(row_count, width).astype(jnp.bfloat16)
    attn_part = jnp.dot(merged, out_w, preferred_element_type=jnp.float32)
    attn_summed = lax.psum(attn_part.astype(jnp.bfloat16), "tensor").astype(jnp.float32)
    first_sum = stream + attn_summed + vector_rows[4]
    normed = layer_norm(first_sum, vector_rows[0], vector_rows[1])
    normed_low = normed.astype(jnp.bfloat16)
    hidden_pre = jnp.dot(normed_low, up_w, preferred_element_type=jnp.float32) + up_row
    hidden_act = gelu_exact(hidden_pre).astype(jnp.bfloat16)
    ffn_part = jnp.dot(hidden_act, down_w, preferred_element_type=jnp.float32)
    ffn_summed = lax.psum(ffn_part.astype(jnp.bfloat16), "tensor").astype(jnp.float32)
    second_sum = normed + ffn_summed + vector_rows[5]
    result = layer_norm(second_sum, vector_rows[2], vector_rows[3])
    kept = (
        stream_low,
        queries,
        key_rows,
        values,
        log_total,
        merged,
        first_sum,
        normed_low,
        hidden_pre,
        hidden_act,
        second_sum,
    )
    return (result, kept)


def layer_backward(grad_out, kept, qkv_w, out_w, up_w, down_w, vector_rows, masks):
    (
        stream_low,
        queries,
        key_rows,
        values,
        log_total,
        merged,
        first_sum,
        normed_low,
        hidden_pre,
        hidden_act,
        second_sum,
    ) = kept
    row_count = stream_low.shape[0]
    width = out_w.shape[0]
    _, pull_second = jax.vjp(layer_norm, second_sum, vector_rows[2], vector_rows[3])
    grad_second, grad_gain_two, grad_shift_two = pull_second(grad_out)
    grad_down_bias = jnp.sum(grad_second, axis=0)
    low_second = grad_second.astype(jnp.bfloat16)
    grad_down = jnp.einsum("tf,td->fd", hidden_act, low_second, preferred_element_type=jnp.float32)
    grad_act = jnp.einsum("td,fd->tf", low_second, down_w, preferred_element_type=jnp.float32)
    _, pull_gelu = jax.vjp(gelu_exact, hidden_pre)
    grad_pre = pull_gelu(grad_act)[0].astype(jnp.bfloat16)
    grad_up_bias = jnp.sum(grad_pre.astype(jnp.float32), axis=0)
    grad_up = jnp.einsum("td,tf->df", normed_low, grad_pre, preferred_element_type=jnp.float32)
    back_normed = jnp.einsum("tf,df->td", grad_pre, up_w, preferred_element_type=jnp.float32)
    grad_normed = grad_second + lax.psum(back_normed.astype(jnp.bfloat16), "tensor").astype(
        jnp.float32
    )
    _, pull_first = jax.vjp(layer_norm, first_sum, vector_rows[0], vector_rows[1])
    grad_first, grad_gain_one, grad_shift_one = pull_first(grad_normed)
    grad_out_bias = jnp.sum(grad_first, axis=0)
    low_first = grad_first.astype(jnp.bfloat16)
    grad_outw = jnp.einsum("tn,td->nd", merged, low_first, preferred_element_type=jnp.float32)
    grad_merged = jnp.einsum(
        "td,nd->tn", low_first, out_w, preferred_element_type=jnp.float32
    ).astype(jnp.bfloat16)
    grad_queries, grad_keys, grad_values = attend_back(
        queries, key_rows, values, grad_merged.reshape(queries.shape), log_total, masks
    )
    grad_project = jnp.stack(
        (
            grad_queries.reshape(row_count, width),
            grad_keys.reshape(row_count, width),
            grad_values.reshape(row_count, width),
        ),
        axis=1,
    )
    grad_qv_bias = jnp.sum(grad_project[:, 0::2].astype(jnp.float32), axis=0)
    grad_qkv = jnp.einsum(
        "td,tcn->dcn", stream_low, grad_project, preferred_element_type=jnp.float32
    )
    back_stream = jnp.einsum("tcn,dcn->td", grad_project, qkv_w, preferred_element_type=jnp.float32)
    grad_stream = grad_first + lax.psum(back_stream.astype(jnp.bfloat16), "tensor").astype(
        jnp.float32
    )
    vector_grad = jnp.stack(
        (
            grad_gain_one,
            grad_shift_one,
            grad_gain_two,
            grad_shift_two,
            grad_out_bias,
            grad_down_bias,
        )
    )
    return (
        grad_stream,
        (grad_qkv, grad_outw, grad_up, grad_down),
        (vector_grad, grad_qv_bias, grad_up_bias),
    )


def adamw(weight, first, second, gradient, factor, rate, decay):
    clipped = gradient * factor
    new_first = BETA_ONE * first + (1.0 - BETA_ONE) * clipped
    new_second = BETA_TWO * second + (1.0 - BETA_TWO) * clipped * clipped
    first_hat = new_first / (1.0 - BETA_ONE**STEP)
    second_hat = new_second / (1.0 - BETA_TWO**STEP)
    new_weight = weight - rate * (first_hat / (jnp.sqrt(second_hat) + ADAM_EPS) + decay * weight)
    return (new_weight, new_first, new_second)


def body(
    inputs,
    pair_lengths,
    out_grad,
    w_qkv,
    m_qkv,
    v_qkv,
    w_out,
    m_out,
    v_out,
    w_up,
    m_up,
    v_up,
    w_down,
    m_down,
    v_down,
    vectors,
    m_vectors,
    v_vectors,
    qv_bias,
    m_qv_bias,
    v_qv_bias,
    up_bias,
    m_up_bias,
    v_up_bias,
):
    full_qkv, full_out, full_up, full_down = (
        lax.all_gather(w_qkv.astype(jnp.bfloat16), "dp", axis=1, tiled=True),
        lax.all_gather(w_out.astype(jnp.bfloat16), "dp", axis=1, tiled=True),
        lax.all_gather(w_up.astype(jnp.bfloat16), "dp", axis=1, tiled=True),
        lax.all_gather(w_down.astype(jnp.bfloat16), "dp", axis=1, tiled=True),
    )
    masks = jax.vmap(pair_mask)(pair_lengths)
    stream = inputs.astype(jnp.float32)
    kept_all = []
    for layer_index in range(LAYERS):
        stream, kept = layer_forward(
            stream,
            full_qkv[layer_index],
            full_out[layer_index],
            full_up[layer_index],
            full_down[layer_index],
            vectors[layer_index],
            qv_bias[layer_index],
            up_bias[layer_index],
            masks,
        )
        kept_all.append(kept)
    activations = stream.astype(jnp.bfloat16)
    grad_stream = out_grad.astype(jnp.float32)
    matrix_grads = [None] * LAYERS
    small_grads = [None] * LAYERS
    for layer_index in reversed(range(LAYERS)):
        grad_stream, mats, smalls = layer_backward(
            grad_stream,
            kept_all[layer_index],
            full_qkv[layer_index],
            full_out[layer_index],
            full_up[layer_index],
            full_down[layer_index],
            vectors[layer_index],
            masks,
        )
        matrix_grads[layer_index] = mats
        small_grads[layer_index] = smalls
    stacked = tuple(
        (
            jnp.stack([matrix_grads[layer_index][kind] for layer_index in range(LAYERS)])
            for kind in range(4)
        )
    )
    g_qkv, g_out, g_up, g_down = (
        lax.psum_scatter(stacked[0], "dp", scatter_dimension=1, tiled=True),
        lax.psum_scatter(stacked[1], "dp", scatter_dimension=1, tiled=True),
        lax.psum_scatter(stacked[2], "dp", scatter_dimension=1, tiled=True),
        lax.psum_scatter(stacked[3], "dp", scatter_dimension=1, tiled=True),
    )
    small_stacked = tuple(
        (
            jnp.stack([small_grads[layer_index][kind] for layer_index in range(LAYERS)])
            for kind in range(3)
        )
    )
    g_vec, g_qv, g_upb = lax.psum(small_stacked, "dp")
    data_count = lax.axis_size("dp")
    tensor_count = lax.axis_size("tensor")
    local_squares = (
        jnp.sum(g_qkv * g_qkv)
        + jnp.sum(g_out * g_out)
        + jnp.sum(g_up * g_up)
        + jnp.sum(g_down * g_down)
        + (jnp.sum(g_qv * g_qv) + jnp.sum(g_upb * g_upb)) / data_count
        + jnp.sum(g_vec * g_vec) / (data_count * tensor_count)
    )
    squares = lax.psum(local_squares, ("dp", "tensor"))
    grad_norm = jnp.sqrt(squares)
    factor = jnp.minimum(1.0, CLIP_LIMIT / grad_norm)
    new_qkv = adamw(w_qkv, m_qkv, v_qkv, g_qkv, factor, LEARN_RATE, WEIGHT_DECAY)
    new_out = adamw(w_out, m_out, v_out, g_out, factor, LEARN_RATE, WEIGHT_DECAY)
    new_up = adamw(w_up, m_up, v_up, g_up, factor, LEARN_RATE, WEIGHT_DECAY)
    new_down = adamw(w_down, m_down, v_down, g_down, factor, LEARN_RATE, WEIGHT_DECAY)
    new_vec = adamw(vectors, m_vectors, v_vectors, g_vec, factor, VECTOR_RATE, 0.0)
    new_qv = adamw(qv_bias, m_qv_bias, v_qv_bias, g_qv, factor, VECTOR_RATE, 0.0)
    new_upb = adamw(up_bias, m_up_bias, v_up_bias, g_upb, factor, VECTOR_RATE, 0.0)
    return (
        activations,
        grad_stream,
        grad_norm,
        new_qkv[0],
        new_qkv[1],
        new_qkv[2],
        new_out[0],
        new_out[1],
        new_out[2],
        new_up[0],
        new_up[1],
        new_up[2],
        new_down[0],
        new_down[1],
        new_down[2],
        new_vec[0],
        new_vec[1],
        new_vec[2],
        new_qv[0],
        new_qv[1],
        new_qv[2],
        new_upb[0],
        new_upb[1],
        new_upb[2],
    )


MESH = pl.DeviceIdType.MESH
F32, BF16 = jnp.float32, jnp.bfloat16
LINE = 4
DM = 768
QKV, OUT, UP, DOWN = KINDS = ("qkv", "out", "up", "down")
FIRST, SECOND, EARLY, LATE = range(4)
BLOCK = {QKV: (96, 576), OUT: (16, 1152), UP: (96, 768), DOWN: (96, 768)}
CUTS = (
    {QKV: (0, 48, 80), OUT: (1, 384, 1024), UP: (0, 32, 80), DOWN: (0, 32, 64)},
    {QKV: (0, 32, 80), OUT: (1, 384, 896), UP: (0, 32, 80), DOWN: (0, 16, 64)},
    {QKV: (0, 48, 96), OUT: (1, 512, 1152), UP: (0, 32, 80), DOWN: (0, 32, 64)},
    {QKV: (0, 32, 80), OUT: (1, 384, 896), UP: (0, 32, 80), DOWN: (0, 16, 64)},
)
G, L, F, S, M, R = range(6)
PLAN = {
    "need0": (
        (G, 1, 0),
        (L, 4, 1),
        (L, 2, 1),
        (G, 0, 1),
        (L, 1, 1),
        (L, 5, 1),
        (G, 2, 0),
        (G, 0, 2),
        (G, 1, 1),
        (L, 3, 1),
        (G, 0, 3),
        (G, 1, 2),
        (L, 2, 2),
        (G, 2, 1),
        (G, 1, 3),
        (L, 1, 2),
        (G, 4, 0),
        (G, 0, 5),
        (G, 0, 4),
        (G, 5, 0),
        (G, 2, 2),
        (G, 3, 0),
        (L, 1, 3),
        (G, 3, 1),
        (G, 2, 3),
        (G, 1, 5),
        (G, 1, 4),
        (G, 3, 2),
        (L, 3, 2),
        (L, 5, 2),
        (L, 1, 4),
        (G, 3, 3),
        (F, 0),
        (L, 2, 3),
        (G, 4, 1),
        (G, 2, 4),
        (L, 4, 2),
    ),
    "f0a2": ((L, 3, 3),),
    "f0o": ((G, 2, 5), (L, 2, 4), (G, 3, 5), (G, 5, 1), (F, 1), (G, 4, 2), (L, 5, 3), (G, 3, 4),),
    "f0v": ((F, 2),),
    "f0d": ((G, 5, 2), (G, 4, 3),),
    "need3": ((L, 3, 4), (F, 3), (L, 4, 3), (G, 5, 3), (L, 5, 4),),
    "f1q": ((G, 4, 5),),
    "f1a0": ((G, 4, 4),),
    "need5": ((F, 5),),
    "b1s": ((R, 0, 0),),
    "b1p": ((S, 3, 1, 6),),
    "b1a": ((S, 3, 1, 2),),
    "b1q": ((S, 3, 1, 1), (S, 2, 1, 2), (S, 2, 1, 6), (S, 2, 1, 1), (S, 3, 1, 8),),
    "b0s": ((S, 3, 1, 3), (S, 1, 1, 6),),
    "b0w": (
        (S, 2, 1, 3),
        (S, 3, 1, 5),
        (S, 3, 1, 9),
        (S, 2, 1, 7),
        (S, 1, 1, 2),
        (S, 0, 1, 7),
        (S, 1, 1, 1),
        (S, 2, 1, 4),
        (S, 1, 1, 7),
        (S, 0, 1, 2),
        (S, 0, 1, 1),
        (S, 3, 1, 10),
    ),
    "b0u": (
        (S, 1, 1, 3),
        (S, 1, 1, 8),
        (S, 0, 1, 8),
        (S, 2, 1, 8),
        (S, 0, 1, 3),
        (S, 1, 1, 4),
        (S, 2, 1, 5),
        (S, 1, 1, 9),
        (S, 0, 1, 4),
        (S, 2, 1, 9),
        (M, 1, 1),
        (S, 1, 1, 5),
        (S, 0, 1, 9),
        (S, 3, 0, 2),
        (S, 3, 0, 6),
        (S, 3, 0, 1),
        (R, 0, 1),
        (S, 0, 1, 5),
        (S, 2, 1, 10),
        (S, 1, 1, 10),
    ),
    "b0p": ((S, 3, 0, 3),),
    "b0a": ((S, 0, 1, 10),),
    "end": (
        (R, 0, 2),
        (S, 2, 0, 6),
        (S, 3, 0, 4),
        (S, 2, 0, 1),
        (S, 2, 0, 2),
        (M, 0, 1),
        (S, 1, 0, 1),
        (S, 1, 0, 6),
        (M, 1, 2),
        (S, 1, 0, 2),
        (S, 3, 0, 5),
        (S, 0, 0, 2),
        (S, 0, 0, 1),
        (S, 0, 0, 6),
        (M, 1, 3),
        (S, 3, 0, 7),
        (S, 2, 0, 3),
        (S, 1, 0, 3),
        (R, 1, 0),
        (S, 2, 0, 7),
        (S, 0, 0, 3),
        (S, 0, 0, 7),
        (S, 2, 0, 4),
        (S, 1, 0, 7),
        (S, 1, 0, 4),
        (S, 0, 0, 8),
        (M, 0, 2),
        (S, 0, 0, 4),
        (S, 1, 0, 8),
        (S, 2, 0, 5),
        (S, 2, 0, 8),
        (S, 3, 0, 8),
        (R, 1, 1),
        (S, 1, 0, 5),
        (S, 2, 0, 9),
        (S, 1, 0, 9),
        (S, 0, 0, 5),
        (M, 0, 3),
        (S, 0, 0, 9),
        (S, 3, 0, 9),
        (S, 0, 0, 10),
        (R, 1, 2),
        (S, 2, 0, 10),
        (S, 1, 0, 10),
        (S, 3, 0, 10),
    ),
    "b1b": ((S, 3, 1, 7),),
    "b0h": ((S, 3, 1, 4), (S, 0, 1, 6),),
    "f1o": ((L, 4, 4), (G, 5, 4), (G, 5, 5),),
    "f1n": ((F, 4),),
}
SEMS = 205
OWN, HALF = 384, 256


def dot(a, b):
    return jnp.dot(a, b, preferred_element_type=F32)


def dot_nt(a, b):
    return lax.dot_general(a, b, (((1,), (1,)), ((), ())), preferred_element_type=F32)


def dot_tn(a, b):
    return lax.dot_general(a, b, (((0,), (0,)), ((), ())), preferred_element_type=F32)


def flat(v):
    return v.reshape((-1, v.shape[-1]))


def gelu_and_slope(u):
    a = jnp.abs(u) * (1.0 / math.sqrt(2.0))
    t = 1.0 / (1.0 + 0.5 * a)
    poly = 0.17087277
    for coeff in (
        -0.82215223,
        1.48851587,
        -1.13520398,
        0.27886807,
        -0.18628806,
        0.09678418,
        0.37409196,
        1.00002368,
        -1.26551223,
    ):
        poly = poly * t + coeff
    bell = jnp.exp(-0.5 * u * u)
    tail = 0.5 * t * bell * jnp.exp(poly)
    below = jnp.where(u >= 0, 1.0 - tail, tail)
    return u * below, below + u * bell * (1.0 / math.sqrt(2.0 * math.pi))


def norm_stats(rows):
    center = rows - jnp.mean(rows, axis=-1, keepdims=True)
    spread = jnp.mean(center * center, axis=-1, keepdims=True)
    scale = lax.rsqrt(spread + NORM_EPS)
    return center * scale, scale


class Moves:
    def __init__(self, send, recv):
        self.send, self.recv, self.count, self.open = send, recv, 0, []
        self.again, self.log = [], []

    def make(self, src, dst, device, lands, can_send=None, can_recv=None):
        if self.again:
            index = self.again.pop(0)
        else:
            index = self.count
            self.count += 1
        assert index < SEMS
        self.log.append(index)
        move = types.SimpleNamespace(index=index)

        def copy(src, dst):
            return pltpu.make_async_remote_copy(
                src_ref=src,
                dst_ref=dst,
                send_sem=self.send.at[index],
                recv_sem=self.recv.at[index],
                device_id=device,
                device_id_type=MESH,
            )

        def guarded(cond, act):
            if cond is None:
                act()
            else:
                pl.when(cond)(act)

        def start():
            guarded(can_send, lambda: copy(src(), dst()).start())
            self.open.append(move)

        move.start = start
        move.wait_recv = lambda: guarded(can_recv, lambda: copy(lands(), lands()).wait_recv())
        move.wait_send = lambda: guarded(can_send, lambda: copy(src(), src()).wait_send())
        return move

    def sent(self, *moves):
        for move in moves:
            move.wait_send()
            self.open.remove(move)

    def drain_but(self, *moves):
        self.sent(*[move for move in self.open if move not in moves])

    def drain(self):
        for move in self.open:
            move.wait_send()
        self.open = []


def fused(names, *refs):
    k = types.SimpleNamespace(**dict(zip(names, refs)))
    dp, tensor = lax.axis_index("dp"), lax.axis_index("tensor")
    z, x, y, c = dp // 2, dp % 2, tensor // 2, tensor % 2
    core_dev = (dp, y * 2 + 1 - c)
    y_dev = (dp, (1 - y) * 2 + c)
    x_dev = (z * 2 + 1 - x, tensor)
    up_dev = ((z + 1) * 2 + x, tensor)
    down_dev = ((z - 1) * 2 + x, tensor)
    xy_dev = (z * 2 + 1 - x, (1 - y) * 2 + c)
    not_last, not_first = z <= LINE - 2, z >= 1

    pack_row = pl.multiple_of(y * (2 * SEQ), SEQ)
    own_a = pl.multiple_of(c * HALF, HALF)
    own_p = pl.multiple_of(SEQ + HALF * y + 128 * c, 128)
    loads = [
        pltpu.make_async_copy(k.wq_in, k.stage_q, k.local.at[0]),
        pltpu.make_async_copy(k.wu_in, k.sum1.at[0, pl.ds(0, 192)], k.local.at[1]),
        pltpu.make_async_copy(k.wd_in, k.sum1.at[0, pl.ds(192, 192)], k.local.at[2]),
        pltpu.make_async_copy(k.wo_in, k.sum1.at[1, pl.ds(0, 48)], k.local.at[3]),
    ]
    x_loads = [
        pltpu.make_async_copy(k.x_in.at[pl.ds(pack_row, SEQ)], k.x_buf.at[pl.ds(0, SEQ)], k.local.at[4]),
        pltpu.make_async_copy(k.x_in.at[pl.ds(SEQ, SEQ)], k.x_buf.at[pl.ds(SEQ, SEQ)], k.local.at[5]),
    ]
    in_a = pl.multiple_of(pack_row + own_a, HALF)
    e_loads = [
        pltpu.make_async_copy(k.e_in.at[pl.ds(in_a, HALF)], k.e_low.at[pl.ds(0, HALF)], k.local.at[6]),
        pltpu.make_async_copy(k.e_in.at[pl.ds(own_p, 128)], k.e_low.at[pl.ds(HALF, 128)], k.local.at[7]),
    ]
    for load in loads + x_loads + e_loads:
        load.start()

    plane_devs = [(z * 2 + (x ^ i // 4), (y ^ i // 2 % 2) * 2 + (c ^ i % 2)) for i in range(1, 8)]
    line_devs = [((z ^ i) * 2 + x, tensor) for i in range(1, LINE)]
    barrier = pltpu.get_barrier_semaphore()
    for device in plane_devs + line_devs:
        pl.semaphore_signal(barrier, inc=1, device_id=device, device_id_type=MESH)

    moves = Moves(k.send, k.recv)
    weights = {QKV: k.w_qkv, OUT: k.w_out, UP: k.w_up, DOWN: k.w_down}

    def one(v):
        return (v, 1)

    both, line = (0, 2), (0, LINE)

    def part(kind, number, cuts=0):
        axis, first, second = CUTS[cuts][kind]
        full = BLOCK[kind]
        low, high = ((0, first), (first, second), (0, second), (second, full[axis]))[number]
        cut = [(0, full[0]), (0, full[1])]
        cut[axis] = (low, high - low)
        return tuple(cut)

    def region(kind, layer, ys, zs, xs, number, cuts=0):
        rows, cols = part(kind, number, 2 if cuts == 0 and layer == 0 and kind in (QKV, OUT) else cuts)
        return weights[kind].at[(layer,) + tuple(pl.ds(*cut) for cut in (ys, zs, xs, rows, cols))]

    def swap(kind, layer, axis, number, ys, zs, xs):
        other_ys, other_xs = (one(1 - y), xs) if axis == "y" else (ys, one(1 - x))
        here = lambda: region(kind, layer, ys, zs, xs, number)
        return [
            moves.make(
                here,
                here,
                y_dev if axis == "y" else x_dev,
                lambda: region(kind, layer, other_ys, zs, other_xs, number),
            )
        ]

    def hop(kind, layer, step, number, ys, xs):
        at = lambda v: (lambda: region(kind, layer, ys, one(v), xs, number))
        return [
            moves.make(
                at(z - step + 1),
                at(z - step + 1),
                up_dev,
                at(z - step),
                (z >= step - 1) & not_last,
                z >= step,
            ),
            moves.make(
                at(z + step - 1),
                at(z + step - 1),
                down_dev,
                at(z + step),
                (z <= LINE - step) & not_first,
                z <= LINE - 1 - step,
            ),
        ]

    def gather_steps(kind, layer):
        a = (kind, layer)
        hops = [hop(*a, step, EARLY, one(y), one(x)) for step in (1, 2, 3)]
        first_x = swap(*a, "x", FIRST, one(y), line, one(x))
        second_y = swap(*a, "y", SECOND, one(y), line, one(x))
        first_y = swap(*a, "y", FIRST, one(y), line, both)
        second_x = swap(*a, "x", SECOND, both, line, one(x))
        early = [
            ([], hops[0]),
            (hops[0], hops[1]),
            (hops[1], hops[2]),
            (hops[2], first_x + second_y),
            (first_x, first_y),
            (second_y, second_x),
            (first_y + second_x, []),
        ]
        if layer == 0 and kind in (QKV, OUT):
            return early, [([], [])] * 6
        late_x = swap(*a, "x", LATE, one(y), one(z), one(x))
        late_y = swap(*a, "y", LATE, one(y), one(z), both)
        hops = [hop(*a, step, LATE, both, both) for step in (1, 2, 3)]
        return early, [([], late_x), (late_x, late_y), (late_y, hops[0]), (hops[0], hops[1]), (hops[1], hops[2]), (hops[2], [])]

    gather_chunks = [
        ((QKV, 0), (OUT, 0)),
        ((UP, 0),),
        ((DOWN, 0),),
        ((QKV, 1), (OUT, 1)),
        ((UP, 1),),
        ((DOWN, 1),),
    ]
    gathers, indices = [], {}
    for chunk in gather_chunks:
        gathers.append([])
        for kind, layer in chunk:
            start = moves.count
            gathers[-1].append(gather_steps(kind, layer))
            indices[kind, layer] = list(range(start, moves.count))

    def gather(chunk, late, step):
        for steps in gathers[chunk]:
            for move in steps[late][step][0]:
                move.wait_recv()
        for steps in gathers[chunk]:
            for move in steps[late][step][1]:
                move.start()

    def add_into(kind, layer, ys, zs, xs, number, buf, from_xs=0, from_ys=0):
        rows, cols = part(kind, number, 1)
        count = (ys[1], zs[1], xs[1])

        @pl.loop(0, count[0] * count[1] * count[2])
        def _(i):
            yi, zi, xi = i // (count[1] * count[2]), (i // count[2]) % count[1], i % count[2]
            at = (layer, ys[0] + yi, zs[0] + zi, xs[0] + xi, pl.ds(*rows), pl.ds(*cols))
            weights[kind][at] = weights[kind][at] + buf[from_ys + yi, zi, from_xs + xi]

    def scatter_swap(kind, layer, axis, number, ys, zs, xs, buf):
        away_ys, away_xs = (one(1 - y), xs) if axis == "y" else (ys, one(1 - x))
        landing = lambda: buf
        return moves.make(
            lambda: region(kind, layer, away_ys, zs, away_xs, number, 1),
            landing,
            y_dev if axis == "y" else x_dev,
            landing,
        )

    def scatter_hop(kind, layer, step, number, ys, xs, buf):
        found = []
        for way, device, goes, sends, comes, receives in (
            (0, up_dev, z + LINE - step, (z <= step - 1) & not_last, z + 3 - step, not_first & (z <= step)),
            (1, down_dev, z - LINE + step, (z >= LINE - step) & not_first, z - 3 + step, not_last & (z >= 3 - step)),
        ):
            landing = lambda way=way: buf.at[way, step - 1]
            move = moves.make(
                lambda goes=goes: region(kind, layer, ys, one(goes), xs, number, 1),
                landing,
                device,
                landing,
                sends,
                receives,
            )

            def add(way=way, comes=comes, receives=receives):
                pl.when(receives)(
                    lambda: add_into(kind, layer, ys, one(comes), xs, number, buf.at[way, step - 1])
                )

            found.append((move, add))
        return found

    def scatter_steps(kind, layer):
        a = (kind, layer)
        r = types.SimpleNamespace(
            **{name[: -len(kind)]: ref for name, ref in vars(k).items() if name[0] == "r" and name.endswith(kind)}
        )
        first_y = scatter_swap(*a, "y", FIRST, both, line, both, r.ry1)
        second_x = scatter_swap(*a, "x", SECOND, both, line, both, r.rx2)
        first_x = scatter_swap(*a, "x", FIRST, one(y), line, both, r.rx1)
        second_y = scatter_swap(*a, "y", SECOND, both, line, one(x), r.ry2)
        late_y = scatter_swap(*a, "y", LATE, both, one(z), both, r.ry3)
        late_x = scatter_swap(*a, "x", LATE, one(y), one(z), both, r.rx3)
        early = [scatter_hop(*a, step, EARLY, one(y), one(x), r.rz) for step in (1, 2, 3)]
        late = [scatter_hop(*a, step, LATE, both, both, r.rz3) for step in (1, 2, 3)]

        def starts(found):
            return [move.start for move, _ in found]

        def onward(found, then):
            steps = []
            for index, (move, add) in enumerate(found):
                steps += [move.wait_recv, add]
                if then:
                    steps.append(then[index][0].start)
            return steps

        return [
            [first_y.start, second_x.start] + starts(late[0]),
            [
                first_y.wait_recv,
                lambda: add_into(*a, one(y), line, one(1 - x), FIRST, r.ry1, from_xs=1 - x),
                first_x.start,
                lambda: add_into(*a, one(y), line, one(x), FIRST, r.ry1, from_xs=x),
            ],
            [
                second_x.wait_recv,
                lambda: add_into(*a, one(1 - y), line, one(x), SECOND, r.rx2, from_ys=1 - y),
                second_y.start,
                lambda: add_into(*a, one(y), line, one(x), SECOND, r.rx2, from_ys=y),
            ],
            [
                first_x.wait_recv,
                lambda: add_into(*a, one(y), line, one(x), FIRST, r.rx1),
                second_y.wait_recv,
                lambda: add_into(*a, one(y), line, one(x), SECOND, r.ry2),
            ]
            + starts(early[0]),
            onward(early[0], early[1]),
            onward(early[1], early[2]),
            onward(late[0], late[1]),
            onward(late[1], late[2]),
            onward(late[2], None) + [late_y.start],
            [late_y.wait_recv, lambda: add_into(*a, one(y), one(z), both, LATE, r.ry3), late_x.start],
            onward(early[2], None)
            + [
                late_x.wait_recv,
                lambda: add_into(*a, one(y), one(z), one(x), LATE, r.rx3),
                lambda: finish(kind, layer),
            ],
        ]

    def finish(kind, layer):
        total = weights[kind][layer, y, z, x].astype(F32)
        size, width = BLOCK[kind]
        k.sq_rows[:, 0:width] += jnp.sum((total * total).reshape((size // 8, 8, width)), axis=0)
        if kind == QKV:
            for j in range(3):
                k.g_qkv[layer, j] = total[:, j * 192 : (j + 1) * 192]
        elif kind == OUT:
            k.g_out[layer, 0:16, :] = total[:, 0:768]
            k.g_out[layer, 16:24, 0:384] = total[0:8, 768:1152]
            k.g_out[layer, 16:24, 384:768] = total[8:16, 768:1152]
        else:
            (k.g_up if kind == UP else k.g_down)[layer] = total

    scatters, used = {}, {}
    lenders = {DOWN: UP, UP: QKV, OUT: OUT, QKV: DOWN}

    def scatter(kind, layer, step):
        chunk = (kind, layer)
        if step == 0:
            if layer:
                moves.again = list(indices[lenders[kind], 0])
            else:
                moves.sent(*[move for move in moves.open if move.index in used[kind]])
                moves.again = list(used[kind])
            before = len(moves.log)
            scatters[chunk] = scatter_steps(kind, layer)
            used[kind] = moves.log[before:]
            moves.again = []
        for act in scatters[chunk][step]:
            act()

    def small_step(layer, step):
        if step:
            total = k.small[layer, step - 1]
            for index, move in small_moves[layer]:
                move.wait_recv()
                total = total + k.small_in[layer, index]
            if step == 1:
                row = lax.broadcasted_iota(jnp.int32, (16, DM), 0)
                total = jnp.where(row < 6, total, k.small[layer, 0])
            k.small[layer, step] = total
        if step < 3:
            devices = ((core_dev,), (x_dev, y_dev, xy_dev), line_devs)[step]
            small_moves[layer] = []
            for i, device in enumerate(devices):
                index = (0, 1, 4)[step] + i
                landing = lambda index=index: k.small_in.at[layer, index]
                move = moves.make(lambda: k.small.at[layer, step], landing, device, landing)
                move.start()
                small_moves[layer].append((index, move))

    small_moves = {}

    spreads = {}

    def at(name):
        for what, *args in PLAN.get(name, ()):
            if what == G:
                gather(args[0], 0, args[1])
            elif what == L:
                gather(args[0], 1, args[1])
            elif what == F:
                gather(args[0], 0, 6)
                gather(args[0], 1, 5)
            elif what == S:
                scatter(KINDS[args[0]], args[1], args[2])
            elif what == M:
                small_step(*args)
            else:
                spreads[args[0]][args[1]]()


    k.small[0, 0] = jnp.zeros((16, DM), F32)
    clear = pltpu.make_async_copy(k.small.at[0, 0], k.small.at[1, 0], k.local.at[15])
    clear.start()
    clear.wait()

    for slot in range(2):
        pack = 1 if slot else 2 * y
        columns = lax.broadcasted_iota(jnp.int32, (8, SEQ), 1)
        rows = lax.broadcasted_iota(jnp.int32, (SEQ, 128), 0)
        pair_col, pair_row = jnp.zeros((8, SEQ), F32), jnp.zeros((SEQ, 128), F32)
        end = jnp.int32(0)
        for j in range(4):
            end = end + k.lens[pack, j]
            pair_col += jnp.where(columns >= end, 1.0, 0.0)
            pair_row += jnp.where(rows >= end, 1.0, 0.0)
        k.pair_col[slot] = pair_col
        k.pair_row[slot] = pair_row
    k.sq_rows[...] = jnp.zeros(k.sq_rows.shape, F32)

    k.bias[y, :, :] = jnp.zeros((8, DM), F32)
    for layer in range(LAYERS):
        k.bias[y, pl.ds(layer, 1), :] = k.upb_in[pl.ds(layer, 1), :]
        k.bias[y, pl.ds(2 + layer, 1), 0:192] = k.qvb_in[layer, 0:1, :]
        k.bias[y, pl.ds(2 + layer, 1), 384:576] = k.qvb_in[layer, 1:2, :]
    loads[0].wait()
    for layer in range(LAYERS):
        for j in range(3):
            k.w_qkv[layer, y, z, x, :, j * 192 : (j + 1) * 192] = k.stage_q[layer, j].astype(BF16)
    loads[3].wait()
    for layer in range(LAYERS):
        rows = k.sum1[1, pl.ds(layer * 24, 24), :]
        k.w_out[layer, y, z, x, :, 0:768] = rows[0:16].astype(BF16)
        k.w_out[layer, y, z, x, :, 768:1152] = jnp.concatenate([rows[16:24, 0:384], rows[16:24, 384:768]], axis=0).astype(BF16)
    loads[1].wait()
    loads[2].wait()
    for layer in range(LAYERS):
        k.w_up[layer, y, z, x] = k.sum1[0, pl.ds(layer * 96, 96), :].astype(BF16)
        k.w_down[layer, y, z, x] = k.sum1[0, pl.ds(192 + layer * 96, 96), :].astype(BF16)

    pl.semaphore_wait(barrier, len(plane_devs + line_devs))
    gather(0, 0, 0)
    for chunk in range(1, len(gathers)):
        gather(chunk, 1, 0)
    bias_move = moves.make(
        lambda: k.bias.at[pl.ds(y, 1)], lambda: k.bias.at[pl.ds(y, 1)], y_dev, lambda: k.bias.at[pl.ds(1 - y, 1)]
    )
    bias_move.start()

    for load in x_loads:
        load.wait()
    k.res[0:HALF, :] = k.x_buf[pl.ds(own_a, HALF), :].astype(F32)
    k.res[HALF:OWN, :] = k.x_buf[pl.ds(own_p, 128), :].astype(F32)
    bias_move.wait_recv()
    at("f0s")

    def gather_pair(buf, layer=None):
        at = lambda slot: (lambda: buf.at[pl.ds(slot, 1)])
        move = moves.make(at(c), at(c), core_dev, at(1 - c))
        move.start()
        return move

    def gather_chip(buf):
        found = []
        for mine, other, size in ((own_a, (1 - c) * HALF, HALF), (SEQ + 128 * c, SEQ + 128 * (1 - c), 128)):
            here = lambda mine=mine, size=size: buf.at[pl.ds(pl.multiple_of(mine, 128), size)]
            there = lambda other=other, size=size: buf.at[pl.ds(pl.multiple_of(other, 128), size)]
            found.append(moves.make(here, here, core_dev, there))
            found[-1].start()
        return found

    def gather_rows(buf):
        rows = lambda start, size: (lambda: buf.at[pl.ds(pl.multiple_of(start, 128), size)])
        other_p = SEQ + HALF * (1 - y) + 128 * c
        mine = rows(own_p, 128)
        far = lambda: k.x_far
        across = moves.make(mine, far, y_dev, far)
        across.start()
        first = moves.make(rows(own_a, HALF), rows(own_a, HALF), core_dev, rows((1 - c) * HALF, HALF))
        first.start()
        second = moves.make(mine, mine, core_dev, rows(SEQ + HALF * y + 128 * (1 - c), 128))
        second.start()

        def relay():
            across.wait_recv()
            buf[pl.ds(pl.multiple_of(other_p, 128), 128), :] = k.x_far[...]
            third = moves.make(far, rows(other_p, 128), core_dev, rows(SEQ + HALF * (1 - y) + 128 * (1 - c), 128))
            third.start()
            return third

        return across, first, second, relay

    def sum_pair(fill):
        def to_send(rows, cols, value):
            k.ex_s[rows, cols] = value.astype(BF16)

        def to_keep(rows, cols, value):
            k.cur[rows, cols] = value

        fill(1 - c, to_send)
        move = moves.make(
            lambda: k.ex_s.at[pl.ds(0, OWN)], lambda: k.ex_r.at[pl.ds(0, OWN)], core_dev, lambda: k.ex_r.at[pl.ds(0, OWN)]
        )
        move.start()
        fill(c, to_keep)

        def end():
            move.wait_recv()
            k.cur[...] += k.ex_r[0:OWN, :].astype(F32)
            moves.sent(move)

        return end

    def fill_rows(part_a, part_p):
        def fill(slot, store):
            store(slice(0, HALF), slice(0, DM), part_a(slot))
            store(slice(HALF, OWN), slice(0, DM), part_p(slot))

        return fill

    def send_away(part):
        k.ex_s[OWN:SEQ, :] = part(1 - c).astype(BF16)
        piece = lambda ref: (lambda: ref.at[pl.ds(OWN, 128)])
        beside = moves.make(piece(k.ex_s), piece(k.ex_r), core_dev, piece(k.ex_r))
        beside.start()
        k.ey_f[...] = part(c)
        across = moves.make(lambda: k.ey_s, lambda: k.ey_r, y_dev, lambda: k.ey_r)

        def go():
            beside.wait_recv()
            k.ey_s[...] = (k.ey_f[...] + k.ex_r[OWN:SEQ, :].astype(F32)).astype(BF16)
            across.start()

        def end():
            across.wait_recv()
            k.cur[HALF:OWN, :] += k.ey_r[...].astype(F32)
            moves.sent(beside, across)

        return go, end

    def spread(low, out, sems):
        piece = lambda ref, start, size: (lambda: ref.at[pl.ds(pl.multiple_of(start, 128), size)])
        other_a, other_p = (1 - y) * (2 * SEQ) + c * HALF, SEQ + HALF * (1 - y) + 128 * c
        copies, across, beside, relays = [], [], [], []
        for index, (start, size, mine, far) in enumerate(((0, HALF, in_a, other_a), (HALF, 128, own_p, other_p))):
            toward = (1 - 2 * c) * size
            own, there = piece(low, start, size), piece(out, mine, size)
            copies.append(
                lambda own=own, there=there, index=index: pltpu.make_async_copy(own(), there(), k.local.at[sems + index])
            )
            across.append(moves.make(own, there, y_dev, piece(out, far, size)))
            beside.append(moves.make(own, there, core_dev, piece(out, mine + toward, size)))
            far_rows = piece(out, far, size)
            relays.append(moves.make(far_rows, far_rows, core_dev, piece(out, far + toward, size)))

        def begin():
            for copy in copies:
                copy().start()
            for move in across + beside:
                move.start()

        def relay():
            for arrived, move in zip(across, relays):
                arrived.wait_recv()
                move.start()

        def end():
            for copy in copies:
                copy().wait()
            for move in beside + relays:
                move.wait_recv()

        return begin, relay, end

    def save(slot, src, dst):
        copy = pltpu.make_async_copy(src, dst, k.local.at[slot])
        copy.start()
        return copy

    def norm_grad(layer, e, xhat, scale, gain_row, bias_row, rows):
        h = e * k.vec[gain_row, layer : layer + 1, :]
        mean_h = jnp.mean(h, axis=-1, keepdims=True)
        mean_hx = jnp.mean(h * xhat, axis=-1, keepdims=True)
        grad = scale * (h - mean_h - xhat * mean_hx)
        k.res[rows, :] = grad
        acc = k.small.at[layer, 0]
        acc[gain_row : gain_row + 1, :] += jnp.sum(e * xhat, axis=0, keepdims=True)
        acc[gain_row + 1 : gain_row + 2, :] += jnp.sum(e, axis=0, keepdims=True)
        acc[bias_row : bias_row + 1, :] += jnp.sum(grad, axis=0, keepdims=True)

    row_tiles = OWN // 128
    saves = []
    for layer in range(LAYERS):
        if layer == 1:
            k.x_buf[pl.ds(own_a, HALF), :] = k.res[0:HALF, :].astype(BF16)
            k.x_buf[pl.ds(own_p, 128), :] = k.res[HALF:OWN, :].astype(BF16)
            _, first, second, relay = gather_rows(k.x_buf)
            at("f1s")
        place = "f" + str(layer)
        at("need" + str(3 * layer))
        if layer == 1:
            for move in (first, second):
                move.wait_recv()

        for group in range(2):
            for zi in range(LINE):
                for xi in range(2):
                    block = k.w_out[layer, group, zi, xi].astype(F32)
                    low = (zi * 2 + xi) * 24
                    k.unpack[low : low + 16, :] = block[:, 0:768]
                    k.unpack[low + 16 : low + 24, 0:384] = block[0:8, 768:1152]
                    k.unpack[low + 16 : low + 24, 384:768] = block[8:16, 768:1152]
            k.w_o[layer, group] = k.unpack[...].astype(BF16)

        shrink = jnp.where(lax.broadcasted_iota(jnp.int32, (1, 576), 1) < 192, HD ** (-0.5), 1.0)

        def project(group, start):
            rows = pl.ds(pl.multiple_of(start, HALF), HALF)
            made = dot(k.x_buf[rows, :], flat(k.w_qkv[layer, group]))
            made = (made + k.bias[group, 2 + layer : 3 + layer, 0:576]) * shrink
            k.qkv[layer, group, rows, :] = made.astype(BF16)

        def attend(group, tile, key_start, pair_start):
            slot = key_start // SEQ
            rows = pl.ds(pl.multiple_of(tile * HALF, HALF), HALF)
            from_rows = pl.ds(pl.multiple_of(key_start + pair_start, HALF), HALF)
            keys = pl.ds(key_start, SEQ)
            allowed = k.pair_row[slot, pl.ds(pl.multiple_of(pair_start, HALF), HALF), 0:1] == k.pair_col[slot, 0:1, :]
            for head in range(3):
                low, high = head * HD, (head + 1) * HD
                queries = k.qkv[layer, group, from_rows, low:high]
                key_rows = k.qkv[layer, group, keys, 192 + low : 192 + high]
                values = k.qkv[layer, group, keys, 384 + low : 384 + high]
                scores = jnp.where(allowed, dot_nt(queries, key_rows), -1e30)
                raised = jnp.exp(scores - jnp.max(scores, axis=-1, keepdims=True))
                probs = (raised * (1.0 / jnp.sum(raised, axis=-1, keepdims=True))).astype(BF16)
                k.probs[group, head, rows, :] = probs
                k.merged[layer, group, rows, low:high] = dot(probs, values).astype(BF16)

        if layer == 0:
            pl.loop(0, 8)(lambda i: project(i // 4, (i % 4) * HALF))
        else:
            pl.loop(0, 6)(lambda i: project(i // 3, jnp.where(i % 3 == 2, SEQ + HALF * y, (i % 3) * HALF)))
            saves[0].wait()
        at(place + "q")

        @pl.loop(0, 4)
        def _(i):
            attend(i // 2, i % 2, 0, (i % 2) * HALF)
            for turn in range(4):
                pl.when(i == turn)(lambda: at(place + "a" + str(turn)))

        if layer == 1:
            relay().wait_recv()
            pl.loop(0, 2)(lambda group: project(group, SEQ + HALF * (1 - y)))
        pl.loop(0, 2)(lambda group: attend(group, 2, SEQ, HALF * y))
        at(place + "p")
        if layer == 0:
            saves.append(save(8, k.probs, k.probs_hbm))

        def out_rows(start, size):
            rows = pl.ds(pl.multiple_of(start, 128), size)
            return dot(k.merged[layer, 0, rows, :], k.w_o[layer, 0]) + dot(k.merged[layer, 1, rows, :], k.w_o[layer, 1])

        end_out = sum_pair(
            fill_rows(lambda slot: out_rows(slot * HALF, HALF), lambda slot: out_rows(SEQ + 128 * slot, 128))
        )

        def first_norm(i):
            rows = pl.ds(pl.multiple_of(i * 128, 128), 128)
            total = k.res[rows, :] + k.cur[rows, :] + k.vec[4, layer : layer + 1, :]
            k.sum1[layer, rows, :] = total
            normed = norm_stats(total)[0] * k.vec[0, layer : layer + 1, :] + k.vec[1, layer : layer + 1, :]
            k.res[rows, :] = normed
            k.nlow[layer, c, rows, :] = normed.astype(BF16)

        at(place + "o")
        end_out()
        pl.loop(0, row_tiles)(first_norm)

        mate_rows = gather_pair(k.nlow.at[layer])
        at(place + "n")
        at("need" + str(3 * layer + 1))
        if layer == 1:
            saves[1].wait()
            saves[2].wait()
        for order in range(2):
            slot = c if order == 0 else 1 - c
            if order:
                mate_rows.wait_recv()

            @pl.loop(0, 6)
            def _(i):
                group, cols = i // 3, pl.ds(pl.multiple_of((i % 3) * 256, 256), 256)
                made = dot(k.nlow[layer, slot], flat(k.w_up[layer, group, :, :, :, cols]))
                made = made + k.bias[group, layer : layer + 1, cols]
                act, slope = gelu_and_slope(made)
                k.act[group, slot, :, cols] = act.astype(BF16)
                k.slope[group, slot, :, cols] = slope.astype(BF16)
                pl.when(i == 2)(lambda: at(place + "xw"[order]))

            at(place + "uv"[order])

        if layer == 0:
            saves.append(save(9, k.act, k.act_hbm))
            saves.append(save(10, k.slope, k.slope_hbm))
        at("need" + str(3 * layer + 2))

        def down_rows(slot, store):
            made = dot(k.act[0, slot], flat(k.w_down[layer, 0]))
            store(slice(0, OWN), slice(0, DM), made + dot(k.act[1, slot], flat(k.w_down[layer, 1])))

        end_down = sum_pair(down_rows)
        at(place + "d")
        if layer == 1:
            for load in e_loads:
                load.wait()
        end_down()

        @pl.loop(0, row_tiles)
        def _(i):
            rows = pl.ds(pl.multiple_of(i * 128, 128), 128)
            total = k.res[rows, :] + k.cur[rows, :] + k.vec[5, layer : layer + 1, :]
            xhat, scale = norm_stats(total)
            result = xhat * k.vec[2, layer : layer + 1, :] + k.vec[3, layer : layer + 1, :]
            if layer == 0:
                k.sum2[rows, :] = total
                k.res[rows, :] = result
            else:
                k.a_low[rows, :] = result.astype(BF16)
                norm_grad(layer, k.e_low[rows, :].astype(F32), xhat, scale, 2, 5, rows)
                k.lsec[c, rows, :] = k.res[rows, :].astype(BF16)

    mate_rows = gather_pair(k.lsec)
    moves.drain_but(mate_rows)
    spreads[0] = spread(k.a_low, k.activations, 11)

    for layer in (1, 0):
        place = "b" + str(layer)
        if layer == 0:

            @pl.loop(0, row_tiles)
            def _(i):
                rows = pl.ds(pl.multiple_of(i * 128, 128), 128)
                xhat, scale = norm_stats(k.sum2[rows, :])
                norm_grad(layer, k.res[rows, :] + k.cur[rows, :], xhat, scale, 2, 5, rows)
                k.lsec[c, rows, :] = k.res[rows, :].astype(BF16)

            mate_rows = gather_pair(k.lsec)
            restore_act.wait()
            restore_slope.wait()
        at(place + "s")
        for order in range(2):
            slot = c if order == 0 else 1 - c
            if order:
                mate_rows.wait_recv()
                moves.sent(mate_rows)

            @pl.loop(0, 4)
            def _(i):
                group, tile = i // 2, i % 2
                cols = pl.ds(pl.multiple_of(tile * OWN, OWN), OWN)
                back = dot_nt(k.lsec[slot], flat(k.w_down[layer, group, pl.ds(tile * 2, 2)]))
                grad = (back * k.slope[group, slot, :, cols].astype(F32)).astype(BF16)
                k.slope[group, slot, :, cols] = grad
                k.small[layer, 0, pl.ds(6 + group, 1), cols] += jnp.sum(grad.astype(F32), axis=0, keepdims=True)

            at(place + "gh"[order])

        @pl.loop(0, 2)
        def _(group):
            made = dot_tn(flat(k.act[group]), flat(k.lsec[...]))
            k.w_down[layer, group] = made.astype(BF16).reshape((LINE, 2, 96, 768))

        at(place + "w")
        scatter(DOWN, layer, 0)
        if layer == 1:
            restore_act = save(9, k.act_hbm, k.act)

        def normed_rows(slot, store):
            @pl.loop(0, 2)
            def _(tile):
                cols = pl.ds(pl.multiple_of(tile * OWN, OWN), OWN)
                made = dot_nt(k.slope[0, slot], flat(k.w_up[layer, 0, pl.ds(tile * 2, 2)]))
                store(slice(0, OWN), cols, made + dot_nt(k.slope[1, slot], flat(k.w_up[layer, 1, pl.ds(tile * 2, 2)])))

        end_normed = sum_pair(normed_rows)
        at(place + "n")
        end_normed()

        @pl.loop(0, row_tiles)
        def _(i):
            rows = pl.ds(pl.multiple_of(i * 128, 128), 128)
            xhat, scale = norm_stats(k.sum1[layer, rows, :])
            norm_grad(layer, k.res[rows, :] + k.cur[rows, :], xhat, scale, 0, 4, rows)
            start = jnp.where(i == 2, SEQ + 128 * c, own_a + i * 128)
            k.lfirst[pl.ds(pl.multiple_of(start, 128), 128), :] = k.res[rows, :].astype(BF16)

        mate_firsts = gather_chip(k.lfirst)
        at(place + "f")

        @pl.loop(0, 2)
        def _(group):
            made = dot_tn(flat(k.nlow[layer]), flat(k.slope[group]))
            k.w_up[layer, group] = made.astype(BF16).reshape((LINE, 2, 96, 768))

        at(place + "u")
        scatter(UP, layer, 0)
        if layer == 1:
            restore_slope = save(10, k.slope_hbm, k.slope)
        for move in mate_firsts:
            move.wait_recv()
        moves.sent(*mate_firsts)

        @pl.loop(0, 6)
        def _(i):
            group, rows = i // 3, pl.ds(pl.multiple_of((i % 3) * HALF, HALF), HALF)
            k.dmerged[group, rows, :] = dot_nt(k.lfirst[rows, :], k.w_o[layer, group]).astype(BF16)

        for group in range(2):
            made = dot_tn(k.merged[layer, group], k.lfirst[...])
            for zi in range(LINE):
                for xi in range(2):
                    rows = made[(zi * 2 + xi) * 24 : (zi * 2 + xi + 1) * 24]
                    k.w_out[layer, group, zi, xi, :, 0:768] = rows[0:16].astype(BF16)
                    k.w_out[layer, group, zi, xi, :, 768:1152] = jnp.concatenate(
                        [rows[16:24, 0:384], rows[16:24, 384:768]], axis=0
                    ).astype(BF16)

        at(place + "m")
        scatter(OUT, layer, 0)
        if layer == 0:
            restore_probs.wait()

        def attend_back(group, key_start, tiles):
            keys = pl.ds(key_start, SEQ)
            for head in range(3):
                low, high = head * HD, (head + 1) * HD
                key_rows = k.qkv[layer, group, keys, 192 + low : 192 + high]
                values = k.qkv[layer, group, keys, 384 + low : 384 + high]
                grad_keys = jnp.zeros((HD, SEQ), F32)
                grad_values = jnp.zeros((HD, SEQ), F32)
                for start, from_start in tiles:
                    rows, from_rows = pl.ds(start, HALF), pl.ds(pl.multiple_of(from_start, HALF), HALF)
                    queries = k.qkv[layer, group, from_rows, low:high]
                    grad_out = k.dmerged[group, rows, low:high]
                    probs = k.probs[group, head, rows, :]
                    row_dot = jnp.sum(
                        grad_out.astype(F32) * k.merged[layer, group, rows, low:high].astype(F32), axis=-1, keepdims=True
                    )
                    grad_probs = dot_nt(grad_out, values)
                    grad_scores = (probs.astype(F32) * (grad_probs - row_dot)).astype(BF16)
                    grad_values += dot(grad_out.astype(F32).T.astype(BF16), probs)
                    grad_keys += dot(queries.astype(F32).T.astype(BF16), grad_scores)
                    grad_queries = (dot(grad_scores, key_rows) * HD ** (-0.5)).astype(BF16)
                    k.qkv[layer, group, from_rows, low:high] = grad_queries
                k.qkv[layer, group, keys, 192 + low : 192 + high] = grad_keys.T.astype(BF16)
                k.qkv[layer, group, keys, 384 + low : 384 + high] = grad_values.T.astype(BF16)

        def stream_rows(start, size):
            rows = pl.ds(pl.multiple_of(start, 128), size)
            made = dot_nt(k.qkv[layer, 0, rows, :], flat(k.w_qkv[layer, 0]))
            return made + dot_nt(k.qkv[layer, 1, rows, :], flat(k.w_qkv[layer, 1]))

        @pl.loop(0, 2)
        def _(group):
            attend_back(group, SEQ, ((SEQ, SEQ + HALF * y),))
            other = pl.ds(pl.multiple_of(SEQ + HALF * (1 - y), HALF), HALF)
            k.qkv[layer, group, other, 0:192] = jnp.zeros((HALF, 192), BF16)

        away_go, away_end = send_away(lambda slot: stream_rows(SEQ + HALF * (1 - y) + 128 * slot, 128))
        at(place + "p")

        @pl.loop(0, 2)
        def _(group):
            attend_back(group, 0, ((0, 0), (HALF, HALF)))
            for j, row in ((0, 8), (2, 9)):
                sums = jnp.sum(k.qkv[layer, group, :, j * 192 : (j + 1) * 192].astype(F32), axis=0, keepdims=True)
                k.small[layer, 0, pl.ds(row + 2 * group, 1), 0:192] += sums

            @pl.when(group == 0)
            def _():
                away_go()
                at(place + "a")

            pl.when(group == 1)(lambda: at(place + "b"))

        small_step(layer, 0)
        if layer == 1:
            restore_probs = save(8, k.probs_hbm, k.probs)

        end_stream = sum_pair(
            fill_rows(
                lambda slot: stream_rows(slot * HALF, HALF), lambda slot: stream_rows(SEQ + HALF * y + 128 * slot, 128)
            )
        )
        at(place + "t")
        if layer == 0:
            for load in x_load_again:
                load.wait()

        @pl.loop(0, 4)
        def _(i):
            group, tile = i // 2, i % 2
            cols = pl.ds(pl.multiple_of(tile * OWN, OWN), OWN)
            made = dot_tn(k.x_buf[:, cols], k.qkv[layer, group])
            k.w_qkv[layer, group, pl.ds(tile * 2, 2)] = made.astype(BF16).reshape((2, 2, 96, 576))

        at(place + "q")
        scatter(QKV, layer, 0)
        if layer == 1:
            x_load_again = [
                pltpu.make_async_copy(k.x_in.at[pl.ds(pack_row, SEQ)], k.x_buf.at[pl.ds(0, SEQ)], k.local.at[4]),
                pltpu.make_async_copy(k.x_in.at[pl.ds(SEQ, SEQ)], k.x_buf.at[pl.ds(SEQ, SEQ)], k.local.at[5]),
            ]
            for load in x_load_again:
                load.start()
        end_stream()
        away_end()

    k.e_low[...] = (k.res[...] + k.cur[...]).astype(BF16)
    spreads[1] = spread(k.e_low, k.input_grad, 13)
    at("end")
    for layer in range(LAYERS):
        total = k.small.at[layer, 3]
        for row, source, share in [(row, row, LINE * 8) for row in range(6)] + [
            (6, 6 + y, LINE * 2),
            (7, 8 + 2 * y, LINE * 2),
            (8, 9 + 2 * y, LINE * 2),
        ]:
            values = total[pl.ds(source, 1), :]
            k.sq_rows[0:1, 0:DM] += values * values * (1.0 / share)
            if row < 6:
                k.vec_out[row, layer : layer + 1, :] = values
            elif row == 6:
                k.upb_out[layer : layer + 1, :] = values
            else:
                k.qvb_out[layer, row - 7 : row - 6, :] = values[:, 0:192]
    squares = jnp.sum(k.sq_rows[...], axis=0, keepdims=True)
    k.sq[0] = jnp.broadcast_to(jnp.sum(squares, axis=1, keepdims=True), (8, 128))
    for step, (devices, landing) in enumerate(((plane_devs, k.sq_plane), (line_devs, k.sq_line))):
        sent = []
        for index, device in enumerate(devices):
            lands = lambda index=index: landing.at[index]
            sent.append(moves.make(lambda: k.sq.at[step], lands, device, lands))
            sent[-1].start()
        total = k.sq[step]
        for index, move in enumerate(sent):
            move.wait_recv()
            total = total + landing[index]
        k.sq[step + 1] = total
    k.squares[...] = k.sq[2]
    moves.drain()


def kernel_call(inputs, out_grad, lens, w_q, w_o, w_u, w_d, vec, qvb, upb):
    any_ = pl.BlockSpec(memory_space=pl.ANY)
    vmem = pl.BlockSpec(memory_space=pltpu.VMEM)
    smem = pl.BlockSpec(memory_space=pltpu.SMEM)
    ins = dict(
        x_in=(inputs, any_),
        e_in=(out_grad, any_),
        lens=(lens, smem),
        wq_in=(w_q, any_),
        wo_in=(w_o.reshape(LAYERS * 24, DM), any_),
        wu_in=(w_u.reshape(LAYERS * 96, DM), any_),
        wd_in=(w_d.reshape(LAYERS * 96, DM), any_),
        vec=(vec, vmem),
        qvb_in=(qvb, vmem),
        upb_in=(upb, vmem),
    )
    outs = dict(
        activations=((3 * SEQ, DM), BF16, any_),
        input_grad=((3 * SEQ, DM), BF16, any_),
        g_qkv=((LAYERS, 3, 96, 192), F32, vmem),
        g_out=((LAYERS, 24, DM), F32, vmem),
        g_up=((LAYERS, 96, DM), F32, vmem),
        g_down=((LAYERS, 96, DM), F32, vmem),
        vec_out=((6, LAYERS, DM), F32, vmem),
        qvb_out=((LAYERS, 2, 192), F32, vmem),
        upb_out=((LAYERS, DM), F32, vmem),
        squares=((8, 128), F32, vmem),
        probs_hbm=((2, 3, 2 * OWN, SEQ), BF16, any_),
        act_hbm=((2, 2, OWN, DM), BF16, any_),
        slope_hbm=((2, 2, OWN, DM), BF16, any_),
    )
    scratch = dict(
        w_qkv=((LAYERS, 2, LINE, 2, 96, 576), BF16),
        w_out=((LAYERS, 2, LINE, 2, 16, 1152), BF16),
        w_up=((LAYERS, 2, LINE, 2, 96, 768), BF16),
        w_down=((LAYERS, 2, LINE, 2, 96, 768), BF16),
        w_o=((LAYERS, 2, 192, DM), BF16),
        unpack=((192, DM), F32),
        stage_q=((LAYERS, 3, 96, 192), F32),
        x_buf=((2 * SEQ, DM), BF16),
        qkv=((LAYERS, 2, 2 * SEQ, 576), BF16),
        probs=((2, 3, 2 * OWN, SEQ), BF16),
        merged=((LAYERS, 2, 2 * OWN, 192), BF16),
        sum1=((LAYERS, OWN, DM), F32),
        sum2=((OWN, DM), F32),
        nlow=((LAYERS, 2, OWN, DM), BF16),
        act=((2, 2, OWN, DM), BF16),
        slope=((2, 2, OWN, DM), BF16),
        res=((OWN, DM), F32),
        cur=((OWN, DM), F32),
        a_low=((OWN, DM), BF16),
        e_low=((OWN, DM), BF16),
        lsec=((2, OWN, DM), BF16),
        lfirst=((2 * OWN, DM), BF16),
        dmerged=((2, 2 * OWN, 192), BF16),
        ex_s=((SEQ, DM), BF16),
        ex_r=((SEQ, DM), BF16),
        x_far=((128, DM), BF16),
        ey_s=((128, DM), BF16),
        ey_r=((128, DM), BF16),
        ey_f=((128, DM), F32),
        bias=((2, 8, DM), F32),
        pair_col=((2, 8, SEQ), F32),
        pair_row=((2, SEQ, 128), F32),
        small=((LAYERS, 4, 16, DM), F32),
        small_in=((LAYERS, 7, 16, DM), F32),
        sq_rows=((8, 1152), F32),
        sq=((3, 8, 128), F32),
        sq_plane=((7, 8, 128), F32),
        sq_line=((LINE - 1, 8, 128), F32),
    )
    landings = {}
    for kind in KINDS:
        axis, first, second = CUTS[1][kind]

        def cut(size):
            shape = list(BLOCK[kind])
            shape[axis] = size
            return tuple(shape)

        p_1, p_2 = cut(first), cut(second - first)
        p_12, p_3 = cut(second), cut(BLOCK[kind][axis] - second)
        landings[kind] = dict(
            ry1=(1, LINE, 2) + p_1,
            rx1=(1, LINE, 1) + p_1,
            rx2=(2, LINE, 1) + p_2,
            ry2=(1, LINE, 1) + p_2,
            rz=(2, 3, 1, 1, 1) + p_12,
            rz3=(2, 3, 2, 1, 2) + p_3,
            ry3=(1, 1, 2) + p_3,
            rx3=(1, 1, 1) + p_3,
        )
    scratch.update({name + kind: (shape, BF16) for kind in KINDS for name, shape in landings[kind].items()})
    names = [*ins, *outs, *scratch, "send", "recv", "local"]
    made = pl.pallas_call(
        lambda *refs: fused(names, *refs),
        out_shape=[jax.ShapeDtypeStruct(shape, dtype) for shape, dtype, _ in outs.values()],
        in_specs=[spec for _, spec in ins.values()],
        out_specs=[spec for *_, spec in outs.values()],
        scratch_shapes=[pltpu.VMEM(shape, dtype) for shape, dtype in scratch.values()]
        + [
            pltpu.SemaphoreType.DMA((SEMS,)),
            pltpu.SemaphoreType.DMA((SEMS,)),
            pltpu.SemaphoreType.DMA((16,)),
        ],
        compiler_params=pltpu.CompilerParams(
            collective_id=0, has_side_effects=True, vmem_limit_bytes=VMEM_BYTES
        ),
        name="encoder_step",
    )(*[value for value, _ in ins.values()])
    return types.SimpleNamespace(**dict(zip(outs, made)))


VMEM_BYTES = 64 * 2**20 - 2**17
UPDATE_VMEM_BYTES = VMEM_BYTES


def update_kernel(names, *refs):
    k = types.SimpleNamespace(**dict(zip(names, refs)))
    norm = jnp.sqrt(k.squares[0:1, 0:1])
    factor = jnp.minimum(1.0, CLIP_LIMIT / norm)

    def update(name, rate, decay):
        made = adamw(*[vars(k)[part + name][...] for part in "wmvg"], factor, rate, decay)
        for part, value in zip("wmv", made):
            vars(k)["new" + part + name][...] = value

    for name in KINDS:
        update(name, LEARN_RATE, WEIGHT_DECAY)

    @pl.when(pl.program_id(0) == 0)
    def _():
        for name in ("vec", "qvb", "upb"):
            update(name, VECTOR_RATE, 0.0)
        k.norm[...] = norm

    k.new_input_grad[...] = k.input_grad[...].astype(F32)
    k.new_activations[...] = k.activations[...]


def update_call(weights, squares, activations, input_grad):
    blocks = dict(
        qkv=pl.BlockSpec((1, 3, 96, 192), lambda i: (i, 0, 0, 0)),
        out=pl.BlockSpec((1, 24, DM), lambda i: (i, 0, 0)),
        up=pl.BlockSpec((1, 96, DM), lambda i: (i, 0, 0)),
        down=pl.BlockSpec((1, 96, DM), lambda i: (i, 0, 0)),
        vec=pl.BlockSpec((6, LAYERS, DM), lambda i: (0, 0, 0)),
        qvb=pl.BlockSpec((LAYERS, 2, 192), lambda i: (0, 0, 0)),
        upb=pl.BlockSpec((LAYERS, DM), lambda i: (0, 0)),
    )
    whole = pl.BlockSpec((8, 128), lambda i: (0, 0))
    rows = pl.BlockSpec((2 * OWN, DM), lambda i: (i, 0))
    ins = dict(squares=(squares, whole), activations=(activations, rows), input_grad=(input_grad, rows))
    outs = dict(
        norm=(jax.ShapeDtypeStruct((1, 1), F32), F32, pl.BlockSpec((1, 1), lambda i: (0, 0))), new_activations=(activations, BF16, rows), new_input_grad=(input_grad, F32, rows)
    )
    for name, arrays in weights.items():
        for part, value in zip("wmvg", arrays):
            ins[part + name] = (value, blocks[name])
            if part != "g":
                outs["new" + part + name] = (value, F32, blocks[name])
    names = [*ins, *outs]
    made = pl.pallas_call(
        lambda *refs: update_kernel(names, *refs),
        grid=(LAYERS,),
        out_shape=[jax.ShapeDtypeStruct(like.shape, dtype) for like, dtype, _ in outs.values()],
        in_specs=[spec for _, spec in ins.values()],
        out_specs=[spec for *_, spec in outs.values()],
        compiler_params=pltpu.CompilerParams(vmem_limit_bytes=UPDATE_VMEM_BYTES),
        name="update",
    )(*[value for value, _ in ins.values()])
    return types.SimpleNamespace(**dict(zip(outs, made)))


def kernel_body(
    inputs,
    pair_lengths,
    out_grad,
    w_qkv,
    m_qkv,
    v_qkv,
    w_out,
    m_out,
    v_out,
    w_up,
    m_up,
    v_up,
    w_down,
    m_down,
    v_down,
    vectors,
    m_vectors,
    v_vectors,
    qv_bias,
    m_qv_bias,
    v_qv_bias,
    up_bias,
    m_up_bias,
    v_up_bias,
):
    turn = lambda v: jnp.transpose(v, (0, 2, 1, 3))
    swap = lambda v: jnp.transpose(v, (1, 0, 2))
    w_qkv, m_qkv, v_qkv = turn(w_qkv), turn(m_qkv), turn(v_qkv)
    vectors, m_vectors, v_vectors = swap(vectors), swap(m_vectors), swap(v_vectors)
    made = kernel_call(inputs, out_grad, pair_lengths, w_qkv, w_out, w_up, w_down, vectors, qv_bias, up_bias)
    weights = dict(
        qkv=(w_qkv, m_qkv, v_qkv, made.g_qkv),
        out=(w_out, m_out, v_out, made.g_out),
        up=(w_up, m_up, v_up, made.g_up),
        down=(w_down, m_down, v_down, made.g_down),
        vec=(vectors, m_vectors, v_vectors, made.vec_out),
        qvb=(qv_bias, m_qv_bias, v_qv_bias, made.qvb_out),
        upb=(up_bias, m_up_bias, v_up_bias, made.upb_out),
    )
    new = update_call(weights, made.squares, made.activations, made.input_grad)
    parts = lambda name: [vars(new)["new" + part + name] for part in "wmv"]
    return (
        new.new_activations,
        new.new_input_grad,
        new.norm.reshape(()),
        *[turn(v) for v in parts(QKV)],
        *parts(OUT),
        *parts(UP),
        *parts(DOWN),
        *[swap(v) for v in parts("vec")],
        *parts("qvb"),
        *parts("upb"),
    )


def solution(mesh):
    rows, matrix = P("dp", None), P(None, ("tensor", "dp"), None)
    qkv, up = P(None, "dp", None, "tensor"), P(None, "dp", "tensor")
    heads, hidden = P(None, None, "tensor"), P(None, "tensor")
    weights = (qkv,) * 3 + (matrix,) * 3 + (up,) * 3 + (matrix,) * 3
    smalls = (P(),) * 3 + (heads,) * 3 + (hidden,) * 3
    fits = mesh.shape["dp"] == 2 * LINE and mesh.shape["tensor"] == 4
    return jax.shard_map(
        kernel_body if fits else body,
        mesh=mesh,
        in_specs=(rows, rows, rows) + weights + smalls,
        out_specs=(rows, rows, P()) + weights + smalls,
        check_vma=False,
    )
```
